32 devices in a mesh: dp: 8 (over z, y), mp: 4 (over x, core).
Axes of the slice: x: 2, y: 2, z: 4, core: 2. Of those that a mesh axis runs over, the one named last changes fastest.
Arguments:
- tokens: bfloat16 [50176, 512], P(('dp', 'mp')), may hold values from -6 to 6
- regions: int32 [128, 392], P('dp'), may hold values from 0 to 7, as said below
- first_gain: float32 [512], P('dp'), may hold values from 0.5 to 1.5
- first_shift: float32 [512], P('dp'), may hold values from -4 to 4
- triple_weight: float32 [3, 512, 512], P(None, 'dp', 'mp'), may hold values from -0.375 to 0.375
- query_bias: float32 [512], P('dp'), may hold values from -6 to 6
- value_bias: float32 [512], P('dp'), may hold values from -6 to 6
- offset_table: float32 [16, 2535], P('mp'), may hold values from -6 to 6
- output_weight: float32 [512, 512], P('mp', 'dp'), may hold values from -1 to 1
- output_bias: float32 [512], P('dp'), may hold values from -4 to 4
- second_gain: float32 [512], P('dp'), may hold values from 0.5 to 1.5
- second_shift: float32 [512], P('dp'), may hold values from -4 to 4
- inner_weight: float32 [512, 2048], P('dp', 'mp'), may hold values from -0.25 to 0.25
- inner_bias: float32 [2048], P('dp'), may hold values from -6 to 6
- outer_weight: float32 [2048, 512], P('mp', 'dp'), may hold values from -0.1875 to 0.1875
- outer_bias: float32 [512], P('dp'), may hold values from -4 to 4
- cotangent: bfloat16 [50176, 512], P(('dp', 'mp')), may hold values from -6 to 6
Outputs:
- result: bfloat16 [50176, 512], P(('dp', 'mp'))
- gradient_tokens: bfloat16 [50176, 512], P(('dp', 'mp'))
- gradient_first_gain: float32 [512], P(('dp', 'mp'))
- gradient_first_shift: float32 [512], P(('dp', 'mp'))
- gradient_triple: float32 [3, 512, 512], P(None, 'dp', 'mp')
- gradient_query_bias: float32 [512], P(('dp', 'mp'))
- gradient_value_bias: float32 [512], P(('dp', 'mp'))
- gradient_offsets: float32 [16, 2535], P('mp')
- gradient_output_weight: float32 [512, 512], P('mp', 'dp')
- gradient_output_bias: float32 [512], P(('dp', 'mp'))
- gradient_second_gain: float32 [512], P(('dp', 'mp'))
- gradient_second_shift: float32 [512], P(('dp', 'mp'))
- gradient_inner_weight: float32 [512, 2048], P('dp', 'mp')
- gradient_inner_bias: float32 [2048], P(('dp', 'mp'))
- gradient_outer_weight: float32 [2048, 512], P('mp', 'dp')
- gradient_outer_bias: float32 [512], P(('dp', 'mp'))
- head_maxima: float32 [16], P('mp')
- clipped_weight: float32 [2, 512, 512], P(None, 'dp', 'mp')
The draws below stay inside these ranges and needn't reach their ends.
Inputs may be any that keep to these rules, and one draw needn't show every extreme that they name: `regions`: for each window there are cut points 0 <= c_t < 8, 0 <= c_h < 7, 0 <= c_w < 7, and the id of the token at place (t, h, w) is 4 * [t >= c_t] + 2 * [h >= c_h] + [w >= c_w]; windows 7, 15, 23 and so on are cut at (4, 3, 3).
All inputs are finite; a program needn't handle non-finite values.
Results may differ from the reference program's by a relative error of at most 0.02.
Values may be sent and summed in bfloat16 or wider, within the bound.
No kernel may reach another device: no remote copies, remote signals or barrier semaphores. Data moves between devices by JAX's collectives and lax.ppermute only.
A program may use at most 192 MiB of HBM per device.

```python
import math
from functools import partial
import jax
import jax.numpy as jnp
from jax import lax

D = 512
HEADS = 16
HEAD_DIM = 32
FF = 2048
WIN_T = 8
WIN_H = 7
WIN_W = 7
WIN_BLOCK = 2
WIN = 392
TABLE = 2535
WINDOWS = 128
TOKENS = 50176


def draw_regions(key, part):
    cut_keys = jax.random.split(key, 3)
    windows_all = jnp.arange(WINDOWS)
    corner = windows_all % 8 == 7
    cut_time = jnp.where(corner, WIN_T // 2, jax.random.randint(cut_keys[0], (WINDOWS,), 0, WIN_T))
    cut_height = jnp.where(corner, WIN_H // 2, jax.random.randint(cut_keys[1], (WINDOWS,), 0, WIN_H))
    cut_width = jnp.where(corner, WIN_W // 2, jax.random.randint(cut_keys[2], (WINDOWS,), 0, WIN_W))
    places = jnp.arange(WIN)
    along_time = places // (WIN_H * WIN_W)
    along_height = places // WIN_W % WIN_H
    along_width = places % WIN_W
    labels = 4 * (along_time[None, :] >= cut_time[:, None]).astype(jnp.int32) + 2 * (along_height[None, :] >= cut_height[:, None]).astype(jnp.int32) + (along_width[None, :] >= cut_width[:, None]).astype(jnp.int32)
    return labels.astype(jnp.int32)


def levels(own_key, shape, shards, smallest, largest):
    gain, own = 1.0, jax.random.fold_in(own_key, 6)
    for dim, blocks in shards:
        heights = jnp.exp(jax.random.uniform(jax.random.fold_in(own, dim), (blocks,), jnp.float32, smallest / len(shards), largest / len(shards)))
        gain = gain * jnp.repeat(heights, shape[dim] // blocks).reshape([-1 if axis == dim else 1 for axis in range(len(shape))])
    return gain


def noise(rng, extent, scale, reach, shards=(), dtype=jnp.bfloat16):
    loudness = levels(rng, extent, shards, -0.22, 0.18) if shards else 1.0
    result = jax.random.normal(rng, extent, jnp.float32) * scale * loudness
    return jnp.minimum(jnp.maximum(result, -reach), reach).astype(dtype)


def setup_inputs(seed: int = 0) -> dict:
    splits = jax.random.split(jax.random.key(seed), 18)
    return {
        "tokens": noise(splits[0], (TOKENS, D), 1.0, 6.0, ((0, 32),)),
        "regions": draw_regions(jax.random.fold_in(splits[17], 71), 0),
        "first_gain": jnp.clip(1.0 + 0.1 * jax.random.normal(splits[2], (D,), jnp.float32), 0.5, 1.5),
        "first_shift": noise(splits[3], (D,), 0.3, 4.0, ((0, 8),), jnp.float32),
        "triple_weight": noise(splits[4], (3, D, D), (D // 2) ** -0.5, 0.375, ((1, 8), (2, 4)), jnp.float32),
        "query_bias": noise(splits[5], (D,), 0.5, 6.0, ((0, 8),), jnp.float32),
        "value_bias": noise(splits[6], (D,), 0.5, 6.0, ((0, 8),), jnp.float32),
        "offset_table": noise(splits[7], (HEADS, TABLE), 1.0, 6.0, ((0, 4),), jnp.float32),
        "output_weight": noise(splits[8], (D, D), HEAD_DIM ** -0.5, 1.0, ((0, 4), (1, 8)), jnp.float32),
        "output_bias": noise(splits[9], (D,), 0.3, 4.0, ((0, 8),), jnp.float32),
        "second_gain": jnp.clip(1.0 + 0.1 * jax.random.normal(splits[10], (D,), jnp.float32), 0.5, 1.5),
        "second_shift": noise(splits[11], (D,), 0.3, 4.0, ((0, 8),), jnp.float32),
        "inner_weight": noise(splits[12], (D, FF), D ** -0.5, 0.25, ((0, 8), (1, 4)), jnp.float32),
        "inner_bias": noise(splits[13], (FF,), 0.5, 6.0, ((0, 8),), jnp.float32),
        "outer_weight": noise(splits[14], (FF, D), (FF // 2) ** -0.5, 0.1875, ((0, 4), (1, 8)), jnp.float32),
        "outer_bias": noise(splits[15], (D,), 0.3, 4.0, ((0, 8),), jnp.float32),
        "cotangent": noise(splits[16], (TOKENS, D), 1.0, 6.0, ((0, 32),)),
    }


@jax.custom_vjp
def low(v):
    return lax.optimization_barrier(v.astype(jnp.bfloat16)).astype(jnp.float32)

@jax.custom_vjp
def low_back(v):
    return v

def low_keep(v):
    return (low(v), None)

def low_pass(kept, grad):
    return (grad,)

def back_keep(v):
    return (v, None)

def back_low(kept, grad):
    return (low(grad),)
low.defvjp(low_keep, low_pass)
low_back.defvjp(back_keep, back_low)
highest_precision = lax.Precision.HIGHEST
norm_epsilon = 1e-05
masked_score = -1000000000.0
clip_target = 10.0

def product(left, right):
    return jnp.dot(left, right, precision=highest_precision, preferred_element_type=jnp.float32)

def layer_norm(values, norm_gain, norm_shift):
    centred = values - lax.optimization_barrier(jnp.mean(values, axis=-1, keepdims=True))
    spread = lax.optimization_barrier(jnp.mean(centred * centred, axis=-1, keepdims=True))
    return centred * lax.rsqrt(spread + norm_epsilon) * norm_gain + norm_shift

def offset_index():
    places = jnp.arange(WIN)
    along_time = places // (WIN_H * WIN_W)
    along_height = places // WIN_W % WIN_H
    along_width = places % WIN_W
    return ((along_time[:, None] - along_time[None, :] + WIN_T - 1) * ((2 * WIN_H - 1) * (2 * WIN_W - 1)) + (along_height[:, None] - along_height[None, :] + WIN_H - 1) * (2 * WIN_W - 1) + (along_width[:, None] - along_width[None, :] + WIN_W - 1)).astype(jnp.int32)

def forward(regions, tokens_float, first_gain, first_shift, triple_weight, query_bias, value_bias, offset_table, output_weight, output_bias, second_gain, second_shift, inner_weight, inner_bias, outer_weight, outer_bias):
    first_gain = low(first_gain)
    first_shift = low(first_shift)
    triple_weight = low(triple_weight)
    query_bias = low(query_bias)
    value_bias = low(value_bias)
    offset_table = low(offset_table)
    output_weight = low(output_weight)
    output_bias = low(output_bias)
    second_gain = low(second_gain)
    second_shift = low(second_shift)
    inner_weight = low(inner_weight)
    inner_bias = low(inner_bias)
    outer_weight = low(outer_weight)
    outer_bias = low(outer_bias)
    bias_grid = offset_table[:, offset_index()]
    score_scale = 1.0 / math.sqrt(HEAD_DIM)
    shaped = (WIN_BLOCK, WIN, HEADS, HEAD_DIM)

    def window_group(tokens_group, regions_group):
        normed = low(layer_norm(tokens_group, first_gain, first_shift))
        queries = low(low_back(product(normed, triple_weight[0])) + query_bias)
        key_rows = low(low_back(product(normed, triple_weight[1])))
        value_rows = low(low_back(product(normed, triple_weight[2])) + value_bias)
        scores = jnp.einsum('wihd,wjhd->whij', queries.reshape(shaped), key_rows.reshape(shaped), precision=highest_precision) * score_scale
        group_max = lax.optimization_barrier(jnp.max(scores, axis=(0, 2, 3)))
        allowed = (regions_group[:, :, None] == regions_group[:, None, :])[:, None]
        logits = jnp.where(allowed, low_back(scores) + bias_grid[None], masked_score)
        weights_soft = low(jax.nn.softmax(logits, axis=3))
        mixed = jnp.einsum('whij,wjhd->wihd', weights_soft, value_rows.reshape(shaped), precision=highest_precision)
        mixed = low(low_back(mixed.reshape(WIN_BLOCK * WIN, D)))
        middle = tokens_group + low_back(product(mixed, output_weight)) + output_bias
        normed_second = low(layer_norm(middle, second_gain, second_shift))
        before = low_back(product(normed_second, inner_weight)) + inner_bias
        hidden = low(jax.nn.gelu(before, approximate=False))
        return (middle + low_back(product(hidden, outer_weight)) + outer_bias, group_max)
    checked = jax.checkpoint(window_group)
    outputs, maxima = lax.map(lambda pair: checked(pair[0], pair[1]), (tokens_float.reshape(WINDOWS // WIN_BLOCK, WIN_BLOCK * WIN, D), regions.reshape(WINDOWS // WIN_BLOCK, WIN_BLOCK, WIN)))
    return (outputs.reshape(TOKENS, D), lax.optimization_barrier(jnp.max(maxima, axis=0)))

def reference(tokens, regions, first_gain, first_shift, triple_weight, query_bias, value_bias, offset_table, output_weight, output_bias, second_gain, second_shift, inner_weight, inner_bias, outer_weight, outer_bias, cotangent):
    primals = (tokens.astype(jnp.float32), first_gain, first_shift, triple_weight, query_bias, value_bias, offset_table, output_weight, output_bias, second_gain, second_shift, inner_weight, inner_bias, outer_weight, outer_bias)
    outputs, pullback, maxima = jax.vjp(partial(forward, regions), *primals, has_aux=True)
    gradients = pullback(cotangent.astype(jnp.float32))
    clip_factor = clip_target / jnp.maximum(maxima, clip_target)
    root_columns = jnp.repeat(jnp.sqrt(clip_factor), HEAD_DIM)
    clipped = triple_weight[:2] * root_columns[None, None, :]
    return (outputs.astype(jnp.bfloat16), gradients[0].astype(jnp.bfloat16), gradients[1], gradients[2], gradients[3], gradients[4], gradients[5], gradients[6], gradients[7], gradients[8], gradients[9], gradients[10], gradients[11], gradients[12], gradients[13], gradients[14], maxima, clipped)
```

```python
import math, functools
import numpy as np
import jax, jax.numpy as jnp
from jax import lax
from jax.experimental import pallas as pl
from jax.experimental.pallas import tpu as pltpu
from jax.sharding import PartitionSpec as P

D = 512
HEADS = 16
HEAD_DIM = 32
FF = 2048
WIN = 392
PLACES = 49
TIMES = 8
SPACE = 169
TABLE = 2535
GROUP = 128
norm_epsilon = 1e-05
masked_score = -1e9
clip_target = 10.0
log2e = math.log2(math.e)
score_scale = 1.0 / math.sqrt(HEAD_DIM)
bf = jnp.bfloat16
f32 = jnp.float32
ROWS = [(s, min(64, WIN - s)) for s in range(0, WIN, 64)]


def dd(a, b, ca, cb):
    return lax.dot_general(a, b, (((ca,), (cb,)), ((), ())), preferred_element_type=f32)


def fold_max(acc, x):
    for r in range(0, x.shape[0], 8):
        acc = jnp.maximum(acc, x[r:r + 8])
    return acc


def load_blocks(me, blocks, src, dst, sem, rows):
    copies = []
    for k, blk in enumerate(blocks):
        at = pl.multiple_of((me ^ blk) * rows, rows)
        copies.append(pltpu.make_async_copy(src.at[k], dst.at[pl.ds(at, rows)], sem.at[k]))
        copies[-1].start()
    for c in copies:
        c.wait()


def fwd_kernel(first, blocks, *refs):
    if first:
        (me_ref, x_ref, ln_ref, w_hbm, qv_ref, t2_ref, rr_ref, rc_ref,
         n1_out, qkv_out, e_out, ot_out, o_out, linv_out, hm_out, w_out,
         wscr, bias, mask, s_scr, wsem) = refs
    else:
        (me_ref, n1_ref, w_hbm, qv_ref, t2_ref, rr_ref, rc_ref,
         qkv_out, e_out, ot_out, o_out, linv_out, hm_out, w_out,
         wscr, bias, mask, s_scr, wsem) = refs
    w = pl.program_id(0)

    @pl.when(w == 0)
    def _():
        load_blocks(me_ref[0], blocks, w_hbm, wscr, wsem, w_hbm.shape[1])
        w_out[...] = wscr[...]
        for h in range(4):
            for t in range(TIMES):
                bias[h, t * PLACES:(t + 1) * PLACES, :] = t2_ref[h, 0:PLACES, (7 - t) * PLACES:(7 - t) * PLACES + WIN]
        hm_out[...] = jnp.full(hm_out.shape, -jnp.inf, f32)

    mask[...] = jnp.where(rc_ref[0] == rr_ref[0], 0.0, masked_score)
    if first:
        x = x_ref[0].astype(f32)
        xc = x - jnp.mean(x, axis=1, keepdims=True)
        inv = lax.rsqrt(jnp.mean(xc * xc, axis=1, keepdims=True) + norm_epsilon)
        n1 = (xc * inv * ln_ref[0:1] + ln_ref[1:2]).astype(bf)
        n1_out[0] = n1
    else:
        n1 = n1_ref[0]
    p = dd(n1, wscr[...], 1, 0)
    q = (p[:, :128] + qv_ref[0:1]) * (score_scale * log2e)
    kb = p[:, 128:256].astype(bf)
    v = p[:, 256:] + qv_ref[1:2]
    qkv_out[0, :, 0:128] = q.astype(bf)
    qkv_out[0, :, 128:256] = kb
    qkv_out[0, :, 256:384] = v.astype(bf)
    qT = q.T.astype(bf)
    vT = v.T.astype(bf)
    ones = jnp.ones((16, WIN), bf)
    outs, linvs = [], []
    for h in range(4):
        sl = slice(h * 32, h * 32 + 32)
        s_scr[...] = dd(kb[:, sl], qT[sl], 1, 0)
        hm = jnp.full((8, WIN), -jnp.inf, f32)
        m = jnp.full((8, WIN), -jnp.inf, f32)
        for r, n in ROWS:
            c = s_scr[r:r + n]
            hm = fold_max(hm, c)
            c = c + bias[h, r:r + n] + mask[r:r + n]
            m = fold_max(m, c)
            s_scr[r:r + n] = c
        hm_out[h] = jnp.maximum(hm_out[h], hm)
        m = jnp.max(m, axis=0, keepdims=True)
        for r, n in ROWS:
            e_out[0, h, r:r + n] = jnp.exp2(s_scr[r:r + n] - m).astype(bf)
        ol = dd(jnp.concatenate([vT[sl], ones], axis=0), e_out[0, h], 1, 0)
        linv = 1.0 / ol[32:33]
        linvs.append(linv)
        outs.append(ol[:32] * linv)
    oT = jnp.concatenate(outs, axis=0)
    ot_out[0] = oT.astype(bf)
    o_out[0] = oT.T.astype(bf)
    linv_out[0] = jnp.concatenate(linvs + [jnp.zeros((4, WIN), f32)], axis=0)


def full(shape):
    return pl.BlockSpec(shape, lambda w, me: (0,) * len(shape))


def win(shape):
    return pl.BlockSpec((1,) + shape, lambda w, me: (w,) + (0,) * len(shape))


def attend_fwd(first, me, x, ln, wblk, qv, t2, rr, rc, blocks):
    nw = x.shape[0]
    sds = jax.ShapeDtypeStruct
    ins = [x] + ([ln] if first else []) + [wblk, qv, t2, rr, rc]
    in_specs = ([win((WIN, D))] + ([full(ln.shape)] if first else []) +
                [pl.BlockSpec(memory_space=pl.ANY), full(qv.shape), full(t2.shape), win((1, WIN)), win((WIN, 1))])
    outs = ([sds((nw, WIN, D), bf)] if first else []) + [
        sds((nw, WIN, 384), bf), sds((nw, 4, WIN, WIN), bf), sds((nw, GROUP, WIN), bf), sds((nw, WIN, GROUP), bf),
        sds((nw, 8, WIN), f32), sds((4, 8, WIN), f32), sds((D, 384), bf)]
    out_specs = ([win((WIN, D))] if first else []) + [
        win((WIN, 384)), win((4, WIN, WIN)), win((GROUP, WIN)), win((WIN, GROUP)), win((8, WIN)), full((4, 8, WIN)), full((D, 384))]
    return pl.pallas_call(
        functools.partial(fwd_kernel, first, blocks), out_shape=outs,
        grid_spec=pltpu.PrefetchScalarGridSpec(
            num_scalar_prefetch=1, grid=(nw,), in_specs=in_specs, out_specs=out_specs,
            scratch_shapes=[pltpu.VMEM((D, 384), bf), pltpu.VMEM((4, WIN, WIN), f32), pltpu.VMEM((WIN, WIN), f32),
                            pltpu.VMEM((WIN, WIN), f32), pltpu.SemaphoreType.DMA((wblk.shape[0],))]),
        compiler_params=pltpu.CompilerParams(vmem_limit_bytes=48 * 2**20),
        cost_estimate=pl.CostEstimate(flops=nw * 2 * 10**9, bytes_accessed=nw * 4 * 10**6, transcendentals=nw * 4 * WIN * WIN),
    )(me, *ins)


def bwd_kernel(first, last, blocks, *refs):
    refs = list(refs)
    take = lambda n: [refs.pop(0) for _ in range(n)]
    me_ref, n1_ref, qkv_ref, e_ref, ot_ref, linv_ref, dyb_ref, wo_ref, w_ref = take(9)
    prev_ref = None if first else take(1)[0]
    if last:
        x_ref, dy_ref, ln_ref = take(3)
    dn_out, dw_out, t2_out, vec_out = take(4)
    if last:
        ln_out, = take(1)
    dwacc, dls, p_scr, dl_scr = take(4)
    w = pl.program_id(0)

    @pl.when(w == 0)
    def _():
        dwacc[...] = jnp.zeros(dwacc.shape, f32)
        dls[...] = jnp.zeros(dls.shape, f32)
        vec_out[...] = jnp.zeros(vec_out.shape, f32)
        if last:
            ln_out[...] = jnp.zeros(ln_out.shape, f32)

    q = qkv_ref[0, :, 0:128]
    k = qkv_ref[0, :, 128:256]
    v = qkv_ref[0, :, 256:384]
    do = dd(dyb_ref[0], wo_ref[...], 1, 0)
    doT = do.T
    oT = ot_ref[0].astype(f32)
    scaled = []
    rs = []
    for h in range(4):
        sl = slice(h * 32, h * 32 + 32)
        s = (doT[sl] * linv_ref[0, h:h + 1]).astype(bf)
        scaled.append(s)
        rs.append(jnp.sum(s.astype(f32) * oT[sl], axis=0, keepdims=True))
    doTs = jnp.concatenate(scaled, axis=0)
    dos = doTs.astype(f32).T.astype(bf)
    kT = k.astype(f32).T.astype(bf)
    lane = lax.broadcasted_iota(jnp.int32, (1, 128), 1) // 32
    dk = jnp.zeros((WIN, 128), f32)
    dv = jnp.zeros((WIN, 128), f32)
    dqT = []
    for h in range(4):
        sl = slice(h * 32, h * 32 + 32)
        p_scr[...] = dd(v[:, sl], doTs[sl], 1, 0)
        for r, n in ROWS:
            dl = e_ref[0, h, r:r + n].astype(f32) * (p_scr[r:r + n] - rs[h])
            dls[h, r:r + n] += dl
            dl_scr[r:r + n] = dl.astype(bf)
        dqT.append(dd(kT[sl], dl_scr[...], 1, 0))
        own = lane == h
        dk += dd(dl_scr[...], jnp.where(own, q, jnp.zeros((), bf)), 1, 0)
        dv += dd(e_ref[0, h], jnp.where(own, dos, jnp.zeros((), bf)), 1, 0)
    dq = jnp.concatenate(dqT, axis=0).T * score_scale
    dk = dk * (1.0 / log2e)
    vec_out[0:1] += jnp.sum(dq, axis=0, keepdims=True)
    vec_out[1:2] += jnp.sum(dv, axis=0, keepdims=True)
    dqkv = jnp.concatenate([dq.astype(bf), dk.astype(bf), dv.astype(bf)], axis=1)
    dwacc[...] += dd(n1_ref[0], dqkv, 0, 0)
    dn1 = dd(dqkv, w_ref[...], 1, 1)
    if not first:
        dn1 = dn1 + prev_ref[0]
    if last:
        x = x_ref[0].astype(f32)
        xc = x - jnp.mean(x, axis=1, keepdims=True)
        inv = lax.rsqrt(jnp.mean(xc * xc, axis=1, keepdims=True) + norm_epsilon)
        u = xc * inv
        ln_out[0:1] += jnp.sum(dn1 * u, axis=0, keepdims=True)
        ln_out[1:2] += jnp.sum(dn1, axis=0, keepdims=True)
        a = dn1 * ln_ref[0:1]
        g = inv * (a - jnp.mean(a, axis=1, keepdims=True) - u * jnp.mean(a * u, axis=1, keepdims=True))
        dn_out[0] = (dy_ref[0] + g).astype(bf)
    else:
        dn_out[0] = dn1

    @pl.when(w == pl.num_programs(0) - 1)
    def _():
        rows = dw_out.shape[1]
        for kk, blk in enumerate(blocks):
            at = pl.multiple_of((me_ref[0] ^ blk) * rows, rows)
            dw_out[kk] = dwacc[pl.ds(at, rows), :].astype(bf)
        t2_out[...] = jnp.zeros(t2_out.shape, f32)
        for h in range(4):
            for t in range(TIMES):
                lo = (7 - t) * PLACES
                t2_out[h, 0:PLACES, lo:lo + WIN] += dls[h, t * PLACES:(t + 1) * PLACES, :]


def attend_bwd(me, n1, qkv, e, oT, linv, dyb, wo, w, prev, last, blocks):
    nblk = len(blocks)
    nw = n1.shape[0]
    sds = jax.ShapeDtypeStruct
    first = prev is None
    ins = [n1, qkv, e, oT, linv, dyb, wo, w] + ([] if first else [prev]) + (list(last) if last else [])
    in_specs = ([win((WIN, D)), win((WIN, 384)), win((4, WIN, WIN)), win((GROUP, WIN)), win((8, WIN)), win((WIN, D)),
                 full((D, GROUP)), full((D, 384))] + ([] if first else [win((WIN, D))]) +
                ([win((WIN, D)), win((WIN, D)), full(last[2].shape)] if last else []))
    outs = [sds((nw, WIN, D), bf if last else f32), sds((nblk, D // nblk, 384), bf), sds((4, 56, 768), f32), sds((8, 128), f32)]
    out_specs = [win((WIN, D)), full((nblk, D // nblk, 384)), full((4, 56, 768)), full((8, 128))]
    if last:
        outs.append(sds((8, D), f32))
        out_specs.append(full((8, D)))
    return pl.pallas_call(
        functools.partial(bwd_kernel, first, bool(last), blocks), out_shape=outs,
        grid_spec=pltpu.PrefetchScalarGridSpec(
            num_scalar_prefetch=1, grid=(nw,), in_specs=in_specs, out_specs=out_specs,
            scratch_shapes=[pltpu.VMEM((D, 384), f32), pltpu.VMEM((4, WIN, WIN), f32), pltpu.VMEM((WIN, WIN), f32),
                            pltpu.VMEM((WIN, WIN), bf)]),
        compiler_params=pltpu.CompilerParams(vmem_limit_bytes=48 * 2**20),
        cost_estimate=pl.CostEstimate(flops=nw * 4 * 10**9, bytes_accessed=nw * 5 * 10**6, transcendentals=0),
    )(me, *ins)


def mlp_kernel(na, *refs):
    places, nblk, brow = na
    refs = list(refs)
    take = lambda n: [refs.pop(0) for _ in range(n)]
    narr = 1 + max(p[0] for p in places)
    me_ref, x_ref, g_ref = take(3)
    o_refs = take(4)
    vin_ref, bi_ref = take(2)
    w_hbm = take(narr)
    res_out, dy_out, dyb_out, wo_out, vec_out, dbi_out = take(6)
    g_outs = take(narr)
    wscr, acc, wsem = take(3)
    t = pl.program_id(0)
    me = me_ref[0]

    @pl.when(t == 0)
    def _():
        copies = []
        for i, (arr, idx, k, blk, off) in enumerate(places):
            at = pl.multiple_of((me ^ blk) * (D // nblk) + off, brow)
            copies.append(pltpu.make_async_copy(w_hbm[arr].at[idx], wscr.at[k, pl.ds(at, brow)], wsem.at[i]))
            copies[-1].start()
        acc[...] = jnp.zeros(acc.shape, f32)
        vec_out[...] = jnp.zeros(vec_out.shape, f32)
        dbi_out[...] = jnp.zeros(dbi_out.shape, f32)
        for c in copies:
            c.wait()

    o = jnp.concatenate([r[...] for r in o_refs], axis=1)
    y = x_ref[...].astype(f32) + vin_ref[0:1]
    for k in range(4):
        y = y + dd(o_refs[k][...], wscr[k, :, 0:128], 1, 1)
    yc = y - jnp.mean(y, axis=1, keepdims=True)
    inv = lax.rsqrt(jnp.mean(yc * yc, axis=1, keepdims=True) + norm_epsilon)
    u = yc * inv
    n2 = (u * vin_ref[1:2] + vin_ref[2:3]).astype(bf)
    gb = g_ref[...]
    gT = gb.astype(f32).T.astype(bf)
    n2T = n2.astype(f32).T.astype(bf)
    ff = jnp.zeros(y.shape, f32)
    dn2 = jnp.zeros(y.shape, f32)
    for k in range(4):
        wi = wscr[k, :, 128:640]
        wo = wscr[k, :, 640:1152]
        z = dd(n2, wi, 1, 0) + bi_ref[:, k * 512:(k + 1) * 512]
        ez = jnp.exp2(z * z * (-0.5 * log2e))
        tt = 1.0 / (1.0 + (0.3275911 * 0.7071067811865476) * jnp.abs(z))
        poly = tt * (0.254829592 + tt * (-0.284496736 + tt * (1.421413741 + tt * (-1.453152027 + tt * 1.061405429))))
        tail = 0.5 * poly * ez
        phi = jnp.where(z >= 0, 1.0 - tail, tail)
        hb = (z * phi).astype(bf)
        slope = phi + z * (ez * 0.3989422804014327)
        ff = ff + dd(hb, wo, 1, 1)
        dz = dd(gb, wo, 1, 0) * slope
        dbi_out[0:1, k * 512:(k + 1) * 512] += jnp.sum(dz, axis=0, keepdims=True)
        dzb = dz.astype(bf)
        dn2 = dn2 + dd(dzb, wi, 1, 1)
        acc[k, :, 640:1152] += dd(gT, hb, 1, 0)
        acc[k, :, 128:640] += dd(n2T, dzb, 1, 0)
    res_out[...] = (y + ff + vin_ref[3:4]).astype(bf)
    g = gb.astype(f32)
    a = dn2 * vin_ref[1:2]
    dy = g + inv * (a - jnp.mean(a, axis=1, keepdims=True) - u * jnp.mean(a * u, axis=1, keepdims=True))
    dy_out[...] = dy
    dyb = dy.astype(bf)
    dyb_out[...] = dyb
    dyT = dy.T.astype(bf)
    for k in range(4):
        acc[k, :, 0:128] += dd(dyT, o_refs[k][...], 1, 0)
    vec_out[0:1] += jnp.sum(g, axis=0, keepdims=True)
    vec_out[1:2] += jnp.sum(dn2 * u, axis=0, keepdims=True)
    vec_out[2:3] += jnp.sum(dn2, axis=0, keepdims=True)
    vec_out[3:4] += jnp.sum(dy, axis=0, keepdims=True)

    @pl.when(t == pl.num_programs(0) - 1)
    def _():
        wo_out[...] = wscr[:, :, 0:128]
        for arr, idx, k, blk, off in places:
            at = pl.multiple_of((me ^ blk) * (D // nblk) + off, brow)
            g_outs[arr][idx] = acc[k, pl.ds(at, brow), :].astype(bf)


def mlp(me, x, g, o_list, vin, bi, warrs, places, nblk, tile):
    T = x.shape[0]
    sds = jax.ShapeDtypeStruct
    brow = warrs[0].shape[1]
    row = lambda c: pl.BlockSpec((tile, c), lambda i, me: (i, 0))
    one = lambda s: pl.BlockSpec(s, lambda i, me: (0,) * len(s), pipeline_mode=pl.Buffered(1))
    ins = [x, g] + list(o_list) + [vin, bi] + list(warrs)
    in_specs = [row(D), row(D)] + [row(GROUP)] * 4 + [one(vin.shape), one(bi.shape)] + [pl.BlockSpec(memory_space=pl.ANY)] * len(warrs)
    outs = [sds((T, D), bf), sds((T, D), f32), sds((T, D), bf), sds((4, D, GROUP), bf), sds((8, D), f32), sds((8, FF), f32)]
    out_specs = [row(D), row(D), row(D), one((4, D, GROUP)), one((8, D)), one((8, FF))]
    for wa in warrs:
        outs.append(sds(wa.shape, bf))
        out_specs.append(one(wa.shape))
    return pl.pallas_call(
        functools.partial(mlp_kernel, (places, nblk, brow)), out_shape=outs,
        grid_spec=pltpu.PrefetchScalarGridSpec(
            num_scalar_prefetch=1, grid=(T // tile,), in_specs=in_specs, out_specs=out_specs,
            scratch_shapes=[pltpu.VMEM((4, D, 1152), bf), pltpu.VMEM((4, D, 1152), f32), pltpu.SemaphoreType.DMA((len(places),))]),
        compiler_params=pltpu.CompilerParams(vmem_limit_bytes=56 * 2**20),
        cost_estimate=pl.CostEstimate(flops=T * 16 * 10**6, bytes_accessed=30 * 10**6, transcendentals=T * FF * 2),
    )(me, *ins)


def place_onehot():
    at = np.arange(PLACES)
    code = (at // 7) * 13 + at % 7
    off = code[None, :] - code[:, None] + 84
    return (off.reshape(-1)[None, :] == np.arange(SPACE)[:, None]).astype(np.float32)


def spread_table(table):
    n = table.shape[0]
    t = jnp.dot(table.astype(bf).reshape(n * 15, SPACE), jnp.asarray(place_onehot(), bf), preferred_element_type=f32)
    t = t.reshape(n, 15, PLACES, PLACES).transpose(0, 2, 1, 3).reshape(n, PLACES, 15 * PLACES) * log2e
    return jnp.pad(t, ((0, 0), (0, 56 - PLACES), (0, 768 - 15 * PLACES)))


def fold_table(t2):
    n = t2.shape[0]
    t = t2[:, :PLACES, :15 * PLACES].reshape(n, PLACES, 15, PLACES).transpose(0, 2, 1, 3).reshape(n * 15, PLACES * PLACES)
    return lax.dot_general(t, jnp.asarray(place_onehot()), (((1,), (1,)), ((), ())), preferred_element_type=f32).reshape(n, TABLE)


def swap(x, axis, bit):
    return lax.ppermute(x, axis, [(i, i ^ bit) for i in range(lax.axis_size(axis))])


def xor_onehot(me, n):
    at = jnp.arange(n)
    return ((at[:, None] ^ at[None, :]) == me)


def xor_order(x, me):
    hot = xor_onehot(me, x.shape[0]).astype(f32)
    return jnp.sum(hot.reshape(hot.shape + (1,) * (x.ndim - 1)) * x[None], axis=1)


Z1, Z0, Y, X, C = ("dp", 4), ("dp", 2), ("dp", 1), ("mp", 2), ("mp", 1)
DP_BLOCKS = [(p & 1) * 4 + (p & 2) + (p >> 2) for p in range(8)]
ORDER_A = [Z1, Z0, Y, X]
ORDER_B = [Z1, Z0, X, Y]


def rest_places():
    out = []
    for arr in range(4):
        for i in range(16):
            first, second = i >> 3, (i >> 2) & 1
            x, y = (first, second) if arr < 2 else (second, first)
            out.append((arr, i, (arr % 2) + 2 * x, (i & 1) * 4 + (i & 2) + y, 32 * (arr // 2)))
    return out


def gather(x, order):
    for axis, bit in order:
        x = jnp.concatenate([x, swap(x, axis, bit)], axis=0)
    return x


def scatter(g, order):
    for axis, bit in order[::-1]:
        half = g.shape[0] // 2
        g = g[:half] + swap(g[half:], axis, bit)
    return g


def canonical(a, parts):
    m, d, rows, width = a.shape
    own = width // parts
    a = a.reshape(4, m // 4, d, rows, parts, own).transpose(0, 2, 3, 4, 1, 5)
    return a.reshape(4, d * rows, parts * (m // 4) * own)


def uncanonical(a, parts, m, d):
    own = a.shape[2] // parts // (m // 4)
    a = a.reshape(4, d, D // d, parts, m // 4, own).transpose(0, 4, 1, 2, 3, 5)
    return a.reshape(m, d, D // d, parts * own)


def shards(tokens, regions, first_gain, first_shift, triple_weight, query_bias, value_bias, offset_table, output_weight,
           output_bias, second_gain, second_shift, inner_weight, inner_bias, outer_weight, outer_bias, cotangent):
    ndp, nmp = lax.axis_size("dp"), lax.axis_size("mp")
    me_dp, me_mp = lax.axis_index("dp"), lax.axis_index("mp")
    fast = (ndp, nmp) == (8, 4)
    T = tokens.shape[0]
    nw = T // WIN
    rows, own = D // ndp, D // nmp
    both = ("mp", "dp")

    triple_local = triple_weight.transpose(1, 0, 2).reshape(rows, 3 * own).astype(bf)
    rest_local = [output_weight.T.astype(bf), inner_weight.astype(bf), outer_weight.T.astype(bf)]
    small = jnp.concatenate([first_gain, first_shift, query_bias, value_bias, output_bias, second_gain, second_shift,
                             outer_bias, inner_bias]).astype(bf)
    if fast:
        me = me_dp.astype(jnp.int32).reshape(1)
        group_me = me_mp
        pad = jnp.pad(small, (0, 16 * 384 - small.shape[0])).reshape(16, 384)
        packed = gather(jnp.concatenate([triple_local, pad], axis=0)[None], [Z1, Z0, Y])
        hot = xor_onehot(me_dp, 8)[:, np.array(DP_BLOCKS)].astype(bf)
        small_all = jnp.dot(hot, packed[:, 64:66].reshape(8, 768), preferred_element_type=f32)
        w0 = packed[:, :64]
        w1 = swap(w0, *C)
        w2 = swap(w0, *X)
        w3 = swap(w2, *C)
        wblocks = [w0, w1, w2, w3]
        blocks = DP_BLOCKS
        t0 = offset_table.astype(bf)
        t01 = jnp.concatenate([t0, swap(t0, *C)], axis=0)
        tables = jnp.concatenate([t01, swap(t01, *X)], axis=0)
        rest = jnp.concatenate(rest_local, axis=1)
        ra = gather(rest[None, :32], ORDER_A)
        rb = gather(rest[None, 32:], ORDER_B)
        warrs = [ra, swap(ra, *C), rb, swap(rb, *C)]
        places = rest_places()
    else:
        me = jnp.zeros((1,), jnp.int32)
        group_me = jnp.int32(0)
        small_all = lax.all_gather(small, "dp").astype(f32)
        shape = (nmp, ndp, rows, -1)
        wcanon = canonical(lax.all_gather(triple_local, both).reshape(shape), 3)
        wblocks = [wcanon[k:k + 1] for k in range(4)]
        blocks = [0]
        tables = lax.all_gather(offset_table.astype(bf), "mp", tiled=True)
        warrs = [jnp.concatenate([canonical(lax.all_gather(r, both).reshape(shape), 1) for r in rest_local], axis=2)]
        places = [(0, k, k, 0, 0) for k in range(4)]
    nblk = len(blocks)
    eight = small_all[:, :8 * rows].reshape(ndp, 8, rows).transpose(1, 0, 2).reshape(8, D)
    bi = xor_order(small_all[:, 8 * rows:].reshape(4, 512), group_me).reshape(1, FF)
    ln1 = jnp.pad(eight[0:2], ((0, 6), (0, 0)))
    qv = xor_order(eight[2:4].reshape(2, 4, GROUP).transpose(1, 0, 2), group_me)
    qv = jnp.pad(qv, ((0, 0), (0, 6), (0, 0)))
    vin = jnp.pad(eight[4:8], ((0, 4), (0, 0)))
    t2 = spread_table(tables)

    mine = lax.dynamic_slice_in_dim(regions, me_mp * nw, nw)
    rr, rc = mine[:, None, :], mine[:, :, None]
    x3 = tokens.reshape(nw, WIN, D)
    saved = []
    for k in range(4):
        t2k = t2[4 * k:4 * k + 4]
        if k == 0:
            n1, *kept = attend_fwd(True, me, x3, ln1, wblocks[k], qv[k], t2k, rr, rc, blocks)
        else:
            kept = attend_fwd(False, me, n1, None, wblocks[k], qv[k], t2k, rr, rc, blocks)
        saved.append(kept)
    tile = 392 if T % 392 == 0 else T
    flat = lambda a: a.reshape(T, a.shape[-1])
    result, dy, dyb, wo, vec, dbi, *rest_grads = mlp(
        me, tokens, cotangent, [flat(s[3]) for s in saved], vin, bi, warrs, places, nblk, tile)
    peaks = jnp.stack([jnp.max(s[5], axis=(1, 2)) for s in saved]) * (1.0 / log2e)
    peaks = xor_order(peaks, group_me).reshape(1, HEADS)

    grads = {}
    dn = None
    for k in (3, 2, 1, 0):
        qkv, e, ot, _, linv, _, w = saved[k]
        last = (x3, dy.reshape(nw, WIN, D), ln1) if k == 0 else None
        out = attend_bwd(me, n1, qkv, e, ot, linv, dyb.reshape(nw, WIN, D), wo[k], w, dn, last, blocks)
        dn = out[0]
        grads[k] = out[1:]
    dx = dn.reshape(T, D)
    lnvec = grads[0][3]

    sums1 = jnp.concatenate([vec[0:4].reshape(-1), xor_order(dbi[0].reshape(4, 512), group_me).reshape(-1)])
    table_grads = [fold_table(grads[k][1]) for k in range(4)]
    qvg = xor_order(jnp.stack([grads[k][2][0:2] for k in range(4)]), group_me)
    sums2 = jnp.concatenate([lnvec[0:2].reshape(-1), qvg.transpose(1, 0, 2).reshape(-1)])
    if fast:
        v = jnp.concatenate([sums1, jnp.pad(peaks[0], (0, 128 - HEADS))]).reshape(33, 128)
        top = lax.broadcasted_iota(jnp.int32, (33, 128), 0) == 32
        for axis, bit in (C, X, Y, Z0, Z1):
            r = swap(v, axis, bit)
            v = jnp.where(top, jnp.maximum(v, r), v + r)
        sums1 = v[:32].reshape(-1)
        peaks = v[32, :HEADS]
        ka, sa, kb, sb = rest_grads
        ga = scatter(ka + swap(sa, *C), ORDER_A)
        gb = scatter(kb + swap(sb, *C), ORDER_B)
        rest_sum = jnp.concatenate([ga[0], gb[0]], axis=0).astype(f32)
        d2 = grads[2][0] + swap(grads[3][0], *C)
        d0 = grads[0][0] + swap(grads[1][0], *C) + swap(d2, *X)
        triple_sum = scatter(d0, [Z1, Z0, Y])[0].astype(f32)
        tg2 = table_grads[2] + swap(table_grads[3], *C)
        tg = table_grads[0] + swap(table_grads[1], *C) + swap(tg2, *X)
        for step in (Y, Z0, Z1):
            tg = tg + swap(tg, *step)
        for step in (C, X, Y, Z0, Z1):
            sums2 = sums2 + swap(sums2, *step)
    else:
        sums1 = lax.psum(sums1, both)
        sums2 = lax.psum(sums2, both)
        peaks = lax.pmax(peaks[0], both)
        tg = lax.dynamic_slice_in_dim(lax.psum(jnp.concatenate(table_grads), both), me_mp * (HEADS // nmp), HEADS // nmp)
        reduce = lambda a, parts: lax.psum_scatter(
            uncanonical(a, parts, nmp, ndp).reshape(nmp * ndp, rows, -1), both, tiled=True)[0].astype(f32)
        triple_sum = reduce(jnp.concatenate([grads[k][0] for k in range(4)]), 3)
        rg = rest_grads[0]
        rest_sum = jnp.concatenate([reduce(rg[:, :, :128], 1), reduce(rg[:, :, 128:640], 1), reduce(rg[:, :, 640:], 1)], axis=1)

    flat_index = me_dp * nmp + me_mp
    count = ndp * nmp

    def piece(vector):
        width = vector.shape[0] // count
        return lax.dynamic_slice_in_dim(vector, flat_index * width, width)

    my_peaks = lax.dynamic_slice_in_dim(peaks, me_mp * (HEADS // nmp), HEADS // nmp)
    factor = clip_target / jnp.maximum(my_peaks, clip_target)
    clipped = triple_weight[:2] * jnp.repeat(jnp.sqrt(factor), HEAD_DIM)[None, None, :]
    wide = 512 * 4 // nmp
    return (result, dx, piece(sums2[0:512]), piece(sums2[512:1024]),
            triple_sum.reshape(rows, 3, own).transpose(1, 0, 2),
            piece(sums2[1024:1536]), piece(sums2[1536:2048]), tg,
            rest_sum[:, :own].T, piece(sums1[1536:2048]), piece(sums1[512:1024]), piece(sums1[1024:1536]),
            rest_sum[:, own:own + wide], piece(sums1[2048:4096]), rest_sum[:, own + wide:].T, piece(sums1[0:512]),
            my_peaks, clipped)


def solution(mesh):
    rows = P(("dp", "mp"), None)
    vector = P("dp")
    every = P(("dp", "mp"))
    three = P(None, "dp", "mp")
    down, across = P("mp", "dp"), P("dp", "mp")
    return jax.shard_map(
        shards,
        mesh=mesh,
        in_specs=(rows, P("dp", None), vector, vector, three, vector, vector, P("mp", None), down, vector, vector, vector,
                  across, vector, down, vector, rows),
        out_specs=(rows, rows, every, every, three, every, every, P("mp", None), down, every, every, every, across, every,
                   down, every, P("mp"), three),
        check_vma=False,
    )
```

```python
import functools
import math

import jax
import jax.numpy as jnp
import numpy as np
from jax import lax
from jax.experimental import pallas as pl
from jax.experimental.pallas import tpu as pltpu
from jax.sharding import PartitionSpec as P

D = 512
HEADS = 16
HEAD_DIM = 32
FF = 2048
WIN = 392
PLACES = 49
TIMES = 8
SPACE = 169
TABLE = 2535
TLANES = 2560
GROUP = 128
QKV = 384
REST = 1152
SMALL = 16
SLANES = 8 * QKV
norm_epsilon = 1e-05
masked_score = -1e9
clip_target = 10.0
log2e = math.log2(math.e)
score_scale = 1.0 / math.sqrt(HEAD_DIM)
bf = jnp.bfloat16
f32 = jnp.float32
ROWS = [(s, min(64, WIN - s)) for s in range(0, WIN, 64)]
VMEM_ALL = 63 * 2**20
sds = jax.ShapeDtypeStruct


def dd(a, b, ca, cb):
    return lax.dot_general(a, b, (((ca,), (cb,)), ((), ())), preferred_element_type=f32)


def fold_max(acc, x):
    for r in range(0, x.shape[0], 8):
        acc = jnp.maximum(acc, x[r:r + 8])
    return acc


def full(shape):
    return pl.BlockSpec(shape, lambda w, me: (0,) * len(shape), pipeline_mode=pl.Buffered(1))


def win(shape):
    return pl.BlockSpec((1,) + shape, lambda w, me: (w,) + (0,) * len(shape))


HBM = pl.BlockSpec(memory_space=pl.ANY)


def small_vector(small, row):
    return jnp.concatenate([small[row:row + 1, d * QKV:d * QKV + 64] for d in range(8)], axis=1)


def group_vector(small, row, group):
    parts = []
    for half in range(2):
        at = pl.multiple_of((group * 2 + half) * QKV, 128)
        parts.append(small[row:row + 1, pl.ds(at, 128)][:, :64])
    return jnp.concatenate(parts, axis=1)


def pack_kernel(tri, outw, inner, outer, table, *refs):
    smalls, (pk, rest, tab) = refs[:9], refs[9:]
    for c in range(3):
        pk[0:64, c * 128:(c + 1) * 128] = tri[c].astype(bf)
    rows = [jnp.pad(s[...].reshape(1, -1), ((0, 0), (0, QKV - s.shape[0]))) for s in smalls]
    pk[64:80, :] = jnp.concatenate(rows + [jnp.zeros((7, QKV), f32)], axis=0).astype(bf)
    rest[:, 0:128] = outw[...].T.astype(bf)
    rest[:, 128:640] = inner[...].astype(bf)
    rest[:, 640:1152] = outer[...].T.astype(bf)
    t = jnp.pad(table[...], ((0, 0), (0, TLANES - TABLE)))
    tab[...] = jnp.concatenate([t[h:h + 1, c * 640:(c + 1) * 640] for h in range(4) for c in range(4)], axis=0).astype(bf)


def pack(*params):
    return pl.pallas_call(
        pack_kernel,
        out_shape=[sds((80, QKV), bf), sds((64, REST), bf), sds((16, 640), bf)],
        compiler_params=pltpu.CompilerParams(vmem_limit_bytes=VMEM_ALL),
    )(*params)


def place_onehot():
    at = np.arange(PLACES)
    code = (at // 7) * 13 + at % 7
    hot = np.zeros((TLANES, 768), np.float32)
    for a in range(15):
        hot[a * SPACE + code, a * PLACES + at] = 1.0
    return hot.astype(bf)


def grid_kernel(t0, t1, t2, t3, hot, out, rolled, spread):
    g = pl.program_id(0)
    for k, t in enumerate((t0, t1, t2, t3)):
        @pl.when(g == k)
        def _(t=t):
            for h in range(4):
                flat = jnp.concatenate([t[4 * h + c:4 * h + c + 1] for c in range(4)], axis=1).astype(f32)
                steps = pltpu.roll(jnp.broadcast_to(flat, (8, TLANES)), 0, 1, stride=1, stride_axis=0)
                for y in range(7):
                    rolled[h * 56 + y * 7:h * 56 + y * 7 + 8, :] = pltpu.roll(steps, TLANES - (84 - 13 * y), 1)
    spread[...] = dd(rolled[0:224].astype(bf), hot[...], 1, 0) * log2e
    for h in range(4):
        for t in range(TIMES):
            lo = (7 - t) * PLACES
            out[h, t * PLACES:(t + 1) * PLACES, :] = spread[h * 56:h * 56 + PLACES, lo:lo + WIN]


def bias_grid(tables, hot):
    whole = lambda s: pl.BlockSpec(s, lambda g: (0,) * len(s), pipeline_mode=pl.Buffered(1))
    return pl.pallas_call(
        grid_kernel, grid=(4,), out_shape=sds((HEADS, WIN, WIN), f32),
        in_specs=[whole((16, 640))] * 4 + [whole((TLANES, 768))],
        out_specs=pl.BlockSpec((4, WIN, WIN), lambda g: (g, 0, 0)),
        scratch_shapes=[pltpu.VMEM((232, TLANES), f32), pltpu.VMEM((224, 768), f32)],
        compiler_params=pltpu.CompilerParams(vmem_limit_bytes=VMEM_ALL),
        cost_estimate=pl.CostEstimate(flops=4 * 10**9, bytes_accessed=2 * 10**7, transcendentals=0),
    )(*tables, hot)


def fwd_kernel(first, k, nwin, blocks, *refs):
    refs = list(refs)
    take = lambda n: [refs.pop(0) for _ in range(n)]
    me_ref, x_ref, w_hbm = take(3)
    s_in, = take(1)
    bias_hbm, reg_ref = take(2)
    if first:
        n1_out, s_out = take(2)
    qkv_out, e_out, ot_out, o_out, linv_out, hm_out, w_out = take(7)
    bias, mask, s_scr, hm_scr, wsem, bsem = take(6)
    if first:
        s_bf, ssem = take(2)
    w = pl.program_id(0)
    group = me_ref[1] ^ k
    rows = D // len(blocks)
    bias_copy = pltpu.make_async_copy(bias_hbm.at[pl.ds(4 * k, 4)], bias, bsem)

    @pl.when(w == 0)
    def _():
        bias_copy.start()
        copies = []
        for p, blk in enumerate(blocks):
            at = pl.multiple_of((me_ref[0] ^ blk) * rows, rows)
            copies.append(pltpu.make_async_copy(w_hbm.at[p, 0:rows], w_out.at[pl.ds(at, rows)], wsem.at[p]))
        if first:
            at_row = s_in.shape[1] - SMALL
            order = blocks if len(blocks) == 8 else list(range(8))
            for p, blk in enumerate(order):
                at = pl.multiple_of((me_ref[0] ^ blk) * QKV, 128)
                copies.append(pltpu.make_async_copy(
                    s_in.at[p, at_row:at_row + SMALL], s_bf.at[:, pl.ds(at, QKV)], ssem.at[p]))
        for c in copies:
            c.start()
        for c in copies:
            c.wait()
        if first:
            s_out[...] = s_bf[...].astype(f32)
        hm_scr[...] = jnp.full(hm_scr.shape, -jnp.inf, f32)

    small = s_out if first else s_in
    region = reg_ref[pl.ds(me_ref[2] + w, 1), :].astype(f32)
    column = jnp.broadcast_to(region, (8, WIN)).T[:, 0:1]
    mask[...] = jnp.where(column == region, 0.0, masked_score)
    if first:
        x = x_ref[0].astype(f32)
        xc = x - jnp.mean(x, axis=1, keepdims=True)
        inv = lax.rsqrt(jnp.mean(xc * xc, axis=1, keepdims=True) + norm_epsilon)
        n1 = (xc * inv * small_vector(small, 0) + small_vector(small, 1)).astype(bf)
        n1_out[0] = n1
    else:
        n1 = x_ref[0]
    p = dd(n1, w_out[...], 1, 0)
    q = (p[:, :128] + group_vector(small, 2, group)) * (score_scale * log2e)
    kb = p[:, 128:256].astype(bf)
    v = p[:, 256:] + group_vector(small, 3, group)
    qkv_out[0, :, 0:128] = q.astype(bf)
    qkv_out[0, :, 128:256] = kb
    qkv_out[0, :, 256:384] = v.astype(bf)
    qT = q.T.astype(bf)
    vT = v.T.astype(bf)
    ones = jnp.ones((16, WIN), bf)

    @pl.when(w == 0)
    def _():
        bias_copy.wait()

    outs, linvs = [], []
    for h in range(4):
        sl = slice(h * 32, h * 32 + 32)
        s_scr[...] = dd(kb[:, sl], qT[sl], 1, 0)
        hm = jnp.full((8, WIN), -jnp.inf, f32)
        m = jnp.full((8, WIN), -jnp.inf, f32)
        for r, n in ROWS:
            c = s_scr[r:r + n]
            hm = fold_max(hm, c)
            c = c + bias[h, r:r + n] + mask[r:r + n]
            m = fold_max(m, c)
            s_scr[r:r + n] = c
        hm_scr[h] = jnp.maximum(hm_scr[h], hm)
        m = jnp.max(m, axis=0, keepdims=True)
        for r, n in ROWS:
            e_out[0, h, r:r + n] = jnp.exp2(s_scr[r:r + n] - m).astype(bf)
        ol = dd(jnp.concatenate([vT[sl], ones], axis=0), e_out[0, h], 1, 0)
        linv = 1.0 / ol[32:33]
        linvs.append(linv)
        outs.append(ol[:32] * linv)
    oT = jnp.concatenate(outs, axis=0)
    ot_out[0] = oT.astype(bf)
    o_out[0] = oT.T.astype(bf)
    linv_out[0] = jnp.concatenate(linvs + [jnp.zeros((4, WIN), f32)], axis=0)

    @pl.when(w == nwin - 1)
    def _():
        tops = [jnp.broadcast_to(jnp.max(hm_scr[h], keepdims=True), (1, 128)) for h in range(4)]
        hm_out[...] = jnp.concatenate(tops + [jnp.zeros((4, 128), f32)], axis=0) * (1.0 / log2e)


def attend_fwd(k, me, x, wblk, small, bias, regions, blocks):
    first = k == 0
    nw = x.shape[0]
    ins = [x, wblk, small, bias, regions]
    in_specs = [win((WIN, D)), HBM, HBM if first else full(small.shape), HBM, full(regions.shape)]
    outs = ([sds((nw, WIN, D), bf), sds((SMALL, SLANES), f32)] if first else []) + [
        sds((nw, WIN, QKV), bf), sds((nw, 4, WIN, WIN), bf), sds((nw, GROUP, WIN), bf), sds((nw, WIN, GROUP), bf),
        sds((nw, 8, WIN), f32), sds((8, 128), f32), sds((D, QKV), bf)]
    out_specs = ([win((WIN, D)), full((SMALL, SLANES))] if first else []) + [
        win((WIN, QKV)), win((4, WIN, WIN)), win((GROUP, WIN)), win((WIN, GROUP)), win((8, WIN)),
        full((8, 128)), full((D, QKV))]
    scratch = [pltpu.VMEM((4, WIN, WIN), f32), pltpu.VMEM((WIN, WIN), f32), pltpu.VMEM((WIN, WIN), f32),
               pltpu.VMEM((4, 8, WIN), f32), pltpu.SemaphoreType.DMA((len(blocks),)), pltpu.SemaphoreType.DMA]
    if first:
        scratch += [pltpu.VMEM((SMALL, SLANES), bf), pltpu.SemaphoreType.DMA((8,))]
    return pl.pallas_call(
        functools.partial(fwd_kernel, first, k, nw, blocks), out_shape=outs,
        grid_spec=pltpu.PrefetchScalarGridSpec(
            num_scalar_prefetch=1, grid=(nw,), in_specs=in_specs, out_specs=out_specs, scratch_shapes=scratch),
        compiler_params=pltpu.CompilerParams(vmem_limit_bytes=VMEM_ALL),
        cost_estimate=pl.CostEstimate(flops=nw * 3 * 10**9, bytes_accessed=nw * 4 * 10**6, transcendentals=nw * 4 * WIN * WIN),
    )(me, *ins)


def bwd_kernel(first, last, nwin, blocks, *refs):
    refs = list(refs)
    take = lambda n: [refs.pop(0) for _ in range(n)]
    me_ref, n1_ref, qkv_ref, e_ref, ot_ref, linv_ref, dyb_ref, wo_ref, w_ref, hot_hbm = take(10)
    prev_ref = None if first else take(1)[0]
    if last:
        x_ref, dy_ref, small_ref = take(3)
    dn_out, dw_out, tab_out, vec_out = take(4)
    if last:
        ln_out, = take(1)
    dwacc, dls, p_scr, dl_scr, hot, spread, rolled, hsem = take(8)
    w = pl.program_id(0)
    hot_copy = pltpu.make_async_copy(hot_hbm, hot, hsem)

    @pl.when(w == 0)
    def _():
        hot_copy.start()
        dwacc[...] = jnp.zeros(dwacc.shape, f32)
        dls[...] = jnp.zeros(dls.shape, f32)
        vec_out[...] = jnp.zeros(vec_out.shape, f32)
        if last:
            ln_out[...] = jnp.zeros(ln_out.shape, f32)

    q = qkv_ref[0, :, 0:128]
    k = qkv_ref[0, :, 128:256]
    v = qkv_ref[0, :, 256:384]
    do = dd(dyb_ref[0], wo_ref[...], 1, 0)
    doT = do.T
    oT = ot_ref[0].astype(f32)
    scaled = []
    rs = []
    for h in range(4):
        sl = slice(h * 32, h * 32 + 32)
        s = (doT[sl] * linv_ref[0, h:h + 1]).astype(bf)
        scaled.append(s)
        rs.append(jnp.sum(s.astype(f32) * oT[sl], axis=0, keepdims=True))
    doTs = jnp.concatenate(scaled, axis=0)
    dos = doTs.astype(f32).T.astype(bf)
    kT = k.astype(f32).T.astype(bf)
    lane = lax.broadcasted_iota(jnp.int32, (1, 128), 1) // 32
    dk = jnp.zeros((WIN, 128), f32)
    dv = jnp.zeros((WIN, 128), f32)
    dqT = []
    for h in range(4):
        sl = slice(h * 32, h * 32 + 32)
        p_scr[...] = dd(v[:, sl], doTs[sl], 1, 0)
        for r, n in ROWS:
            dl = e_ref[0, h, r:r + n].astype(f32) * (p_scr[r:r + n] - rs[h])
            dls[h, r:r + n] += dl
            dl_scr[r:r + n] = dl.astype(bf)
        dqT.append(dd(kT[sl], dl_scr[...], 1, 0))
        own = lane == h
        dk += dd(dl_scr[...], jnp.where(own, q, jnp.zeros((), bf)), 1, 0)
        dv += dd(e_ref[0, h], jnp.where(own, dos, jnp.zeros((), bf)), 1, 0)
    dq = jnp.concatenate(dqT, axis=0).T * score_scale
    dk = dk * (1.0 / log2e)
    vec_out[0:1] += jnp.sum(dq, axis=0, keepdims=True)
    vec_out[1:2] += jnp.sum(dv, axis=0, keepdims=True)
    dqkv = jnp.concatenate([dq.astype(bf), dk.astype(bf), dv.astype(bf)], axis=1)
    dwacc[...] += dd(n1_ref[0], dqkv, 0, 0)
    dn1 = dd(dqkv, w_ref[...], 1, 1)
    if not first:
        dn1 = dn1 + prev_ref[0]
    if last:
        x = x_ref[0].astype(f32)
        xc = x - jnp.mean(x, axis=1, keepdims=True)
        inv = lax.rsqrt(jnp.mean(xc * xc, axis=1, keepdims=True) + norm_epsilon)
        u = xc * inv
        ln_out[0:1] += jnp.sum(dn1 * u, axis=0, keepdims=True)
        ln_out[1:2] += jnp.sum(dn1, axis=0, keepdims=True)
        a = dn1 * small_vector(small_ref, 0)
        g = inv * (a - jnp.mean(a, axis=1, keepdims=True) - u * jnp.mean(a * u, axis=1, keepdims=True))
        dn_out[0] = (dy_ref[0] + g).astype(bf)
    else:
        dn_out[0] = dn1

    @pl.when(w == nwin - 1)
    def _():
        rows = D // len(blocks)
        for kk, blk in enumerate(blocks):
            at = pl.multiple_of((me_ref[0] ^ blk) * rows, rows)
            dw_out[kk * rows:(kk + 1) * rows] = dwacc[pl.ds(at, rows), :].astype(bf)
        spread[...] = jnp.zeros(spread.shape, f32)
        for h in range(4):
            for t in range(TIMES):
                lo = (7 - t) * PLACES
                spread[h * 56:h * 56 + PLACES, lo:lo + WIN] += dls[h, t * PLACES:(t + 1) * PLACES, :]
        hot_copy.wait()
        rolled[0:224] = dd(spread[...].astype(bf), hot[...], 1, 1)
        rolled[224:232] = jnp.zeros((8, TLANES), f32)
        row = lax.broadcasted_iota(jnp.int32, (8, 1), 0)
        for h in range(4):
            acc = jnp.zeros((8, TLANES), f32)
            for y in range(7):
                part = rolled[h * 56 + y * 7:h * 56 + y * 7 + 8, :]
                acc += pltpu.roll(jnp.where(row < 7, part, 0.0), 84 - 13 * y, 1)
            for bit in (1, 2, 4):
                acc = jnp.where((row & bit) != 0, pltpu.roll(acc, TLANES - bit, 1), acc)
            flat = jnp.sum(acc, axis=0, keepdims=True)
            for c in range(7):
                hi = min(QKV, TLANES - c * QKV)
                tab_out[h * 7 + c:h * 7 + c + 1, 0:hi] = flat[:, c * QKV:c * QKV + hi]
                if hi < QKV:
                    tab_out[h * 7 + c:h * 7 + c + 1, hi:QKV] = jnp.zeros((1, QKV - hi), f32)
        tab_out[28:32] = jnp.zeros((4, QKV), f32)


def attend_bwd(me, n1, qkv, e, oT, linv, dyb, wo, w, hot, prev, last, blocks):
    nw = n1.shape[0]
    first = prev is None
    ins = [n1, qkv, e, oT, linv, dyb, wo, w, hot] + ([] if first else [prev]) + (list(last) if last else [])
    in_specs = ([win((WIN, D)), win((WIN, QKV)), win((4, WIN, WIN)), win((GROUP, WIN)), win((8, WIN)), win((WIN, D)),
                 full((D, GROUP)), full((D, QKV)), HBM] + ([] if first else [win((WIN, D))]) +
                ([win((WIN, D)), win((WIN, D)), full(last[2].shape)] if last else []))
    outs = [sds((nw, WIN, D), bf if last else f32), sds((D, QKV), bf), sds((32, QKV), f32), sds((8, 128), f32)]
    out_specs = [win((WIN, D)), full((D, QKV)), full((32, QKV)), full((8, 128))]
    if last:
        outs.append(sds((8, D), f32))
        out_specs.append(full((8, D)))
    return pl.pallas_call(
        functools.partial(bwd_kernel, first, bool(last), nw, blocks), out_shape=outs,
        grid_spec=pltpu.PrefetchScalarGridSpec(
            num_scalar_prefetch=1, grid=(nw,), in_specs=in_specs, out_specs=out_specs,
            scratch_shapes=[pltpu.VMEM((D, QKV), f32), pltpu.VMEM((4, WIN, WIN), f32), pltpu.VMEM((WIN, WIN), f32),
                            pltpu.VMEM((WIN, WIN), bf), pltpu.VMEM((TLANES, 768), bf), pltpu.VMEM((224, 768), f32),
                            pltpu.VMEM((232, TLANES), f32), pltpu.SemaphoreType.DMA]),
        compiler_params=pltpu.CompilerParams(vmem_limit_bytes=VMEM_ALL),
        cost_estimate=pl.CostEstimate(flops=nw * 4 * 10**9, bytes_accessed=nw * 5 * 10**6, transcendentals=0),
    )(me, *ins)


def mlp_kernel(spec, *refs):
    places, brow, nkeep, narr, ntile = spec
    refs = list(refs)
    take = lambda n: [refs.pop(0) for _ in range(n)]
    me_ref, x_ref, g_ref = take(3)
    o_refs = take(4)
    small, = take(1)
    w_hbm = take(narr)
    res_out, dy_out, dyb_out, wo_out, vec_out, dbi_out = take(6)
    keeps = take(nkeep)
    send = take(1)[0] if narr > nkeep else None
    wscr, acc, vin, bi, wsem = take(5)
    t = pl.program_id(0)
    me = me_ref[0]

    @pl.when(t == 0)
    def _():
        copies = []
        for i, (arr, idx, k, blk) in enumerate(places):
            at = pl.multiple_of((me ^ blk) * brow, brow)
            copies.append(pltpu.make_async_copy(w_hbm[arr].at[idx], wscr.at[k, pl.ds(at, brow)], wsem.at[i]))
            copies[-1].start()
        for i in range(4):
            vin[i:i + 1] = small_vector(small, 4 + i)
        for k in range(4):
            for half in range(2):
                at = pl.multiple_of(((me_ref[1] ^ k) * 2 + half) * QKV, 128)
                bi[0:1, k * 512 + half * 256:k * 512 + half * 256 + 256] = small[8:9, pl.ds(at, 256)]
        acc[...] = jnp.zeros(acc.shape, f32)
        vec_out[...] = jnp.zeros(vec_out.shape, f32)
        dbi_out[...] = jnp.zeros(dbi_out.shape, f32)
        for c in copies:
            c.wait()

    y = x_ref[...].astype(f32) + vin[0:1]
    for k in range(4):
        y = y + dd(o_refs[k][...], wscr[k, :, 0:128], 1, 1)
    yc = y - jnp.mean(y, axis=1, keepdims=True)
    inv = lax.rsqrt(jnp.mean(yc * yc, axis=1, keepdims=True) + norm_epsilon)
    u = yc * inv
    n2 = (u * vin[1:2] + vin[2:3]).astype(bf)
    gb = g_ref[...]
    gT = gb.astype(f32).T.astype(bf)
    n2T = n2.astype(f32).T.astype(bf)
    ff = jnp.zeros(y.shape, f32)
    dn2 = jnp.zeros(y.shape, f32)
    for k in range(4):
        wi = wscr[k, :, 128:640]
        wo = wscr[k, :, 640:1152]
        z = dd(n2, wi, 1, 0) + bi[0:1, k * 512:(k + 1) * 512]
        ez = jnp.exp2(z * z * (-0.5 * log2e))
        tt = 1.0 / (1.0 + (0.3275911 * 0.7071067811865476) * jnp.abs(z))
        poly = tt * (0.254829592 + tt * (-0.284496736 + tt * (1.421413741 + tt * (-1.453152027 + tt * 1.061405429))))
        tail = 0.5 * poly * ez
        phi = jnp.where(z >= 0, 1.0 - tail, tail)
        hb = (z * phi).astype(bf)
        slope = phi + z * (ez * 0.3989422804014327)
        ff = ff + dd(hb, wo, 1, 1)
        dz = dd(gb, wo, 1, 0) * slope
        dbi_out[k:k + 1] += jnp.sum(dz, axis=0, keepdims=True)
        dzb = dz.astype(bf)
        dn2 = dn2 + dd(dzb, wi, 1, 1)
        acc[k, :, 640:1152] += dd(gT, hb, 1, 0)
        acc[k, :, 128:640] += dd(n2T, dzb, 1, 0)
    res_out[...] = (y + ff + vin[3:4]).astype(bf)
    g = gb.astype(f32)
    a = dn2 * vin[1:2]
    dy = g + inv * (a - jnp.mean(a, axis=1, keepdims=True) - u * jnp.mean(a * u, axis=1, keepdims=True))
    dy_out[...] = dy
    dyb_out[...] = dy.astype(bf)
    dyT = dy.T.astype(bf)
    for k in range(4):
        acc[k, :, 0:128] += dd(dyT, o_refs[k][...], 1, 0)
    vec_out[0:1] += jnp.sum(g, axis=0, keepdims=True)
    vec_out[1:2] += jnp.sum(dn2 * u, axis=0, keepdims=True)
    vec_out[2:3] += jnp.sum(dn2, axis=0, keepdims=True)
    vec_out[3:4] += jnp.sum(dy, axis=0, keepdims=True)

    @pl.when(t == ntile - 1)
    def _():
        wo_out[...] = wscr[:, :, 0:128]
        for arr, idx, k, blk in places:
            at = pl.multiple_of((me ^ blk) * brow, brow)
            block = acc[k, pl.ds(at, brow), :].astype(bf)
            if arr < nkeep:
                keeps[arr][idx] = block
            else:
                send[(arr - nkeep) * keeps[0].shape[0] + idx] = block


def mlp(me, x, g, o_list, small, warrs, places, nkeep, tile):
    T = x.shape[0]
    narr = len(warrs)
    n, brow, _ = warrs[0].shape
    row = lambda c: pl.BlockSpec((tile, c), lambda i, me: (i, 0))
    ins = [x, g] + list(o_list) + [small] + list(warrs)
    in_specs = [row(D), row(D)] + [row(GROUP)] * 4 + [full(small.shape)] + [HBM] * narr
    outs = [sds((T, D), bf), sds((T, D), f32), sds((T, D), bf), sds((4, D, GROUP), bf), sds((8, D), f32), sds((8, 512), f32)]
    out_specs = [row(D), row(D), row(D), full((4, D, GROUP)), full((8, D)), full((8, 512))]
    outs += [sds((n, brow, REST), bf)] * nkeep
    out_specs += [full((n, brow, REST))] * nkeep
    if narr > nkeep:
        outs.append(sds((n * (narr - nkeep), brow, REST), bf))
        out_specs.append(full((n * (narr - nkeep), brow, REST)))
    return pl.pallas_call(
        functools.partial(mlp_kernel, (places, brow, nkeep, narr, T // tile)), out_shape=outs,
        grid_spec=pltpu.PrefetchScalarGridSpec(
            num_scalar_prefetch=1, grid=(T // tile,), in_specs=in_specs, out_specs=out_specs,
            scratch_shapes=[pltpu.VMEM((4, D, REST), bf), pltpu.VMEM((4, D, REST), f32), pltpu.VMEM((8, D), f32),
                            pltpu.VMEM((8, FF), f32), pltpu.SemaphoreType.DMA((len(places),))]),
        compiler_params=pltpu.CompilerParams(vmem_limit_bytes=VMEM_ALL),
        cost_estimate=pl.CostEstimate(flops=T * 19 * 10**6, bytes_accessed=30 * 10**6, transcendentals=T * FF * 2),
    )(me, *ins)


def assemble_kernel(me_ref, vec, dbi, ln, q0, q1, q2, q3, p0, p1, p2, p3, out, nat):
    out[...] = jnp.zeros(out.shape, f32)
    nat[0:2] = ln[0:2]
    nat[4:8] = vec[0:4]
    lane = lax.broadcasted_iota(jnp.int32, (1, 128), 1)
    top = jnp.full((1, 128), masked_score, f32)
    for k, (q, p) in enumerate(((q0, p0), (q1, p1), (q2, p2), (q3, p3))):
        group = me_ref[1] ^ k
        at = pl.multiple_of(group * 128, 128)
        nat[2:4, pl.ds(at, 128)] = q[0:2]
        nat[pl.ds(8 + group, 1), :] = dbi[k:k + 1]
        for h in range(4):
            top = jnp.where(lane == group * 4 + h, p[h:h + 1], top)
    for i in range(12):
        out[2 * i:2 * i + 1] = nat[i:i + 1, 0:384]
        out[2 * i + 1:2 * i + 2, 0:128] = nat[i:i + 1, 384:512]
    out[24:25, 0:128] = top


def assemble(me, vec, dbi, ln, qs, ps):
    smem = pl.BlockSpec(memory_space=pltpu.SMEM)
    vmem = pl.BlockSpec(memory_space=pltpu.VMEM)
    return pl.pallas_call(
        assemble_kernel, out_shape=sds((32, QKV), f32), in_specs=[smem] + [vmem] * 11,
        scratch_shapes=[pltpu.VMEM((16, D), f32)],
        compiler_params=pltpu.CompilerParams(vmem_limit_bytes=VMEM_ALL),
    )(me, vec, dbi, ln, *qs, *ps)


def unpack_rest_kernel(rest, outw, inner, outer):
    outw[...] = rest[:, 0:128].astype(f32).T
    inner[...] = rest[:, 128:640].astype(f32)
    outer[...] = rest[:, 640:1152].astype(f32).T


def unpack_rest(rest):
    return pl.pallas_call(
        unpack_rest_kernel, out_shape=[sds((128, 64), f32), sds((64, 512), f32), sds((512, 64), f32)],
        compiler_params=pltpu.CompilerParams(vmem_limit_bytes=VMEM_ALL),
    )(rest)


def unpack_kernel(me_ref, buf, tri, triple, table, clipped, peaks, dbi, *vectors):
    flat = me_ref[3]
    b = buf[...].astype(f32)
    for c in range(3):
        triple[c] = b[0:64, c * 128:(c + 1) * 128]
    for h in range(4):
        for c in range(7):
            hi = min(QKV, TABLE - c * QKV)
            table[h:h + 1, c * QKV:c * QKV + hi] = b[64 + h * 7 + c:65 + h * 7 + c, 0:hi]
    rows = [jnp.concatenate([b[96 + 2 * i:97 + 2 * i], b[97 + 2 * i:98 + 2 * i, 0:128]], axis=1) for i in range(12)]
    first = jnp.concatenate(rows[0:8], axis=0)
    first = pltpu.roll(first, 512 - flat * 16, 1)
    for i in range(8):
        vectors[i][...] = first[i:i + 1, 0:16].reshape(16)
    wide = rows[8]
    for i in range(1, 4):
        wide = jnp.where(flat // 8 == i, rows[8 + i], wide)
    dbi[...] = pltpu.roll(jnp.broadcast_to(wide, (8, 512)), 512 - (flat % 8) * 64, 1)[0:1, 0:64].reshape(64)
    top = jnp.broadcast_to(b[120:121, 0:128], (8, 128))
    top = pltpu.roll(top, 128 - me_ref[1] * 4, 1)[0:1]
    peaks[...] = top[:, 0:4].reshape(4)
    root = jnp.sqrt(clip_target / jnp.maximum(top, clip_target))
    lane = lax.broadcasted_iota(jnp.int32, (1, 128), 1) // 32
    scale = jnp.zeros((1, 128), f32)
    for h in range(4):
        scale = jnp.where(lane == h, root[:, h:h + 1], scale)
    for c in range(2):
        clipped[c] = tri[c] * scale


def unpack(me, buf, triple_weight):
    smem = pl.BlockSpec(memory_space=pltpu.SMEM)
    vmem = pl.BlockSpec(memory_space=pltpu.VMEM)
    return pl.pallas_call(
        unpack_kernel,
        out_shape=[sds((3, 64, 128), f32), sds((4, TABLE), f32), sds((2, 64, 128), f32), sds((4,), f32), sds((64,), f32)] +
        [sds((16,), f32)] * 8,
        in_specs=[smem, vmem, vmem], compiler_params=pltpu.CompilerParams(vmem_limit_bytes=VMEM_ALL),
    )(me, buf, triple_weight)


def swap(x, axis, bit):
    return lax.ppermute(x, axis, [(i, i ^ bit) for i in range(lax.axis_size(axis))])


Z1, Z0, Y, X, C = ("dp", 4), ("dp", 2), ("dp", 1), ("mp", 2), ("mp", 1)
DP_BLOCKS = [(p & 1) * 4 + (p & 2) + (p >> 2) for p in range(8)]


def widen(x, step):
    return jnp.concatenate([x, swap(x, *step)], axis=0)


def gather_rest(rest):
    a = widen(rest[None], Z1)
    b = swap(a, *Z0)
    a0, b0 = widen(a, Y), widen(b, X)
    a1, b1 = swap(a0, *X), swap(b0, *Y)
    out = [a0, a1, b0, b1]
    return out + [swap(v, *C) for v in out]


def rest_places():
    out = []
    for arr in range(8):
        c, kind = arr >> 2, arr & 3
        for i in range(4):
            z1, z0 = i & 1, kind >> 1
            x, y = (kind & 1, i >> 1) if z0 == 0 else (i >> 1, kind & 1)
            out.append((arr, i, c + 2 * x, z1 * 4 + z0 * 2 + y))
    return out


def scatter_rest(keeps, sent):
    got = swap(sent, *C)
    a0, a1, b0, b1 = [keeps[i] + got[4 * i:4 * i + 4] for i in range(4)]
    a0 = a0 + swap(a1, *X)
    b0 = b0 + swap(b1, *Y)
    a = a0[:2] + swap(a0[2:], *Y)
    b = b0[:2] + swap(b0[2:], *X)
    a = a + swap(b, *Z0)
    return a[0] + swap(a[1], *Z1)


def canonical(a, parts):
    m, d, rows, width = a.shape
    own = width // parts
    a = a.reshape(4, m // 4, d, rows, parts, own).transpose(0, 2, 3, 4, 1, 5)
    return a.reshape(4, d * rows, parts * (m // 4) * own)


def uncanonical(a, parts, m, d):
    own = a.shape[2] // parts // (m // 4)
    a = a.reshape(4, d, D // d, parts, m // 4, own).transpose(0, 4, 1, 2, 3, 5)
    return a.reshape(m * d, D // d, parts * own)


def compute(me, tokens, cotangent, regions, wblocks, blocks, small_src, bias, hot, warrs, places, nkeep):
    T = tokens.shape[0]
    nw = T // WIN
    x3 = tokens.reshape(nw, WIN, D)
    n1, small, *kept = attend_fwd(0, me, x3, wblocks[0], small_src, bias, regions, blocks)
    saved = [kept] + [attend_fwd(k, me, n1, wblocks[k], small, bias, regions, blocks) for k in (1, 2, 3)]
    tile = 392 if T % 392 == 0 else T
    flat = lambda a: a.reshape(T, a.shape[-1])
    result, dy, dyb, wo, vec, dbi, *rest_grads = mlp(
        me, tokens, cotangent, [flat(s[3]) for s in saved], small, warrs, places, nkeep, tile)
    grads = {}
    dn = None
    for k in (3, 2, 1, 0):
        qkv, e, ot, _, linv, _, w = saved[k]
        last = (x3, dy.reshape(nw, WIN, D), small) if k == 0 else None
        out = attend_bwd(me, n1, qkv, e, ot, linv, dyb.reshape(nw, WIN, D), wo[k], w, hot, dn, last, blocks)
        dn = out[0]
        grads[k] = out[1:]
    vecs = assemble(me, vec, dbi, grads[0][3], [grads[k][2] for k in range(4)], [saved[k][5] for k in range(4)])
    return result, dn.reshape(T, D), [grads[k][0] for k in range(4)], [grads[k][1] for k in range(4)], rest_grads, vecs


def shards(tokens, regions, first_gain, first_shift, triple_weight, query_bias, value_bias, offset_table, output_weight,
           output_bias, second_gain, second_shift, inner_weight, inner_bias, outer_weight, outer_bias, cotangent):
    ndp, nmp = lax.axis_size("dp"), lax.axis_size("mp")
    me_dp, me_mp = lax.axis_index("dp"), lax.axis_index("mp")
    nw = tokens.shape[0] // WIN
    hot = jnp.asarray(place_onehot())
    smalls = [first_gain, first_shift, query_bias, value_bias, output_bias, second_gain, second_shift, outer_bias, inner_bias]
    if (ndp, nmp) == (8, 4):
        me = jnp.stack([me_dp, me_mp, me_mp * nw, me_dp * nmp + me_mp]).astype(jnp.int32)
        pk, rest, t0 = pack(triple_weight, output_weight, inner_weight, outer_weight, offset_table, *smalls)
        w0 = widen(widen(widen(pk[None], Z1), Z0), Y)
        w1 = swap(w0, *C)
        w2 = swap(w0, *X)
        w3 = swap(w2, *C)
        t2 = swap(t0, *X)
        bias = bias_grid([t0, swap(t0, *C), t2, swap(t2, *C)], hot)
        result, dx, dw, tab, rg, vecs = compute(
            me, tokens, cotangent, regions, [w0, w1, w2, w3], DP_BLOCKS, w0, bias, hot, gather_rest(rest), rest_places(), 4)
        pairs = [jnp.concatenate([dw[k], tab[k].astype(bf)], axis=0) for k in range(4)]
        far = swap(jnp.concatenate([pairs[2], pairs[3]], axis=0), *X)
        near = swap(pairs[1] + far[544:], *C)
        peak_row = lax.broadcasted_iota(jnp.int32, (32, QKV), 0) == 24
        for step in (X, C):
            got = swap(vecs, *step)
            vecs = jnp.where(peak_row, jnp.maximum(vecs, got), vecs + got)
        buf = jnp.concatenate([pairs[0] + far[:544] + near, vecs.astype(bf)], axis=0)
        for step in (Y, Z0, Z1):
            half = (buf.shape[0] - 64) // 2
            got = swap(buf[half:], *step)
            own = jnp.concatenate([buf[:half], buf[2 * half:]], axis=0)
            peak = lax.broadcasted_iota(jnp.int32, own.shape, 0) == half + 56
            buf = jnp.where(peak, jnp.maximum(own, got), own + got)
        outw, inner, outer = unpack_rest(scatter_rest(rg[:4], rg[4]))
        triple, table, clipped, peaks, dbi, *v = unpack(me, buf, triple_weight)
        return (result, dx, v[0], v[1], triple, v[2], v[3], table, outw, v[7], v[5], v[6], inner, dbi, outer, v[4], peaks, clipped)

    rows, own = D // ndp, D // nmp
    both = ("mp", "dp")
    shape = (nmp, ndp, rows, -1)
    me = jnp.stack([0 * me_dp, 0 * me_mp, me_mp * nw, me_dp * nmp + me_mp]).astype(jnp.int32)
    everywhere = lambda a: lax.all_gather(a.astype(bf), both).reshape(shape)
    wcanon = canonical(everywhere(triple_weight.transpose(1, 0, 2).reshape(rows, 3 * own)), 3)
    warrs = [jnp.concatenate([canonical(everywhere(a), 1) for a in (output_weight.T, inner_weight, outer_weight.T)], axis=2)]
    eight = lax.all_gather(jnp.stack(smalls[:8]).astype(bf), "dp", axis=1, tiled=True).reshape(8, 8, 64).transpose(1, 0, 2)
    eight = jnp.pad(eight, ((0, 0), (0, 0), (0, QKV - 64)))
    ninth = lax.all_gather(inner_bias.astype(bf), "dp", tiled=True).reshape(8, 1, 256)
    ninth = jnp.pad(ninth, ((0, 0), (0, 7), (0, QKV - 256)))
    small_src = jnp.concatenate([eight, ninth], axis=1)
    tables = lax.all_gather(offset_table.astype(bf), "mp", tiled=True)
    tables = jnp.pad(tables, ((0, 0), (0, TLANES - TABLE))).reshape(4, 16, 640)
    bias = bias_grid([tables[k] for k in range(4)], hot)
    result, dx, dw, tab, rg, vecs = compute(
        me, tokens, cotangent, regions, [wcanon[k:k + 1] for k in range(4)], [0], small_src, bias, hot,
        [warrs[0]], [(0, k, k, 0) for k in range(4)], 1)
    reduce = lambda a, parts: lax.psum_scatter(uncanonical(a, parts, nmp, ndp), both, tiled=True)[0].astype(f32)
    triple = reduce(jnp.stack(dw), 3).reshape(rows, 3, own).transpose(1, 0, 2)
    outw = reduce(rg[0][:, :, 0:128], 1).T
    inner = reduce(rg[0][:, :, 128:640], 1)
    outer = reduce(rg[0][:, :, 640:1152], 1).T
    here = HEADS // nmp
    table = lax.psum(jnp.stack(tab)[:, :28].reshape(HEADS, 7 * QKV)[:, :TABLE], both)
    table = lax.dynamic_slice_in_dim(table, me_mp * here, here)
    peaks = lax.dynamic_slice_in_dim(lax.pmax(vecs[24, :HEADS], both), me_mp * here, here)
    sums = lax.psum(vecs[:24].reshape(12, 2 * QKV)[:, :D], both)

    def piece(vector):
        width = vector.shape[0] // (ndp * nmp)
        return lax.dynamic_slice_in_dim(vector, (me_dp * nmp + me_mp) * width, width)

    factor = clip_target / jnp.maximum(peaks, clip_target)
    clipped = triple_weight[:2] * jnp.repeat(jnp.sqrt(factor), HEAD_DIM)[None, None, :]
    v = [piece(sums[i]) for i in range(8)]
    dbi = piece(sums[8:12].reshape(FF))
    return (result, dx, v[0], v[1], triple, v[2], v[3], table, outw, v[7], v[5], v[6], inner, dbi, outer, v[4], peaks, clipped)


def solution(mesh):
    rows = P(("dp", "mp"), None)
    vector = P("dp")
    every = P(("dp", "mp"))
    three = P(None, "dp", "mp")
    down, across = P("mp", "dp"), P("dp", "mp")
    return jax.shard_map(
        shards,
        mesh=mesh,
        in_specs=(rows, P("dp", None), vector, vector, three, vector, vector, P("mp", None), down, vector, vector, vector,
                  across, vector, down, vector, rows),
        out_specs=(rows, rows, every, every, three, every, every, P("mp", None), down, every, every, every, across, every,
                   down, every, P("mp"), three),
        check_vma=False,
    )
```

```python
import functools
import math

import jax
import jax.numpy as jnp
import numpy as np
from jax import lax
from jax.experimental import pallas as pl
from jax.experimental.pallas import tpu as pltpu
from jax.sharding import PartitionSpec as P

D = 512
HEADS = 16
HEAD_DIM = 32
FF = 2048
WIN = 392
PLACES = 49
TIMES = 8
SPACE = 169
TABLE = 2535
TLANES = 2560
GROUP = 128
QKV = 384
REST = 1152
SMALL = 16
SLANES = 8 * QKV
norm_epsilon = 1e-05
masked_score = -1e9
clip_target = 10.0
log2e = math.log2(math.e)
score_scale = 1.0 / math.sqrt(HEAD_DIM)
bf = jnp.bfloat16
f32 = jnp.float32
ROWS = [(s, min(64, WIN - s)) for s in range(0, WIN, 64)]
PAIR = D + 32
VMEM_ALL = 63 * 2**20
sds = jax.ShapeDtypeStruct


def dd(a, b, ca, cb):
    return lax.dot_general(a, b, (((ca,), (cb,)), ((), ())), preferred_element_type=f32)


def fold_max(acc, x):
    for r in range(0, x.shape[0], 8):
        acc = jnp.maximum(acc, x[r:r + 8])
    return acc


def full(shape):
    return pl.BlockSpec(shape, lambda w, me: (0,) * len(shape), pipeline_mode=pl.Buffered(1))


def win(shape):
    return pl.BlockSpec((1,) + shape, lambda w, me: (w,) + (0,) * len(shape))


HBM = pl.BlockSpec(memory_space=pl.ANY)


def small_vector(small, row):
    return jnp.concatenate([small[row:row + 1, d * QKV:d * QKV + 64] for d in range(8)], axis=1)


def group_vector(small, row, group):
    parts = []
    for half in range(2):
        at = pl.multiple_of((group * 2 + half) * QKV, 128)
        parts.append(small[row:row + 1, pl.ds(at, 128)][:, :64])
    return jnp.concatenate(parts, axis=1)


def pack_kernel(tri, outw, inner, outer, table, *refs):
    smalls, (pk, rest, tab) = refs[:9], refs[9:]
    for c in range(3):
        pk[0:64, c * 128:(c + 1) * 128] = tri[c].astype(bf)
    rows = [jnp.pad(s[...].reshape(1, -1), ((0, 0), (0, QKV - s.shape[0]))) for s in smalls]
    pk[64:80, :] = jnp.concatenate(rows + [jnp.zeros((7, QKV), f32)], axis=0).astype(bf)
    rest[:, 0:128] = outw[...].astype(bf)
    rest[:, 128:640] = inner[...].astype(bf)
    rest[:, 640:1152] = outer[...].astype(bf)
    t = jnp.pad(table[...], ((0, 0), (0, TLANES - TABLE)))
    tab[...] = jnp.concatenate([t[h:h + 1, c * 640:(c + 1) * 640] for h in range(4) for c in range(4)], axis=0).astype(bf)


def pack(*params):
    return pl.pallas_call(
        pack_kernel,
        out_shape=[sds((80, QKV), bf), sds((64, REST), bf), sds((16, 640), bf)],
        compiler_params=pltpu.CompilerParams(vmem_limit_bytes=VMEM_ALL),
    )(*params)


SLABS = (0, 768, 1408)
SLAB = 1152


def place_onehot():
    at = np.arange(PLACES)
    code = (at // 7) * 13 + at % 7
    hot = np.zeros((TLANES, 768), np.float32)
    for a in range(15):
        hot[a * SPACE + code, a * PLACES + at] = 1.0
    return np.stack([hot[r:r + SLAB, j * 256:(j + 1) * 256] for j, r in enumerate(SLABS)]).astype(bf)


def grid_kernel(t0, t1, hot_hbm, out_hbm, hot, rolled, spread, out, hsem, osem):
    hot_copy = pltpu.make_async_copy(hot_hbm, hot, hsem)
    hot_copy.start()
    for h in range(8):
        t = t0 if h < 4 else t1
        flat = jnp.concatenate([t[4 * (h % 4) + c:4 * (h % 4) + c + 1] for c in range(4)], axis=1).astype(f32)
        steps = pltpu.roll(jnp.broadcast_to(flat, (8, TLANES)), 0, 1, stride=1, stride_axis=0)
        for y in range(7):
            rolled[h * 56 + y * 7:h * 56 + y * 7 + 8, :] = pltpu.roll(steps, TLANES - (84 - 13 * y), 1)
    hot_copy.wait()
    copies = []
    for j, r in enumerate(SLABS):
        spread[:, j * 256:(j + 1) * 256] = dd(rolled[0:448, r:r + SLAB].astype(bf), hot[j], 1, 0) * log2e
    for h in range(8):
        for t in range(TIMES):
            lo = (7 - t) * PLACES
            out[h, t * PLACES:(t + 1) * PLACES, :] = spread[h * 56:h * 56 + PLACES, lo:lo + WIN]
        copies.append(pltpu.make_async_copy(out.at[h], out_hbm.at[h], osem.at[h]))
        copies[-1].start()
    for c in copies:
        c.wait()


def bias_grid(tables, hot):
    vmem = pl.BlockSpec(memory_space=pltpu.VMEM)
    return pl.pallas_call(
        grid_kernel, out_shape=sds((8, WIN, WIN), f32),
        in_specs=[vmem, vmem, HBM], out_specs=HBM,
        scratch_shapes=[pltpu.VMEM((3, SLAB, 256), bf), pltpu.VMEM((456, TLANES), f32), pltpu.VMEM((448, 768), f32),
                        pltpu.VMEM((8, WIN, WIN), f32), pltpu.SemaphoreType.DMA, pltpu.SemaphoreType.DMA((8,))],
        compiler_params=pltpu.CompilerParams(vmem_limit_bytes=VMEM_ALL),
        cost_estimate=pl.CostEstimate(flops=5 * 10**9, bytes_accessed=9 * 10**6, transcendentals=0),
    )(*tables, hot)


def fwd_kernel(first, ks, nwin, blocks, *refs):
    ng = len(ks)
    refs = list(refs)
    take = lambda n: [refs.pop(0) for _ in range(n)]
    me_ref, x_ref = take(2)
    w_hbm = take(ng)
    s_in, = take(1)
    bias_hbm, = take(1)
    reg_ref, = take(1)
    if first:
        n1_out, s_out = take(2)
    qkv_out, e_out, ot_out, o_out, linv_out, hm_out, w_out = take(7)
    bias, mask, s_scr, hm_scr, wsem, bsem = take(6)
    if first:
        s_bf, ssem = take(2)
    w = pl.program_id(0)
    rows = D // len(blocks)
    bias_copies = [pltpu.make_async_copy(bias_hbm.at[pl.ds(4 * g, 4)], bias.at[pl.ds(4 * g, 4)], bsem.at[g]) for g in range(ng)]

    @pl.when(w == 0)
    def _():
        copies = []
        if first:
            at_row = s_in.shape[1] - SMALL
            order = blocks if len(blocks) == 8 else list(range(8))
            for p, blk in enumerate(order):
                at = pl.multiple_of((me_ref[0] ^ blk) * QKV, 128)
                copies.append(pltpu.make_async_copy(
                    s_in.at[p, at_row:at_row + SMALL], s_bf.at[:, pl.ds(at, QKV)], ssem.at[p]))
        for g in range(ng):
            for p, blk in enumerate(blocks):
                at = pl.multiple_of((me_ref[0] ^ blk) * rows, rows)
                copies.append(pltpu.make_async_copy(
                    w_hbm[g].at[p, 0:rows], w_out.at[pl.ds(at, rows), g * QKV:(g + 1) * QKV], wsem.at[g * len(blocks) + p]))
        for c in copies + bias_copies:
            c.start()
        for c in copies:
            c.wait()
        if first:
            s_out[...] = s_bf[...].astype(f32)
        hm_scr[...] = jnp.full(hm_scr.shape, -jnp.inf, f32)

    small = s_out if first else s_in
    region = reg_ref[pl.ds(me_ref[2] + w, 1), :].astype(f32)
    column = jnp.broadcast_to(region, (8, WIN)).T[:, 0:1]
    mask[...] = jnp.where(column == region, 0.0, masked_score)
    if first:
        x = x_ref[0].astype(f32)
        xc = x - jnp.mean(x, axis=1, keepdims=True)
        inv = lax.rsqrt(jnp.mean(xc * xc, axis=1, keepdims=True) + norm_epsilon)
        n1 = (xc * inv * small_vector(small, 0) + small_vector(small, 1)).astype(bf)
        n1_out[0] = n1
    else:
        n1 = x_ref[0]
    pall = dd(n1, w_out[...], 1, 0)
    ones = jnp.ones((16, WIN), bf)
    linvs = []
    for g in range(ng):
        group = me_ref[1] ^ ks[g]
        p = pall[:, g * QKV:(g + 1) * QKV]
        q = (p[:, :128] + group_vector(small, 2, group)) * (score_scale * log2e)
        kb = p[:, 128:256].astype(bf)
        v = p[:, 256:] + group_vector(small, 3, group)
        qkv_out[0, :, g * QKV:g * QKV + 128] = q.astype(bf)
        qkv_out[0, :, g * QKV + 128:g * QKV + 256] = kb
        qkv_out[0, :, g * QKV + 256:g * QKV + 384] = v.astype(bf)
        qT = q.T.astype(bf)
        vT = v.T.astype(bf)

        @pl.when(w == 0)
        def _(g=g):
            bias_copies[g].wait()

        outs = []
        for h in range(4):
            sl = slice(h * 32, h * 32 + 32)
            s = dd(kb[:, sl], qT[sl], 1, 0)
            hm = jnp.full((8, WIN), -jnp.inf, f32)
            m = jnp.full((8, WIN), -jnp.inf, f32)
            for r, n in ROWS:
                c = s[r:r + n]
                hm = fold_max(hm, c)
                c = c + bias[4 * g + h, r:r + n] + mask[r:r + n]
                m = fold_max(m, c)
                s_scr[h % 2, r:r + n] = c
            hm_scr[4 * g + h] = jnp.maximum(hm_scr[4 * g + h], hm)
            m = jnp.max(m, axis=0, keepdims=True)
            for r, n in ROWS:
                e_out[0, 4 * g + h, r:r + n] = jnp.exp2(s_scr[h % 2, r:r + n] - m).astype(bf)
            ol = dd(jnp.concatenate([vT[sl], ones], axis=0), e_out[0, 4 * g + h], 1, 0)
            linv = 1.0 / ol[32:33]
            linvs.append(linv)
            outs.append(ol[:32] * linv)
        oT = jnp.concatenate(outs, axis=0)
        ot_out[0, g * 128:(g + 1) * 128] = oT.astype(bf)
        o_out[0, :, g * 128:(g + 1) * 128] = oT.T.astype(bf)
    if ng == 1:
        linvs.append(jnp.zeros((4, WIN), f32))
    linv_out[0] = jnp.concatenate(linvs, axis=0)

    @pl.when(w == nwin - 1)
    def _():
        tops = [jnp.broadcast_to(jnp.max(hm_scr[h], keepdims=True), (1, 128)) for h in range(4 * ng)]
        if ng == 1:
            tops.append(jnp.zeros((4, 128), f32))
        hm_out[...] = jnp.concatenate(tops, axis=0) * (1.0 / log2e)


def attend_fwd(ks, me, x, wblk, small, bias, regions, blocks):
    first = ks[0] == 0
    ng = len(ks)
    nw = x.shape[0]
    ins = [x, *wblk, small, bias, regions]
    in_specs = [win((WIN, D))] + [HBM] * ng + [HBM if first else full(small.shape), HBM, full(regions.shape)]
    outs = ([sds((nw, WIN, D), bf), sds((SMALL, SLANES), f32)] if first else []) + [
        sds((nw, WIN, ng * QKV), bf), sds((nw, ng * 4, WIN, WIN), bf), sds((nw, ng * GROUP, WIN), bf),
        sds((nw, WIN, ng * GROUP), bf), sds((nw, 8, WIN), f32), sds((8, 128), f32), sds((D, ng * QKV), bf)]
    out_specs = ([win((WIN, D)), full((SMALL, SLANES))] if first else []) + [
        win((WIN, ng * QKV)), win((ng * 4, WIN, WIN)), win((ng * GROUP, WIN)), win((WIN, ng * GROUP)), win((8, WIN)),
        full((8, 128)), full((D, ng * QKV))]
    scratch = [pltpu.VMEM((ng * 4, WIN, WIN), f32), pltpu.VMEM((WIN, WIN), f32), pltpu.VMEM((2, WIN, WIN), f32),
               pltpu.VMEM((ng * 4, 8, WIN), f32), pltpu.SemaphoreType.DMA((ng * len(blocks),)), pltpu.SemaphoreType.DMA((ng,))]
    if first:
        scratch += [pltpu.VMEM((SMALL, SLANES), bf), pltpu.SemaphoreType.DMA((8,))]
    return pl.pallas_call(
        functools.partial(fwd_kernel, first, ks, nw, blocks), out_shape=outs,
        grid_spec=pltpu.PrefetchScalarGridSpec(
            num_scalar_prefetch=1, grid=(nw,), in_specs=in_specs, out_specs=out_specs, scratch_shapes=scratch),
        compiler_params=pltpu.CompilerParams(vmem_limit_bytes=VMEM_ALL),
        cost_estimate=pl.CostEstimate(flops=ng * nw * 3 * 10**9, bytes_accessed=nw * ng * 4 * 10**6,
                                      transcendentals=ng * nw * 4 * WIN * WIN),
    )(me, *ins)


def bwd_kernel(ks, first, last, nwin, blocks, *refs):
    ng = len(ks)
    refs = list(refs)
    take = lambda n: [refs.pop(0) for _ in range(n)]
    me_ref, n1_ref, qkv_ref, e_ref, ot_ref, linv_ref, dyb_ref, wo_ref, w_ref, hot_hbm = take(10)
    prev_ref = None if first else take(1)[0]
    if last:
        x_ref, dy_ref, small_ref = take(3)
    dn_out, dw_out, vec_out = take(3)
    if last:
        ln_out, = take(1)
    dwacc, dls, p_scr, dl_scr, hot, spread, rolled, hsem = take(8)
    w = pl.program_id(0)
    hot_copy = pltpu.make_async_copy(hot_hbm, hot, hsem)

    @pl.when(w == 0)
    def _():
        hot_copy.start()
        dwacc[...] = jnp.zeros(dwacc.shape, f32)
        dls[...] = jnp.zeros(dls.shape, f32)
        vec_out[...] = jnp.zeros(vec_out.shape, f32)
        if last:
            ln_out[...] = jnp.zeros(ln_out.shape, f32)

    do_all = dd(dyb_ref[0], wo_ref[:, ks[0] * 128:(ks[0] + ng) * 128], 1, 0)
    lane = lax.broadcasted_iota(jnp.int32, (1, 128), 1) // 32
    parts = []
    for g in range(ng):
        q = qkv_ref[0, :, g * QKV:g * QKV + 128]
        k = qkv_ref[0, :, g * QKV + 128:g * QKV + 256]
        v = qkv_ref[0, :, g * QKV + 256:g * QKV + 384]
        doT = do_all[:, g * 128:(g + 1) * 128].T
        oT = ot_ref[0, g * 128:(g + 1) * 128].astype(f32)
        scaled = []
        rs = []
        for h in range(4):
            sl = slice(h * 32, h * 32 + 32)
            s = (doT[sl] * linv_ref[0, 4 * g + h:4 * g + h + 1]).astype(bf)
            scaled.append(s)
            rs.append(jnp.sum(s.astype(f32) * oT[sl], axis=0, keepdims=True))
        doTs = jnp.concatenate(scaled, axis=0)
        dos = doTs.astype(f32).T.astype(bf)
        kT = k.astype(f32).T.astype(bf)
        dk = jnp.zeros((WIN, 128), f32)
        dv = jnp.zeros((WIN, 128), f32)
        dqT = []
        for h in range(4):
            sl = slice(h * 32, h * 32 + 32)
            p = dd(v[:, sl], doTs[sl], 1, 0)
            for r, n in ROWS:
                dl = e_ref[0, 4 * g + h, r:r + n].astype(f32) * (p[r:r + n] - rs[h])
                dls[4 * g + h, r:r + n] += dl
                dl_scr[h % 2, r:r + n] = dl.astype(bf)
            dqT.append(dd(kT[sl], dl_scr[h % 2], 1, 0))
            own = lane == h
            dk += dd(dl_scr[h % 2], jnp.where(own, q, jnp.zeros((), bf)), 1, 0)
            dv += dd(e_ref[0, 4 * g + h], jnp.where(own, dos, jnp.zeros((), bf)), 1, 0)
        dq = jnp.concatenate(dqT, axis=0).T * score_scale
        dk = dk * (1.0 / log2e)
        vec_out[2 * g:2 * g + 1] += jnp.sum(dq, axis=0, keepdims=True)
        vec_out[2 * g + 1:2 * g + 2] += jnp.sum(dv, axis=0, keepdims=True)
        parts += [dq.astype(bf), dk.astype(bf), dv.astype(bf)]
    dqkv = jnp.concatenate(parts, axis=1)
    dwacc[...] += dd(n1_ref[0], dqkv, 0, 0)
    dn1 = dd(dqkv, w_ref[...], 1, 1)
    if not first:
        dn1 = dn1 + prev_ref[0]
    if last:
        x = x_ref[0].astype(f32)
        xc = x - jnp.mean(x, axis=1, keepdims=True)
        inv = lax.rsqrt(jnp.mean(xc * xc, axis=1, keepdims=True) + norm_epsilon)
        u = xc * inv
        ln_out[0:1] += jnp.sum(dn1 * u, axis=0, keepdims=True)
        ln_out[1:2] += jnp.sum(dn1, axis=0, keepdims=True)
        a = dn1 * small_vector(small_ref, 0)
        gr = inv * (a - jnp.mean(a, axis=1, keepdims=True) - u * jnp.mean(a * u, axis=1, keepdims=True))
        dn_out[0] = (dy_ref[0] + gr).astype(bf)
    else:
        dn_out[0] = dn1

    @pl.when(w == nwin - 1)
    def _():
        rows = D // len(blocks)
        spread[...] = jnp.zeros(spread.shape, f32)
        for h in range(4 * ng):
            for t in range(TIMES):
                lo = (7 - t) * PLACES
                spread[h * 56:h * 56 + PLACES, lo:lo + WIN] += dls[h, t * PLACES:(t + 1) * PLACES, :]
        for g in range(ng):
            for kk, blk in enumerate(blocks):
                at = pl.multiple_of((me_ref[0] ^ blk) * rows, rows)
                dw_out[g * PAIR + kk * rows:g * PAIR + (kk + 1) * rows] = dwacc[pl.ds(at, rows), g * QKV:(g + 1) * QKV].astype(bf)
        hot_copy.wait()
        rolled[...] = jnp.zeros(rolled.shape, f32)
        for j, r in enumerate(SLABS):
            rolled[0:224 * ng, r:r + SLAB] += dd(spread[:, j * 256:(j + 1) * 256].astype(bf), hot[j], 1, 1)
        row = lax.broadcasted_iota(jnp.int32, (8, 1), 0)
        for g in range(ng):
            lines = []
            for h in range(4 * g, 4 * g + 4):
                acc = jnp.zeros((8, TLANES), f32)
                for y in range(7):
                    part = rolled[h * 56 + y * 7:h * 56 + y * 7 + 8, :]
                    acc += pltpu.roll(jnp.where(row < 7, part, 0.0), 84 - 13 * y, 1)
                for bit in (1, 2, 4):
                    acc = jnp.where((row & bit) != 0, pltpu.roll(acc, TLANES - bit, 1), acc)
                flat = jnp.sum(acc, axis=0, keepdims=True)
                flat = jnp.concatenate([flat, jnp.zeros((1, 7 * QKV - TLANES), f32)], axis=1)
                lines += [flat[:, c * QKV:(c + 1) * QKV] for c in range(7)]
            lines.append(jnp.zeros((4, QKV), f32))
            dw_out[g * PAIR + D:(g + 1) * PAIR] = jnp.concatenate(lines, axis=0).astype(bf)


def attend_bwd(ks, me, n1, qkv, e, oT, linv, dyb, wo, w, hot, prev, last, blocks):
    ng = len(ks)
    nw = n1.shape[0]
    first = prev is None
    ins = [n1, qkv, e, oT, linv, dyb, wo, w, hot] + ([] if first else [prev]) + (list(last) if last else [])
    in_specs = ([win((WIN, D)), win((WIN, ng * QKV)), win((ng * 4, WIN, WIN)), win((ng * GROUP, WIN)), win((8, WIN)),
                 win((WIN, D)), full((D, D)), full((D, ng * QKV)), HBM] + ([] if first else [win((WIN, D))]) +
                ([win((WIN, D)), win((WIN, D)), full(last[2].shape)] if last else []))
    outs = [sds((nw, WIN, D), bf if last else f32), sds((ng * PAIR, QKV), bf), sds((8, 128), f32)]
    out_specs = [win((WIN, D)), full((ng * PAIR, QKV)), full((8, 128))]
    if last:
        outs.append(sds((8, D), f32))
        out_specs.append(full((8, D)))
    return pl.pallas_call(
        functools.partial(bwd_kernel, ks, first, bool(last), nw, blocks), out_shape=outs,
        grid_spec=pltpu.PrefetchScalarGridSpec(
            num_scalar_prefetch=1, grid=(nw,), in_specs=in_specs, out_specs=out_specs,
            scratch_shapes=[pltpu.VMEM((D, ng * QKV), f32), pltpu.VMEM((ng * 4, WIN, WIN), f32), pltpu.VMEM((8, 128), f32),
                            pltpu.VMEM((2, WIN, WIN), bf), pltpu.VMEM((3, SLAB, 256), bf), pltpu.VMEM((224 * ng, 768), f32),
                            pltpu.VMEM((224 * ng + 8, TLANES), f32), pltpu.SemaphoreType.DMA]),
        compiler_params=pltpu.CompilerParams(vmem_limit_bytes=VMEM_ALL),
        cost_estimate=pl.CostEstimate(flops=ng * nw * 4 * 10**9, bytes_accessed=ng * nw * 5 * 10**6, transcendentals=0),
    )(me, *ins)


def mlp_kernel(spec, *refs):
    places, brow, nkeep, narr, ntile, groups = spec
    refs = list(refs)
    take = lambda n: [refs.pop(0) for _ in range(n)]
    me_ref, x_ref, g_ref = take(3)
    o_refs = take(len(groups))
    small, = take(1)
    w_hbm = take(narr)
    res_out, dy_out, dyb_out, wo_out, vec_out, dbi_out = take(6)
    keeps = take(nkeep)
    send = take(1)[0] if narr > nkeep else None
    wscr, acc, vin, bi, wsem = take(5)
    t = pl.program_id(0)
    me = me_ref[0]

    @pl.when(t == 0)
    def _():
        copies = []
        for i, (arr, idx, k, blk) in enumerate(places):
            at = pl.multiple_of((me ^ blk) * brow, brow)
            copies.append(pltpu.make_async_copy(w_hbm[arr].at[idx], wscr.at[k, pl.ds(at, brow)], wsem.at[i]))
            copies[-1].start()
        for i in range(4):
            vin[i:i + 1] = small_vector(small, 4 + i)
        for k in range(4):
            for half in range(2):
                at = pl.multiple_of(((me_ref[1] ^ k) * 2 + half) * QKV, 128)
                bi[0:1, k * 512 + half * 256:k * 512 + half * 256 + 256] = small[8:9, pl.ds(at, 256)]
        acc[...] = jnp.zeros(acc.shape, f32)
        vec_out[...] = jnp.zeros(vec_out.shape, f32)
        dbi_out[...] = jnp.zeros(dbi_out.shape, f32)
        for c in copies:
            c.wait()

    y = x_ref[...].astype(f32) + vin[0:1]
    for o_ref, ks in zip(o_refs, groups):
        y = y + dd(o_ref[...], jnp.concatenate([wscr[k, :, 0:128] for k in ks], axis=1), 1, 1)
    yc = y - jnp.mean(y, axis=1, keepdims=True)
    inv = lax.rsqrt(jnp.mean(yc * yc, axis=1, keepdims=True) + norm_epsilon)
    u = yc * inv
    n2 = (u * vin[1:2] + vin[2:3]).astype(bf)
    gb = g_ref[...]
    gT = gb.astype(f32).T.astype(bf)
    n2T = n2.astype(f32).T.astype(bf)
    ff = jnp.zeros(y.shape, f32)
    dn2 = jnp.zeros(y.shape, f32)
    for k in range(4):
        wi = wscr[k, :, 128:640]
        wo = wscr[k, :, 640:1152]
        z = dd(n2, wi, 1, 0) + bi[0:1, k * 512:(k + 1) * 512]
        ez = jnp.exp2(z * z * (-0.5 * log2e))
        tt = 1.0 / (1.0 + (0.3275911 * 0.7071067811865476) * jnp.abs(z))
        poly = tt * (0.254829592 + tt * (-0.284496736 + tt * (1.421413741 + tt * (-1.453152027 + tt * 1.061405429))))
        tail = 0.5 * poly * ez
        phi = jnp.where(z >= 0, 1.0 - tail, tail)
        hb = (z * phi).astype(bf)
        slope = phi + z * (ez * 0.3989422804014327)
        ff = ff + dd(hb, wo, 1, 1)
        dz = dd(gb, wo, 1, 0) * slope
        dbi_out[k:k + 1] += jnp.sum(dz, axis=0, keepdims=True)
        dzb = dz.astype(bf)
        dn2 = dn2 + dd(dzb, wi, 1, 1)
        acc[k, :, 640:1152] += dd(gT, hb, 1, 0)
        acc[k, :, 128:640] += dd(n2T, dzb, 1, 0)
    res_out[...] = (y + ff + vin[3:4]).astype(bf)
    g = gb.astype(f32)
    a = dn2 * vin[1:2]
    dy = g + inv * (a - jnp.mean(a, axis=1, keepdims=True) - u * jnp.mean(a * u, axis=1, keepdims=True))
    dy_out[...] = dy
    dyb_out[...] = dy.astype(bf)
    dyT = dy.T.astype(bf)
    for o_ref, ks in zip(o_refs, groups):
        part = dd(dyT, o_ref[...], 1, 0)
        for i, k in enumerate(ks):
            acc[k, :, 0:128] += part[:, i * 128:(i + 1) * 128]
    vec_out[0:1] += jnp.sum(g, axis=0, keepdims=True)
    vec_out[1:2] += jnp.sum(dn2 * u, axis=0, keepdims=True)
    vec_out[2:3] += jnp.sum(dn2, axis=0, keepdims=True)
    vec_out[3:4] += jnp.sum(dy, axis=0, keepdims=True)

    @pl.when(t == ntile - 1)
    def _():
        for k in range(4):
            wo_out[:, k * 128:(k + 1) * 128] = wscr[k, :, 0:128]
        for arr, idx, k, blk in places:
            at = pl.multiple_of((me ^ blk) * brow, brow)
            block = acc[k, pl.ds(at, brow), :].astype(bf)
            if arr < nkeep:
                keeps[arr][idx] = block
            else:
                send[(arr - nkeep) * keeps[0].shape[0] + idx] = block


def mlp(me, x, g, o_list, groups, small, warrs, places, nkeep, tile):
    T = x.shape[0]
    narr = len(warrs)
    n, brow, _ = warrs[0].shape
    row = lambda c: pl.BlockSpec((tile, c), lambda i, me: (i, 0))
    ins = [x, g] + list(o_list) + [small] + list(warrs)
    in_specs = [row(D), row(D)] + [row(o.shape[1]) for o in o_list] + [full(small.shape)] + [HBM] * narr
    outs = [sds((T, D), bf), sds((T, D), f32), sds((T, D), bf), sds((D, D), bf), sds((8, D), f32), sds((8, 512), f32)]
    out_specs = [row(D), row(D), row(D), full((D, D)), full((8, D)), full((8, 512))]
    outs += [sds((n, brow, REST), bf)] * nkeep
    out_specs += [full((n, brow, REST))] * nkeep
    if narr > nkeep:
        outs.append(sds((n * (narr - nkeep), brow, REST), bf))
        out_specs.append(full((n * (narr - nkeep), brow, REST)))
    return pl.pallas_call(
        functools.partial(mlp_kernel, (places, brow, nkeep, narr, T // tile, groups)), out_shape=outs,
        grid_spec=pltpu.PrefetchScalarGridSpec(
            num_scalar_prefetch=1, grid=(T // tile,), in_specs=in_specs, out_specs=out_specs,
            scratch_shapes=[pltpu.VMEM((4, D, REST), bf), pltpu.VMEM((4, D, REST), f32), pltpu.VMEM((8, D), f32),
                            pltpu.VMEM((8, FF), f32), pltpu.SemaphoreType.DMA((len(places),))]),
        compiler_params=pltpu.CompilerParams(vmem_limit_bytes=VMEM_ALL),
        cost_estimate=pl.CostEstimate(flops=T * 19 * 10**6, bytes_accessed=30 * 10**6, transcendentals=T * FF * 2),
    )(me, *ins)


def assemble_kernel(me_ref, vec, dbi, ln, q01, q23, p01, p23, out, nat):
    out[...] = jnp.zeros(out.shape, f32)
    nat[0:2] = ln[0:2]
    nat[4:8] = vec[0:4]
    lane = lax.broadcasted_iota(jnp.int32, (1, 128), 1)
    top = jnp.full((1, 128), masked_score, f32)
    for k in range(4):
        q, p, i = (q01, p01, k) if k < 2 else (q23, p23, k - 2)
        group = me_ref[1] ^ k
        at = pl.multiple_of(group * 128, 128)
        nat[2:4, pl.ds(at, 128)] = q[2 * i:2 * i + 2]
        nat[pl.ds(8 + group, 1), :] = dbi[k:k + 1]
        for h in range(4):
            top = jnp.where(lane == group * 4 + h, p[4 * i + h:4 * i + h + 1], top)
    for i in range(12):
        out[2 * i:2 * i + 1] = nat[i:i + 1, 0:384]
        out[2 * i + 1:2 * i + 2, 0:128] = nat[i:i + 1, 384:512]
    out[24:25, 0:128] = top


def assemble(me, vec, dbi, ln, qs, ps):
    smem = pl.BlockSpec(memory_space=pltpu.SMEM)
    vmem = pl.BlockSpec(memory_space=pltpu.VMEM)
    return pl.pallas_call(
        assemble_kernel, out_shape=sds((32, QKV), f32), in_specs=[smem] + [vmem] * 7,
        scratch_shapes=[pltpu.VMEM((16, D), f32)],
        compiler_params=pltpu.CompilerParams(vmem_limit_bytes=VMEM_ALL),
    )(me, vec, dbi, ln, *qs, *ps)


def unpack_rest_kernel(rest, outw, inner, outer):
    outw[...] = rest[:, 0:128].astype(f32)
    inner[...] = rest[:, 128:640].astype(f32)
    outer[...] = rest[:, 640:1152].astype(f32)


def unpack_rest(rest):
    return pl.pallas_call(
        unpack_rest_kernel, out_shape=[sds((64, 128), f32), sds((64, 512), f32), sds((64, 512), f32)],
        compiler_params=pltpu.CompilerParams(vmem_limit_bytes=VMEM_ALL),
    )(rest)


def unpack_kernel(me_ref, buf, tri, triple, table, clipped, peaks, dbi, *vectors):
    flat = me_ref[3]
    b = buf[...].astype(f32)
    for c in range(3):
        triple[c] = b[0:64, c * 128:(c + 1) * 128]
    for h in range(4):
        for c in range(7):
            hi = min(QKV, TABLE - c * QKV)
            table[h:h + 1, c * QKV:c * QKV + hi] = b[64 + h * 7 + c:65 + h * 7 + c, 0:hi]
    rows = [jnp.concatenate([b[96 + 2 * i:97 + 2 * i], b[97 + 2 * i:98 + 2 * i, 0:128]], axis=1) for i in range(12)]
    first = jnp.concatenate(rows[0:8], axis=0)
    first = pltpu.roll(first, 512 - flat * 16, 1)
    for i in range(8):
        vectors[i][...] = first[i:i + 1, 0:16].reshape(16)
    wide = rows[8]
    for i in range(1, 4):
        wide = jnp.where(flat // 8 == i, rows[8 + i], wide)
    dbi[...] = pltpu.roll(jnp.broadcast_to(wide, (8, 512)), 512 - (flat % 8) * 64, 1)[0:1, 0:64].reshape(64)
    top = jnp.broadcast_to(b[120:121, 0:128], (8, 128))
    top = pltpu.roll(top, 128 - me_ref[1] * 4, 1)[0:1]
    peaks[...] = top[:, 0:4].reshape(4)
    root = jnp.sqrt(clip_target / jnp.maximum(top, clip_target))
    lane = lax.broadcasted_iota(jnp.int32, (1, 128), 1) // 32
    scale = jnp.zeros((1, 128), f32)
    for h in range(4):
        scale = jnp.where(lane == h, root[:, h:h + 1], scale)
    for c in range(2):
        clipped[c] = tri[c] * scale


def unpack(me, buf, triple_weight):
    smem = pl.BlockSpec(memory_space=pltpu.SMEM)
    vmem = pl.BlockSpec(memory_space=pltpu.VMEM)
    return pl.pallas_call(
        unpack_kernel,
        out_shape=[sds((3, 64, 128), f32), sds((4, TABLE), f32), sds((2, 64, 128), f32), sds((4,), f32), sds((64,), f32)] +
        [sds((16,), f32)] * 8,
        in_specs=[smem, vmem, vmem], compiler_params=pltpu.CompilerParams(vmem_limit_bytes=VMEM_ALL),
    )(me, buf, triple_weight)


def swap(x, axis, bit):
    return lax.ppermute(x, axis, [(i, i ^ bit) for i in range(lax.axis_size(axis))])


Z1, Z0, Y, X, C = ("dp", 4), ("dp", 2), ("dp", 1), ("mp", 2), ("mp", 1)
DP_BLOCKS = [(p & 1) * 4 + (p & 2) + (p >> 2) for p in range(8)]


def after(x, *deps):
    return lax.optimization_barrier((x,) + deps)[0]


def join(x, y):
    return jnp.concatenate([x, y], axis=0)


def widen(x, step):
    return join(x, swap(x, *step))


def rest_places():
    out = []
    for arr in range(8):
        c, kind = arr >> 2, arr & 3
        for i in range(4):
            z1, z0 = i & 1, kind >> 1
            x, y = (kind & 1, i >> 1) if z0 == 0 else (i >> 1, kind & 1)
            out.append((arr, i, c + 2 * x, z1 * 4 + z0 * 2 + y))
    return out


def canonical(a, parts):
    m, d, rows, width = a.shape
    own = width // parts
    a = a.reshape(4, m // 4, d, rows, parts, own).transpose(0, 2, 3, 4, 1, 5)
    return a.reshape(4, d * rows, parts * (m // 4) * own)


def uncanonical(a, parts, m, d):
    own = a.shape[2] // parts // (m // 4)
    a = a.reshape(4, d, D // d, parts, m // 4, own).transpose(0, 4, 1, 2, 3, 5)
    return a.reshape(m * d, D // d, parts * own)


def shards(tokens, regions, first_gain, first_shift, triple_weight, query_bias, value_bias, offset_table, output_weight,
           output_bias, second_gain, second_shift, inner_weight, inner_bias, outer_weight, outer_bias, cotangent):
    ndp, nmp = lax.axis_size("dp"), lax.axis_size("mp")
    me_dp, me_mp = lax.axis_index("dp"), lax.axis_index("mp")
    nw = tokens.shape[0] // WIN
    hot = jnp.asarray(place_onehot())
    smalls = [first_gain, first_shift, query_bias, value_bias, output_bias, second_gain, second_shift, outer_bias, inner_bias]
    T = tokens.shape[0]
    x3 = tokens.reshape(nw, WIN, D)
    three = lambda a: a.reshape(nw, WIN, a.shape[-1])
    flat = lambda a: a.reshape(T, a.shape[-1])
    tile = 392 if T % 392 == 0 else T
    near_ks, far_ks = (0, 1), (2, 3)
    if (ndp, nmp) == (8, 4):
        me = jnp.stack([me_dp, me_mp, me_mp * nw, me_dp * nmp + me_mp]).astype(jnp.int32)
        pk, rest, t0 = pack(triple_weight, output_weight.T, inner_weight, outer_weight.T, offset_table, *smalls)
        t1 = swap(t0, *C)
        t2 = swap(t0, *X)
        w = pk[None]
        w_z1 = swap(w, *Z1)
        t3 = swap(t2, *C)
        a = rest[None]
        a_z1 = swap(a, *Z1)
        near_bias = bias_grid([t0, t1], hot)
        w = join(w, after(w_z1, near_bias))
        a = join(a, after(a_z1, near_bias))
        b = swap(a, *Z0)
        w_z0 = swap(w, *Z0)
        far_bias = bias_grid([after(t2, w, a), t3], hot)
        w = join(w, after(w_z0, far_bias))
        w_y = swap(w, *Y)
        ay = swap(a, *Y)
        w0 = join(w, w_y)
        w1 = swap(w0, *C)
        w2 = swap(w0, *X)
        n1, small, *near = attend_fwd(near_ks, me, after(x3, b), [w0, w1], w0, near_bias, regions, DP_BLOCKS)
        bx = swap(b, *X)
        w3 = swap(after(w2, n1), *C)
        a0, b_0 = join(a, after(ay, n1)), join(b, after(bx, n1))
        a1, b_1 = swap(a0, *X), swap(b_0, *Y)
        ca0, cb0 = swap(a0, *C), swap(b_0, *C)
        far = attend_fwd(far_ks, me, after(n1, a0, b_0), [w2, w3], small, far_bias, regions, DP_BLOCKS)
        ca1, cb1 = swap(after(a1, far[0]), *C), swap(after(b_1, far[0]), *C)
        result, dy, dyb, wo, vec, dbi, k0, k1, k2, k3, sent = mlp(
            me, tokens, cotangent, [flat(near[3]), flat(far[3])], (near_ks, far_ks), small,
            [a0, a1, b_0, b_1, ca0, ca1, cb0, cb1], rest_places(), 4, tile)
        got = swap(sent, *C)
        dn, far_pair, far_vec = attend_bwd(far_ks, me, n1, far[0], far[1], far[2], far[4], three(dyb), wo, far[6], hot,
                                           None, None, DP_BLOCKS)
        got = after(got, dn)
        ga0, ga1, gb0, gb1 = [kept + got[4 * i:4 * i + 4] for i, kept in enumerate((k0, k1, k2, k3))]
        xa1, yb1 = swap(ga1, *X), swap(gb1, *Y)
        xfar = swap(far_pair, *X)
        dn, near_pair, near_vec, ln = attend_bwd(
            near_ks, me, n1, near[0], near[1], near[2], near[4], three(dyb), wo, near[6], hot,
            after(dn, ga0, ga1, gb0, gb1), (x3, three(dy), small), DP_BLOCKS)
        near_vec, near_pair, xfar, xa1, yb1 = lax.optimization_barrier((near_vec, near_pair, xfar, xa1, yb1))
        vecs = assemble(me, vec, dbi, ln, [near_vec, far_vec], [near[5], far[5]])
        core = swap(near_pair[PAIR:] + xfar[PAIR:], *C)
        peak_row = lax.broadcasted_iota(jnp.int32, (32, QKV), 0) == 24
        for step in (X, C):
            got = swap(vecs, *step)
            vecs = jnp.where(peak_row, jnp.maximum(vecs, got), vecs + got)
        buf = join(near_pair[:PAIR] + xfar[:PAIR] + core, vecs.astype(bf))
        ga0, gb0 = ga0 + xa1, gb0 + yb1
        ga, gb = ga0[:2] + swap(ga0[2:], *Y), gb0[:2] + swap(gb0[2:], *X)
        ga = ga + swap(gb, *Z0)
        rest_sum = ga[0] + swap(ga[1], *Z1)
        for step in (Y, Z0, Z1):
            half = (buf.shape[0] - 64) // 2
            got = swap(buf[half:], *step)
            own = join(buf[:half], buf[2 * half:])
            peak = lax.broadcasted_iota(jnp.int32, own.shape, 0) == half + 56
            buf = jnp.where(peak, jnp.maximum(own, got), own + got)
        outw, inner, outer = unpack_rest(rest_sum)
        triple, table, clipped, peaks, dbi, *v = unpack(me, buf, triple_weight)
        return (result, flat(dn), v[0], v[1], triple, v[2], v[3], table, outw.T, v[7], v[5], v[6], inner, dbi, outer.T, v[4],
                peaks, clipped)

    rows, own = D // ndp, D // nmp
    both = ("mp", "dp")
    shape = (nmp, ndp, rows, -1)
    me = jnp.stack([0 * me_dp, 0 * me_mp, me_mp * nw, me_dp * nmp + me_mp]).astype(jnp.int32)
    everywhere = lambda a: lax.all_gather(a.astype(bf), both).reshape(shape)
    wcanon = canonical(everywhere(triple_weight.transpose(1, 0, 2).reshape(rows, 3 * own)), 3)
    warrs = [jnp.concatenate([canonical(everywhere(a), 1) for a in (output_weight.T, inner_weight, outer_weight.T)], axis=2)]
    eight = lax.all_gather(jnp.stack(smalls[:8]).astype(bf), "dp", axis=1, tiled=True).reshape(8, 8, 64).transpose(1, 0, 2)
    eight = jnp.pad(eight, ((0, 0), (0, 0), (0, QKV - 64)))
    ninth = lax.all_gather(inner_bias.astype(bf), "dp", tiled=True).reshape(8, 1, 256)
    ninth = jnp.pad(ninth, ((0, 0), (0, 7), (0, QKV - 256)))
    small_src = jnp.concatenate([eight, ninth], axis=1)
    tables = lax.all_gather(offset_table.astype(bf), "mp", tiled=True)
    tables = jnp.pad(tables, ((0, 0), (0, TLANES - TABLE))).reshape(4, 16, 640)
    bias = [bias_grid([tables[k], tables[k + 1]], hot) for k in (0, 2)]
    blocks = [0]
    wk = [wcanon[k:k + 1] for k in range(4)]
    n1, small, *near = attend_fwd(near_ks, me, x3, wk[:2], small_src, bias[0], regions, blocks)
    far = attend_fwd(far_ks, me, n1, wk[2:], small, bias[1], regions, blocks)
    result, dy, dyb, wo, vec, dbi, rg = mlp(
        me, tokens, cotangent, [flat(near[3]), flat(far[3])], (near_ks, far_ks), small, warrs,
        [(0, k, k, 0) for k in range(4)], 1, tile)
    dn, far_pair, far_vec = attend_bwd(far_ks, me, n1, far[0], far[1], far[2], far[4], three(dyb), wo, far[6], hot,
                                       None, None, blocks)
    dx, near_pair, near_vec, ln = attend_bwd(
        near_ks, me, n1, near[0], near[1], near[2], near[4], three(dyb), wo, near[6], hot, dn, (x3, three(dy), small), blocks)
    vecs = assemble(me, vec, dbi, ln, [near_vec, far_vec], [near[5], far[5]])
    pairs = jnp.concatenate([near_pair, far_pair]).reshape(4, PAIR, QKV)
    dx = flat(dx)
    reduce = lambda a, parts: lax.psum_scatter(uncanonical(a, parts, nmp, ndp), both, tiled=True)[0].astype(f32)
    triple = reduce(pairs[:, :D], 3).reshape(rows, 3, own).transpose(1, 0, 2)
    outw = reduce(rg[:, :, 0:128], 1).T
    inner = reduce(rg[:, :, 128:640], 1)
    outer = reduce(rg[:, :, 640:1152], 1).T
    here = HEADS // nmp
    table = lax.psum(pairs[:, D:D + 28].astype(f32).reshape(HEADS, 7 * QKV)[:, :TABLE], both)
    table = lax.dynamic_slice_in_dim(table, me_mp * here, here)
    peaks = lax.dynamic_slice_in_dim(lax.pmax(vecs[24, :HEADS], both), me_mp * here, here)
    sums = lax.psum(vecs[:24].reshape(12, 2 * QKV)[:, :D], both)

    def piece(vector):
        width = vector.shape[0] // (ndp * nmp)
        return lax.dynamic_slice_in_dim(vector, (me_dp * nmp + me_mp) * width, width)

    factor = clip_target / jnp.maximum(peaks, clip_target)
    clipped = triple_weight[:2] * jnp.repeat(jnp.sqrt(factor), HEAD_DIM)[None, None, :]
    v = [piece(sums[i]) for i in range(8)]
    dbi = piece(sums[8:12].reshape(FF))
    return (result, dx, v[0], v[1], triple, v[2], v[3], table, outw, v[7], v[5], v[6], inner, dbi, outer, v[4], peaks, clipped)


def solution(mesh):
    rows = P(("dp", "mp"), None)
    vector = P("dp")
    every = P(("dp", "mp"))
    three = P(None, "dp", "mp")
    down, across = P("mp", "dp"), P("dp", "mp")
    return jax.shard_map(
        shards,
        mesh=mesh,
        in_specs=(rows, P("dp", None), vector, vector, three, vector, vector, P("mp", None), down, vector, vector, vector,
                  across, vector, down, vector, rows),
        out_specs=(rows, rows, every, every, three, every, every, P("mp", None), down, every, every, every, across, every,
                   down, every, P("mp"), three),
        check_vma=False,
    )
```

```python
import functools
import math

import jax
import jax.numpy as jnp
import numpy as np
from jax import lax
from jax.experimental import pallas as pl
from jax.experimental.pallas import tpu as pltpu
from jax.sharding import PartitionSpec as P

D = 512
HEADS = 16
HEAD_DIM = 32
FF = 2048
WIN = 392
PLACES = 49
TIMES = 8
SPACE = 169
TABLE = 2535
TLANES = 2560
GROUP = 128
QKV = 384
REST = 1152
SMALL = 16
SLANES = 8 * QKV
norm_epsilon = 1e-05
masked_score = -1e9
clip_target = 10.0
log2e = math.log2(math.e)
score_scale = 1.0 / math.sqrt(HEAD_DIM)
bf = jnp.bfloat16
f32 = jnp.float32
ROWS = [(s, min(64, WIN - s)) for s in range(0, WIN, 64)]
PAIR = D + 32
density_scale = 0.3989422804014327
ERFC = [c * 0.5 / density_scale for c in (0.254829592, -0.284496736, 1.421413741, -1.453152027, 1.061405429)]
VMEM_ALL = 63 * 2**20
sds = jax.ShapeDtypeStruct


def dd(a, b, ca, cb):
    return lax.dot_general(a, b, (((ca,), (cb,)), ((), ())), preferred_element_type=f32)


def fold_max(acc, x):
    for r in range(0, x.shape[0], 8):
        acc = jnp.maximum(acc, x[r:r + 8])
    return acc


def full(shape):
    return pl.BlockSpec(shape, lambda w, me: (0,) * len(shape), pipeline_mode=pl.Buffered(1))


def win(shape):
    return pl.BlockSpec((1,) + shape, lambda w, me: (w,) + (0,) * len(shape))


HBM = pl.BlockSpec(memory_space=pl.ANY)


def small_vector(small, row):
    return jnp.concatenate([small[row:row + 1, d * QKV:d * QKV + 64] for d in range(8)], axis=1)


def group_vector(small, row, group):
    parts = []
    for half in range(2):
        at = pl.multiple_of((group * 2 + half) * QKV, 128)
        parts.append(small[row:row + 1, pl.ds(at, 128)][:, :64])
    return jnp.concatenate(parts, axis=1)


def pack_kernel(tri, outw, inner, outer, table, *refs):
    smalls, (pk, rest, tab) = refs[:9], refs[9:]
    for c in range(3):
        pk[0:64, c * 128:(c + 1) * 128] = tri[c].astype(bf)
    rows = [jnp.pad(s[...].reshape(1, -1), ((0, 0), (0, QKV - s.shape[0]))) for s in smalls]
    pk[64:80, :] = jnp.concatenate(rows + [jnp.zeros((7, QKV), f32)], axis=0).astype(bf)
    rest[:, 0:128] = outw[...].astype(bf)
    rest[:, 128:640] = inner[...].astype(bf)
    rest[:, 640:1152] = outer[...].astype(bf)
    t = jnp.pad(table[...], ((0, 0), (0, TLANES - TABLE)))
    tab[...] = jnp.concatenate([t[h:h + 1, c * 640:(c + 1) * 640] for h in range(4) for c in range(4)], axis=0).astype(bf)


def pack(*params):
    return pl.pallas_call(
        pack_kernel,
        out_shape=[sds((80, QKV), bf), sds((64, REST), bf), sds((16, 640), bf)],
        compiler_params=pltpu.CompilerParams(vmem_limit_bytes=VMEM_ALL),
    )(*params)


SLABS = (0, 768, 1408)
SLAB = 1152


def place_onehot():
    at = np.arange(PLACES)
    code = (at // 7) * 13 + at % 7
    hot = np.zeros((TLANES, 768), np.float32)
    for a in range(15):
        hot[a * SPACE + code, a * PLACES + at] = 1.0
    return np.stack([hot[r:r + SLAB, j * 256:(j + 1) * 256] for j, r in enumerate(SLABS)]).astype(bf)


def grid_kernel(t0, t1, hot_hbm, out_hbm, hot, rolled, spread, out, hsem, osem):
    hot_copy = pltpu.make_async_copy(hot_hbm, hot, hsem)
    hot_copy.start()
    for h in range(8):
        t = t0 if h < 4 else t1
        flat = jnp.concatenate([t[4 * (h % 4) + c:4 * (h % 4) + c + 1] for c in range(4)], axis=1).astype(f32)
        steps = pltpu.roll(jnp.broadcast_to(flat, (8, TLANES)), 0, 1, stride=1, stride_axis=0)
        for y in range(7):
            rolled[h * 56 + y * 7:h * 56 + y * 7 + 8, :] = pltpu.roll(steps, TLANES - (84 - 13 * y), 1)
    hot_copy.wait()
    copies = []
    for j, r in enumerate(SLABS):
        spread[:, j * 256:(j + 1) * 256] = dd(rolled[0:448, r:r + SLAB].astype(bf), hot[j], 1, 0) * log2e
    for h in range(8):
        for t in range(TIMES):
            lo = (7 - t) * PLACES
            out[h, t * PLACES:(t + 1) * PLACES, :] = spread[h * 56:h * 56 + PLACES, lo:lo + WIN]
        copies.append(pltpu.make_async_copy(out.at[h], out_hbm.at[h], osem.at[h]))
        copies[-1].start()
    for c in copies:
        c.wait()


def bias_grid(tables, hot):
    vmem = pl.BlockSpec(memory_space=pltpu.VMEM)
    return pl.pallas_call(
        grid_kernel, out_shape=sds((8, WIN, WIN), f32),
        in_specs=[vmem, vmem, HBM], out_specs=HBM,
        scratch_shapes=[pltpu.VMEM((3, SLAB, 256), bf), pltpu.VMEM((456, TLANES), f32), pltpu.VMEM((448, 768), f32),
                        pltpu.VMEM((8, WIN, WIN), f32), pltpu.SemaphoreType.DMA, pltpu.SemaphoreType.DMA((8,))],
        compiler_params=pltpu.CompilerParams(vmem_limit_bytes=VMEM_ALL),
        cost_estimate=pl.CostEstimate(flops=5 * 10**9, bytes_accessed=9 * 10**6, transcendentals=0),
    )(*tables, hot)


def fwd_kernel(first, ks, nwin, blocks, *refs):
    ng = len(ks)
    refs = list(refs)
    take = lambda n: [refs.pop(0) for _ in range(n)]
    me_ref, x_ref = take(2)
    w_hbm = take(ng)
    s_in, = take(1)
    bias_hbm, = take(1)
    reg_ref, = take(1)
    if first:
        n1_out, s_out = take(2)
    qkv_out, e_out, ot_out, o_out, linv_out, hm_out, w_out = take(7)
    bias, mask, s_scr, hm_scr, wsem, bsem = take(6)
    if first:
        s_bf, ssem = take(2)
    w = pl.program_id(0)
    rows = D // len(blocks)
    bias_copies = [pltpu.make_async_copy(bias_hbm.at[pl.ds(4 * g, 4)], bias.at[pl.ds(4 * g, 4)], bsem.at[g]) for g in range(ng)]

    @pl.when(w == 0)
    def _():
        copies = []
        if first:
            at_row = s_in.shape[1] - SMALL
            order = blocks if len(blocks) == 8 else list(range(8))
            for p, blk in enumerate(order):
                at = pl.multiple_of((me_ref[0] ^ blk) * QKV, 128)
                copies.append(pltpu.make_async_copy(
                    s_in.at[p, at_row:at_row + SMALL], s_bf.at[:, pl.ds(at, QKV)], ssem.at[p]))
        for g in range(ng):
            for p, blk in enumerate(blocks):
                at = pl.multiple_of((me_ref[0] ^ blk) * rows, rows)
                copies.append(pltpu.make_async_copy(
                    w_hbm[g].at[p, 0:rows], w_out.at[pl.ds(at, rows), g * QKV:(g + 1) * QKV], wsem.at[g * len(blocks) + p]))
        for c in copies + bias_copies:
            c.start()
        for c in copies:
            c.wait()
        if first:
            s_out[...] = s_bf[...].astype(f32)
        hm_scr[...] = jnp.full(hm_scr.shape, -jnp.inf, f32)

    small = s_out if first else s_in
    region = reg_ref[pl.ds(me_ref[2] + w, 1), :].astype(f32)
    column = jnp.broadcast_to(region, (8, WIN)).T[:, 0:1]
    mask[...] = jnp.where(column == region, 0.0, masked_score)
    if first:
        x = x_ref[0].astype(f32)
        xc = x - jnp.mean(x, axis=1, keepdims=True)
        inv = lax.rsqrt(jnp.mean(xc * xc, axis=1, keepdims=True) + norm_epsilon)
        n1 = (xc * inv * small_vector(small, 0) + small_vector(small, 1)).astype(bf)
        n1_out[0] = n1
    else:
        n1 = x_ref[0]
    pall = dd(n1, w_out[...], 1, 0)
    ones = jnp.ones((16, WIN), bf)

    @pl.when(w == 0)
    def _():
        for c in bias_copies:
            c.wait()

    kbs, qTs, vTs = [], [], []
    for g in range(ng):
        group = me_ref[1] ^ ks[g]
        p = pall[:, g * QKV:(g + 1) * QKV]
        q = (p[:, :128] + group_vector(small, 2, group)) * (score_scale * log2e)
        kb = p[:, 128:256].astype(bf)
        v = p[:, 256:] + group_vector(small, 3, group)
        qkv_out[0, :, g * QKV:g * QKV + 128] = q.astype(bf)
        qkv_out[0, :, g * QKV + 128:g * QKV + 256] = kb
        qkv_out[0, :, g * QKV + 256:g * QKV + 384] = v.astype(bf)
        kbs.append(kb)
        qTs.append(q.T.astype(bf))
        vTs.append(v.T.astype(bf))

    nh = 4 * ng
    outs, linvs = [], []

    def scores(h):
        sl = slice(h % 4 * 32, h % 4 * 32 + 32)
        return dd(kbs[h // 4][:, sl], qTs[h // 4][sl], 1, 0)

    def mix(h):
        sl = slice(h % 4 * 32, h % 4 * 32 + 32)
        ol = dd(jnp.concatenate([vTs[h // 4][sl], ones], axis=0), e_out[0, h], 1, 0)
        linv = 1.0 / ol[32:33]
        linvs.append(linv)
        outs.append(ol[:32] * linv)
        if h % 4 == 3:
            g = h // 4
            oT = jnp.concatenate(outs[-4:], axis=0)
            ot_out[0, g * 128:(g + 1) * 128] = oT.astype(bf)
            o_out[0, :, g * 128:(g + 1) * 128] = oT.T.astype(bf)

    s = scores(0)
    for h in range(nh):
        after_s = scores(h + 1) if h + 1 < nh else None
        hm = jnp.full((8, WIN), -jnp.inf, f32)
        m = jnp.full((8, WIN), -jnp.inf, f32)
        for r, n in ROWS:
            c = s[r:r + n]
            hm = fold_max(hm, c)
            c = c + bias[h, r:r + n] + mask[r:r + n]
            m = fold_max(m, c)
            s_scr[h % 2, r:r + n] = c
        hm_scr[h] = jnp.maximum(hm_scr[h], hm)
        m = jnp.max(m, axis=0, keepdims=True)
        if h > 0:
            mix(h - 1)
        for r, n in ROWS:
            e_out[0, h, r:r + n] = jnp.exp2(s_scr[h % 2, r:r + n] - m).astype(bf)
        s = after_s
    mix(nh - 1)
    if ng == 1:
        linvs.append(jnp.zeros((4, WIN), f32))
    linv_out[0] = jnp.concatenate(linvs, axis=0)

    @pl.when(w == nwin - 1)
    def _():
        tops = [jnp.broadcast_to(jnp.max(hm_scr[h], keepdims=True), (1, 128)) for h in range(4 * ng)]
        if ng == 1:
            tops.append(jnp.zeros((4, 128), f32))
        hm_out[...] = jnp.concatenate(tops, axis=0) * (1.0 / log2e)


def attend_fwd(ks, me, x, wblk, small, bias, regions, blocks):
    first = ks[0] == 0
    ng = len(ks)
    nw = x.shape[0]
    ins = [x, *wblk, small, bias, regions]
    in_specs = [win((WIN, D))] + [HBM] * ng + [HBM if first else full(small.shape), HBM, full(regions.shape)]
    outs = ([sds((nw, WIN, D), bf), sds((SMALL, SLANES), f32)] if first else []) + [
        sds((nw, WIN, ng * QKV), bf), sds((nw, ng * 4, WIN, WIN), bf), sds((nw, ng * GROUP, WIN), bf),
        sds((nw, WIN, ng * GROUP), bf), sds((nw, 8, WIN), f32), sds((8, 128), f32), sds((D, ng * QKV), bf)]
    out_specs = ([win((WIN, D)), full((SMALL, SLANES))] if first else []) + [
        win((WIN, ng * QKV)), win((ng * 4, WIN, WIN)), win((ng * GROUP, WIN)), win((WIN, ng * GROUP)), win((8, WIN)),
        full((8, 128)), full((D, ng * QKV))]
    scratch = [pltpu.VMEM((ng * 4, WIN, WIN), f32), pltpu.VMEM((WIN, WIN), f32), pltpu.VMEM((2, WIN, WIN), f32),
               pltpu.VMEM((ng * 4, 8, WIN), f32), pltpu.SemaphoreType.DMA((ng * len(blocks),)), pltpu.SemaphoreType.DMA((ng,))]
    if first:
        scratch += [pltpu.VMEM((SMALL, SLANES), bf), pltpu.SemaphoreType.DMA((8,))]
    return pl.pallas_call(
        functools.partial(fwd_kernel, first, ks, nw, blocks), out_shape=outs,
        grid_spec=pltpu.PrefetchScalarGridSpec(
            num_scalar_prefetch=1, grid=(nw,), in_specs=in_specs, out_specs=out_specs, scratch_shapes=scratch),
        compiler_params=pltpu.CompilerParams(vmem_limit_bytes=VMEM_ALL),
        cost_estimate=pl.CostEstimate(flops=ng * nw * 3 * 10**9, bytes_accessed=nw * ng * 4 * 10**6,
                                      transcendentals=ng * nw * 4 * WIN * WIN),
    )(me, *ins)


def bwd_kernel(ks, first, last, nwin, blocks, *refs):
    ng = len(ks)
    refs = list(refs)
    take = lambda n: [refs.pop(0) for _ in range(n)]
    me_ref, n1_ref, qkv_ref, e_ref, ot_ref, linv_ref, dyb_ref, wo_ref, w_ref, hot_hbm = take(10)
    prev_ref = None if first else take(1)[0]
    if last:
        x_ref, dy_ref, small_ref = take(3)
    dn_out, dw_out, vec_out = take(3)
    if last:
        ln_out, = take(1)
    dwacc, dls, p_scr, dl_scr, hot, spread, rolled, hsem = take(8)
    w = pl.program_id(0)
    hot_copy = pltpu.make_async_copy(hot_hbm, hot, hsem)

    @pl.when(w == 0)
    def _():
        hot_copy.start()
        dwacc[...] = jnp.zeros(dwacc.shape, f32)
        dls[...] = jnp.zeros(dls.shape, f32)
        vec_out[...] = jnp.zeros(vec_out.shape, f32)
        if last:
            ln_out[...] = jnp.zeros(ln_out.shape, f32)

    do_all = dd(dyb_ref[0], wo_ref[:, ks[0] * 128:(ks[0] + ng) * 128], 1, 0)
    lane = lax.broadcasted_iota(jnp.int32, (1, 128), 1) // 32
    nh = 4 * ng
    qs, vs, kTs, doTs, dos, rs = [], [], [], [], [], []
    for g in range(ng):
        qs.append(qkv_ref[0, :, g * QKV:g * QKV + 128])
        k = qkv_ref[0, :, g * QKV + 128:g * QKV + 256]
        vs.append(qkv_ref[0, :, g * QKV + 256:g * QKV + 384])
        doT = do_all[:, g * 128:(g + 1) * 128].T
        oT = ot_ref[0, g * 128:(g + 1) * 128].astype(f32)
        scaled = []
        for h in range(4):
            sl = slice(h * 32, h * 32 + 32)
            s = (doT[sl] * linv_ref[0, 4 * g + h:4 * g + h + 1]).astype(bf)
            scaled.append(s)
            rs.append(jnp.sum(s.astype(f32) * oT[sl], axis=0, keepdims=True))
        doTs.append(jnp.concatenate(scaled, axis=0))
        dos.append(doTs[g].astype(f32).T.astype(bf))
        kTs.append(k.astype(f32).T.astype(bf))
    none = jnp.zeros((), bf)
    dks = [jnp.zeros((WIN, 128), f32)] * ng
    dvs = [jnp.zeros((WIN, 128), f32)] * ng
    dqT = []

    def slopes(h):
        sl = slice(h % 4 * 32, h % 4 * 32 + 32)
        return dd(vs[h // 4][:, sl], doTs[h // 4][sl], 1, 0)

    def products(h):
        g = h // 4
        own = lane == h % 4
        dqT.append(dd(kTs[g][h % 4 * 32:h % 4 * 32 + 32], dl_scr[h % 2], 1, 0))
        yield
        dks[g] = dks[g] + dd(dl_scr[h % 2], jnp.where(own, qs[g], none), 1, 0)
        yield
        dvs[g] = dvs[g] + dd(e_ref[0, h], jnp.where(own, dos[g], none), 1, 0)
        yield

    p = slopes(0)
    for h in range(nh):
        nextp = slopes(h + 1) if h + 1 < nh else None
        heavy = products(h - 1) if h > 0 else iter(())
        for i, (r, n) in enumerate(ROWS):
            if i % 3 == 0:
                next(heavy, None)
            dl = e_ref[0, h, r:r + n].astype(f32) * (p[r:r + n] - rs[h])
            dls[h, r:r + n] += dl
            dl_scr[h % 2, r:r + n] = dl.astype(bf)
        for _ in heavy:
            pass
        p = nextp
    for _ in products(nh - 1):
        pass
    parts = []
    for g in range(ng):
        dq = jnp.concatenate(dqT[4 * g:4 * g + 4], axis=0).T * score_scale
        vec_out[2 * g:2 * g + 1] += jnp.sum(dq, axis=0, keepdims=True)
        vec_out[2 * g + 1:2 * g + 2] += jnp.sum(dvs[g], axis=0, keepdims=True)
        parts += [dq.astype(bf), (dks[g] * (1.0 / log2e)).astype(bf), dvs[g].astype(bf)]
    dqkv = jnp.concatenate(parts, axis=1)
    dwacc[...] += dd(n1_ref[0], dqkv, 0, 0)
    dn1 = dd(dqkv, w_ref[...], 1, 1)
    if not first:
        dn1 = dn1 + prev_ref[0]
    if last:
        x = x_ref[0].astype(f32)
        xc = x - jnp.mean(x, axis=1, keepdims=True)
        inv = lax.rsqrt(jnp.mean(xc * xc, axis=1, keepdims=True) + norm_epsilon)
        u = xc * inv
        ln_out[0:1] += jnp.sum(dn1 * u, axis=0, keepdims=True)
        ln_out[1:2] += jnp.sum(dn1, axis=0, keepdims=True)
        a = dn1 * small_vector(small_ref, 0)
        gr = inv * (a - jnp.mean(a, axis=1, keepdims=True) - u * jnp.mean(a * u, axis=1, keepdims=True))
        dn_out[0] = (dy_ref[0] + gr).astype(bf)
    else:
        dn_out[0] = dn1

    @pl.when(w == nwin - 1)
    def _():
        rows = D // len(blocks)
        spread[...] = jnp.zeros(spread.shape, f32)
        for h in range(4 * ng):
            for t in range(TIMES):
                lo = (7 - t) * PLACES
                spread[h * 56:h * 56 + PLACES, lo:lo + WIN] += dls[h, t * PLACES:(t + 1) * PLACES, :]
        for g in range(ng):
            for kk, blk in enumerate(blocks):
                at = pl.multiple_of((me_ref[0] ^ blk) * rows, rows)
                dw_out[g * PAIR + kk * rows:g * PAIR + (kk + 1) * rows] = dwacc[pl.ds(at, rows), g * QKV:(g + 1) * QKV].astype(bf)
        hot_copy.wait()
        rolled[...] = jnp.zeros(rolled.shape, f32)
        for j, r in enumerate(SLABS):
            rolled[0:224 * ng, r:r + SLAB] += dd(spread[:, j * 256:(j + 1) * 256].astype(bf), hot[j], 1, 1)
        row = lax.broadcasted_iota(jnp.int32, (8, 1), 0)
        for g in range(ng):
            lines = []
            for h in range(4 * g, 4 * g + 4):
                acc = jnp.zeros((8, TLANES), f32)
                for y in range(7):
                    part = rolled[h * 56 + y * 7:h * 56 + y * 7 + 8, :]
                    acc += pltpu.roll(jnp.where(row < 7, part, 0.0), 84 - 13 * y, 1)
                for bit in (1, 2, 4):
                    acc = jnp.where((row & bit) != 0, pltpu.roll(acc, TLANES - bit, 1), acc)
                flat = jnp.sum(acc, axis=0, keepdims=True)
                flat = jnp.concatenate([flat, jnp.zeros((1, 7 * QKV - TLANES), f32)], axis=1)
                lines += [flat[:, c * QKV:(c + 1) * QKV] for c in range(7)]
            lines.append(jnp.zeros((4, QKV), f32))
            dw_out[g * PAIR + D:(g + 1) * PAIR] = jnp.concatenate(lines, axis=0).astype(bf)


def attend_bwd(ks, me, n1, qkv, e, oT, linv, dyb, wo, w, hot, prev, last, blocks):
    ng = len(ks)
    nw = n1.shape[0]
    first = prev is None
    ins = [n1, qkv, e, oT, linv, dyb, wo, w, hot] + ([] if first else [prev]) + (list(last) if last else [])
    in_specs = ([win((WIN, D)), win((WIN, ng * QKV)), win((ng * 4, WIN, WIN)), win((ng * GROUP, WIN)), win((8, WIN)),
                 win((WIN, D)), full((D, D)), full((D, ng * QKV)), HBM] + ([] if first else [win((WIN, D))]) +
                ([win((WIN, D)), win((WIN, D)), full(last[2].shape)] if last else []))
    outs = [sds((nw, WIN, D), bf if last else f32), sds((ng * PAIR, QKV), bf), sds((8, 128), f32)]
    out_specs = [win((WIN, D)), full((ng * PAIR, QKV)), full((8, 128))]
    if last:
        outs.append(sds((8, D), f32))
        out_specs.append(full((8, D)))
    return pl.pallas_call(
        functools.partial(bwd_kernel, ks, first, bool(last), nw, blocks), out_shape=outs,
        grid_spec=pltpu.PrefetchScalarGridSpec(
            num_scalar_prefetch=1, grid=(nw,), in_specs=in_specs, out_specs=out_specs,
            scratch_shapes=[pltpu.VMEM((D, ng * QKV), f32), pltpu.VMEM((ng * 4, WIN, WIN), f32), pltpu.VMEM((8, 128), f32),
                            pltpu.VMEM((2, WIN, WIN), bf), pltpu.VMEM((3, SLAB, 256), bf), pltpu.VMEM((224 * ng, 768), f32),
                            pltpu.VMEM((224 * ng + 8, TLANES), f32), pltpu.SemaphoreType.DMA]),
        compiler_params=pltpu.CompilerParams(vmem_limit_bytes=VMEM_ALL),
        cost_estimate=pl.CostEstimate(flops=ng * nw * 4 * 10**9, bytes_accessed=ng * nw * 5 * 10**6, transcendentals=0),
    )(me, *ins)


def chunks(n, size):
    return [(r, min(size, n - r)) for r in range(0, n, size)]


def mlp_kernel(spec, *refs):
    places, brow, nkeep, narr, ntile, groups = spec
    refs = list(refs)
    take = lambda n: [refs.pop(0) for _ in range(n)]
    me_ref, x_ref, g_ref = take(3)
    o_refs = take(len(groups))
    small, = take(1)
    w_hbm = take(narr)
    res_out, dy_out, dyb_out, wo_out, vec_out, dbi_out = take(6)
    keeps = take(nkeep)
    send = take(1)[0] if narr > nkeep else None
    wscr, acc, stage, vin, bi, y_scr, u_scr, inv_scr, n2_scr, ff_scr, dn_scr, z_scr, dh_scr, hb_scr, dz_scr, wsem, osem = take(17)
    t = pl.program_id(0)
    me = me_ref[0]
    tile = x_ref.shape[0]
    bits = ((0, 128), (128, REST))

    def rows_of(blk):
        return pl.ds(pl.multiple_of((me ^ blk) * brow, brow), brow)

    def fetch(part, i):
        arr, idx, k, blk = places[i]
        lo, hi = bits[part]
        return pltpu.make_async_copy(
            w_hbm[arr].at[idx, :, lo:hi], wscr.at[k, rows_of(blk), lo:hi], wsem.at[part * len(places) + i])

    def leave(part, i):
        arr, idx, k, blk = places[i]
        lo, hi = bits[part]
        dst = keeps[arr].at[idx] if arr < nkeep else send.at[(arr - nkeep) * keeps[0].shape[0] + idx]
        return pltpu.make_async_copy(stage.at[k, rows_of(blk), lo:hi], dst.at[:, lo:hi], osem.at[part * len(places) + i])

    of = lambda k: [i for i, p in enumerate(places) if p[2] == k]

    @pl.when(t == 0)
    def _():
        for i in range(len(places)):
            fetch(0, i).start()
        for k in range(4):
            for i in of(k):
                fetch(1, i).start()
        for i in range(4):
            vin[i:i + 1] = small_vector(small, 4 + i)
        for k in range(4):
            for half in range(2):
                at = pl.multiple_of(((me_ref[1] ^ k) * 2 + half) * QKV, 128)
                bi[0:1, k * 512 + half * 256:k * 512 + half * 256 + 256] = small[8:9, pl.ds(at, 256)]
        acc[...] = jnp.zeros(acc.shape, f32)
        vec_out[...] = jnp.zeros(vec_out.shape, f32)
        dbi_out[...] = jnp.zeros(dbi_out.shape, f32)
        for i in range(len(places)):
            fetch(0, i).wait()
            fetch(1, i).wait()

    total = None
    for o_ref, ks in zip(o_refs, groups):
        part = dd(o_ref[...], jnp.concatenate([wscr[k, :, 0:128] for k in ks], axis=1), 1, 1)
        total = part if total is None else total + part
    y_scr[...] = total
    for r, n in chunks(tile, 32):
        y = x_ref[r:r + n].astype(f32) + y_scr[r:r + n] + vin[0:1]
        y_scr[r:r + n] = y
        yc = y - jnp.mean(y, axis=1, keepdims=True)
        inv = lax.rsqrt(jnp.mean(yc * yc, axis=1, keepdims=True) + norm_epsilon)
        u = yc * inv
        u_scr[r:r + n] = u
        inv_scr[r:r + n] = jnp.broadcast_to(inv, (n, 128))
        n2_scr[r:r + n] = (u * vin[1:2] + vin[2:3]).astype(bf)
    n2 = n2_scr[...]
    gb = g_ref[...]
    gT = gb.astype(f32).T.astype(bf)
    n2T = n2.astype(f32).T.astype(bf)
    def inner(k):
        z_scr[k % 2] = dd(n2, wscr[k, :, 128:640], 1, 0)
        dh_scr[k % 2] = dd(gb, wscr[k, :, 640:1152], 1, 0)

    def gelu(k):
        bias = bi[0:1, k * 512:(k + 1) * 512]
        total = jnp.zeros((8, 512), f32)
        for r, n in chunks(tile, 16):
            z = z_scr[k % 2, r:r + n] + bias
            pdf = jnp.exp2(z * z * (-0.5 * log2e) + math.log2(density_scale))
            tt = 1.0 / (1.0 + (0.3275911 * 0.7071067811865476) * jnp.abs(z))
            c1, c2, c3, c4, c5 = ERFC
            tail = tt * (c1 + tt * (c2 + tt * (c3 + tt * (c4 + tt * c5)))) * pdf
            phi = jnp.where(z >= 0, 1.0 - tail, tail)
            hb_scr[k % 2, r:r + n] = (z * phi).astype(bf)
            dz = dh_scr[k % 2, r:r + n] * (phi + z * pdf)
            for i in range(0, n, 8):
                total = total + dz[i:i + 8]
            dz_scr[k % 2, r:r + n] = dz.astype(bf)
            yield
        dbi_out[k:k + 1] += jnp.sum(total, axis=0, keepdims=True)

    def outer(k):
        hb = hb_scr[k % 2]
        dzb = dz_scr[k % 2]
        for c in range(2):
            lo, hi = c * 256, (c + 1) * 256
            part = dd(hb, wscr[k, lo:hi, 640:1152], 1, 1)
            ff_scr[:, lo:hi] = part if k == 0 else ff_scr[:, lo:hi] + part
            yield
            part = dd(dzb, wscr[k, lo:hi, 128:640], 1, 1)
            dn_scr[:, lo:hi] = part if k == 0 else dn_scr[:, lo:hi] + part
            yield
            acc[k, :, 640 + lo:640 + hi] += dd(gT, hb[:, lo:hi], 1, 0)
            yield
            acc[k, :, 128 + lo:128 + hi] += dd(n2T, dzb[:, lo:hi], 1, 0)
            yield

    inner(0)
    for _ in gelu(0):
        pass
    for k in range(4):
        if k < 3:
            inner(k + 1)
            light = gelu(k + 1)
        per = -(-len(chunks(tile, 16)) // 8)
        for _ in outer(k):
            if k < 3:
                for _ in range(per):
                    next(light, None)
        if k < 3:
            for _ in light:
                pass

    sums = [jnp.zeros((8, D), f32) for _ in range(4)]
    for r, n in chunks(tile, 32):
        res_out[r:r + n] = (y_scr[r:r + n] + ff_scr[r:r + n] + vin[3:4]).astype(bf)
        g = g_ref[r:r + n].astype(f32)
        u = u_scr[r:r + n]
        dn2 = dn_scr[r:r + n]
        a = dn2 * vin[1:2]
        dy = g + inv_scr[r:r + n, 0:1] * (
            a - jnp.mean(a, axis=1, keepdims=True) - u * jnp.mean(a * u, axis=1, keepdims=True))
        dy_out[r:r + n] = dy
        dyb_out[r:r + n] = dy.astype(bf)
        for j, term in enumerate((g, dn2 * u, dn2, dy)):
            for i in range(0, n, 8):
                sums[j] = sums[j] + term[i:i + 8]
    for j in range(4):
        vec_out[j:j + 1] += jnp.sum(sums[j], axis=0, keepdims=True)
    dyT = dyb_out[...].astype(f32).T.astype(bf)
    for o_ref, ks in zip(o_refs, groups):
        part = dd(dyT, o_ref[...], 1, 0)
        for i, k in enumerate(ks):
            acc[k, :, 0:128] += part[:, i * 128:(i + 1) * 128]

    @pl.when(t == ntile - 1)
    def _():
        for k in range(4):
            stage[k] = acc[k].astype(bf)
            for i in of(k):
                leave(0, i).start()
                leave(1, i).start()
        for k in range(4):
            wo_out[:, k * 128:(k + 1) * 128] = wscr[k, :, 0:128]
        for part in (1, 0):
            for i in range(len(places)):
                leave(part, i).wait()


def mlp(me, x, g, o_list, groups, small, warrs, places, nkeep, tile):
    T = x.shape[0]
    narr = len(warrs)
    n, brow, _ = warrs[0].shape
    row = lambda c: pl.BlockSpec((tile, c), lambda i, me: (i, 0))
    ins = [x, g] + list(o_list) + [small] + list(warrs)
    in_specs = [row(D), row(D)] + [row(o.shape[1]) for o in o_list] + [full(small.shape)] + [HBM] * narr
    outs = [sds((T, D), bf), sds((T, D), f32), sds((T, D), bf), sds((D, D), bf), sds((8, D), f32), sds((8, 512), f32)]
    out_specs = [row(D), row(D), row(D), full((D, D)), full((8, D)), full((8, 512))]
    outs += [sds((n, brow, REST), bf)] * nkeep
    out_specs += [HBM] * nkeep
    if narr > nkeep:
        outs.append(sds((n * (narr - nkeep), brow, REST), bf))
        out_specs.append(HBM)
    return pl.pallas_call(
        functools.partial(mlp_kernel, (places, brow, nkeep, narr, T // tile, groups)), out_shape=outs,
        grid_spec=pltpu.PrefetchScalarGridSpec(
            num_scalar_prefetch=1, grid=(T // tile,), in_specs=in_specs, out_specs=out_specs,
            scratch_shapes=[pltpu.VMEM((4, D, REST), bf), pltpu.VMEM((4, D, REST), f32), pltpu.VMEM((4, D, REST), bf),
                            pltpu.VMEM((8, D), f32), pltpu.VMEM((8, FF), f32), pltpu.VMEM((tile, D), f32),
                            pltpu.VMEM((tile, D), f32), pltpu.VMEM((tile, 128), f32), pltpu.VMEM((tile, D), bf),
                            pltpu.VMEM((tile, D), f32), pltpu.VMEM((tile, D), f32), pltpu.VMEM((2, tile, 512), f32),
                            pltpu.VMEM((2, tile, 512), f32), pltpu.VMEM((2, tile, 512), bf), pltpu.VMEM((2, tile, 512), bf),
                            pltpu.SemaphoreType.DMA((2 * len(places),)), pltpu.SemaphoreType.DMA((2 * len(places),))]),
        compiler_params=pltpu.CompilerParams(vmem_limit_bytes=VMEM_ALL),
        cost_estimate=pl.CostEstimate(flops=T * 19 * 10**6, bytes_accessed=30 * 10**6, transcendentals=T * FF * 2),
    )(me, *ins)


def assemble_kernel(me_ref, vec, dbi, ln, q01, q23, p01, p23, out, nat):
    out[...] = jnp.zeros(out.shape, f32)
    nat[0:2] = ln[0:2]
    nat[4:8] = vec[0:4]
    lane = lax.broadcasted_iota(jnp.int32, (1, 128), 1)
    top = jnp.full((1, 128), masked_score, f32)
    for k in range(4):
        q, p, i = (q01, p01, k) if k < 2 else (q23, p23, k - 2)
        group = me_ref[1] ^ k
        at = pl.multiple_of(group * 128, 128)
        nat[2:4, pl.ds(at, 128)] = q[2 * i:2 * i + 2]
        nat[pl.ds(8 + group, 1), :] = dbi[k:k + 1]
        for h in range(4):
            top = jnp.where(lane == group * 4 + h, p[4 * i + h:4 * i + h + 1], top)
    for i in range(12):
        out[2 * i:2 * i + 1] = nat[i:i + 1, 0:384]
        out[2 * i + 1:2 * i + 2, 0:128] = nat[i:i + 1, 384:512]
    out[24:25, 0:128] = top


def assemble(me, vec, dbi, ln, qs, ps):
    smem = pl.BlockSpec(memory_space=pltpu.SMEM)
    vmem = pl.BlockSpec(memory_space=pltpu.VMEM)
    return pl.pallas_call(
        assemble_kernel, out_shape=sds((32, QKV), f32), in_specs=[smem] + [vmem] * 7,
        scratch_shapes=[pltpu.VMEM((16, D), f32)],
        compiler_params=pltpu.CompilerParams(vmem_limit_bytes=VMEM_ALL),
    )(me, vec, dbi, ln, *qs, *ps)


def unpack_rest_kernel(rest, outw, inner, outer):
    outw[...] = rest[:, 0:128].astype(f32)
    inner[...] = rest[:, 128:640].astype(f32)
    outer[...] = rest[:, 640:1152].astype(f32)


def unpack_rest(rest):
    return pl.pallas_call(
        unpack_rest_kernel, out_shape=[sds((64, 128), f32), sds((64, 512), f32), sds((64, 512), f32)],
        compiler_params=pltpu.CompilerParams(vmem_limit_bytes=VMEM_ALL),
    )(rest)


def unpack_kernel(me_ref, buf, tri, triple, table, clipped, peaks, dbi, *vectors):
    flat = me_ref[3]
    b = buf[...].astype(f32)
    for c in range(3):
        triple[c] = b[0:64, c * 128:(c + 1) * 128]
    for h in range(4):
        for c in range(7):
            hi = min(QKV, TABLE - c * QKV)
            table[h:h + 1, c * QKV:c * QKV + hi] = b[64 + h * 7 + c:65 + h * 7 + c, 0:hi]
    rows = [jnp.concatenate([b[96 + 2 * i:97 + 2 * i], b[97 + 2 * i:98 + 2 * i, 0:128]], axis=1) for i in range(12)]
    first = jnp.concatenate(rows[0:8], axis=0)
    first = pltpu.roll(first, 512 - flat * 16, 1)
    for i in range(8):
        vectors[i][...] = first[i:i + 1, 0:16].reshape(16)
    wide = rows[8]
    for i in range(1, 4):
        wide = jnp.where(flat // 8 == i, rows[8 + i], wide)
    dbi[...] = pltpu.roll(jnp.broadcast_to(wide, (8, 512)), 512 - (flat % 8) * 64, 1)[0:1, 0:64].reshape(64)
    top = jnp.broadcast_to(b[120:121, 0:128], (8, 128))
    top = pltpu.roll(top, 128 - me_ref[1] * 4, 1)[0:1]
    peaks[...] = top[:, 0:4].reshape(4)
    root = jnp.sqrt(clip_target / jnp.maximum(top, clip_target))
    lane = lax.broadcasted_iota(jnp.int32, (1, 128), 1) // 32
    scale = jnp.zeros((1, 128), f32)
    for h in range(4):
        scale = jnp.where(lane == h, root[:, h:h + 1], scale)
    for c in range(2):
        clipped[c] = tri[c] * scale


def unpack(me, buf, triple_weight):
    smem = pl.BlockSpec(memory_space=pltpu.SMEM)
    vmem = pl.BlockSpec(memory_space=pltpu.VMEM)
    return pl.pallas_call(
        unpack_kernel,
        out_shape=[sds((3, 64, 128), f32), sds((4, TABLE), f32), sds((2, 64, 128), f32), sds((4,), f32), sds((64,), f32)] +
        [sds((16,), f32)] * 8,
        in_specs=[smem, vmem, vmem], compiler_params=pltpu.CompilerParams(vmem_limit_bytes=VMEM_ALL),
    )(me, buf, triple_weight)


def swap(x, axis, bit):
    return lax.ppermute(x, axis, [(i, i ^ bit) for i in range(lax.axis_size(axis))])


Z1, Z0, Y, X, C = ("dp", 4), ("dp", 2), ("dp", 1), ("mp", 2), ("mp", 1)
DP_BLOCKS = [(p & 1) * 4 + (p & 2) + (p >> 2) for p in range(8)]


def after(x, *deps):
    return lax.optimization_barrier((x,) + deps)[0]


def join(x, y):
    return jnp.concatenate([x, y], axis=0)


def widen(x, step):
    return join(x, swap(x, *step))


def rest_places():
    out = []
    for arr in range(8):
        c, kind = arr >> 2, arr & 3
        for i in range(4):
            z1, z0 = i & 1, kind >> 1
            x, y = (kind & 1, i >> 1) if z0 == 0 else (i >> 1, kind & 1)
            out.append((arr, i, c + 2 * x, z1 * 4 + z0 * 2 + y))
    return out


def canonical(a, parts):
    m, d, rows, width = a.shape
    own = width // parts
    a = a.reshape(4, m // 4, d, rows, parts, own).transpose(0, 2, 3, 4, 1, 5)
    return a.reshape(4, d * rows, parts * (m // 4) * own)


def uncanonical(a, parts, m, d):
    own = a.shape[2] // parts // (m // 4)
    a = a.reshape(4, d, D // d, parts, m // 4, own).transpose(0, 4, 1, 2, 3, 5)
    return a.reshape(m * d, D // d, parts * own)


def shards(tokens, regions, first_gain, first_shift, triple_weight, query_bias, value_bias, offset_table, output_weight,
           output_bias, second_gain, second_shift, inner_weight, inner_bias, outer_weight, outer_bias, cotangent):
    ndp, nmp = lax.axis_size("dp"), lax.axis_size("mp")
    me_dp, me_mp = lax.axis_index("dp"), lax.axis_index("mp")
    nw = tokens.shape[0] // WIN
    hot = jnp.asarray(place_onehot())
    smalls = [first_gain, first_shift, query_bias, value_bias, output_bias, second_gain, second_shift, outer_bias, inner_bias]
    T = tokens.shape[0]
    x3 = tokens.reshape(nw, WIN, D)
    three = lambda a: a.reshape(nw, WIN, a.shape[-1])
    flat = lambda a: a.reshape(T, a.shape[-1])
    tile = 392 if T % 392 == 0 else T
    near_ks, far_ks = (0, 1), (2, 3)
    if (ndp, nmp) == (8, 4):
        me = jnp.stack([me_dp, me_mp, me_mp * nw, me_dp * nmp + me_mp]).astype(jnp.int32)
        pk, rest, t0 = pack(triple_weight, output_weight.T, inner_weight, outer_weight.T, offset_table, *smalls)
        t1 = swap(t0, *C)
        t2 = swap(t0, *X)
        w = pk[None]
        w_z1 = swap(w, *Z1)
        t3 = swap(t2, *C)
        a = rest[None]
        a_z1 = swap(a, *Z1)
        near_bias = bias_grid([t0, t1], hot)
        w = join(w, after(w_z1, near_bias))
        a = join(a, after(a_z1, near_bias))
        w_z0 = swap(w, *Z0)
        b = swap(a, *Z0)
        w = join(w, w_z0)
        w_y = swap(w, *Y)
        far_bias = bias_grid([after(t2, w), t3], hot)
        w0 = join(w, after(w_y, far_bias, b))
        ay = swap(after(a, w0), *Y)
        w1 = swap(w0, *C)
        w2 = swap(w0, *X)
        n1, small, *near = attend_fwd(near_ks, me, after(x3, b), [w0, w1], w0, near_bias, regions, DP_BLOCKS)
        bx = swap(b, *X)
        w3 = swap(after(w2, n1), *C)
        a0, b_0 = join(a, after(ay, n1)), join(b, after(bx, n1))
        a1, b_1 = swap(a0, *X), swap(b_0, *Y)
        ca0, cb0 = swap(a0, *C), swap(b_0, *C)
        far = attend_fwd(far_ks, me, after(n1, a0, b_0), [w2, w3], small, far_bias, regions, DP_BLOCKS)
        ca1, cb1 = swap(after(a1, far[0]), *C), swap(after(b_1, far[0]), *C)
        result, dy, dyb, wo, vec, dbi, k0, k1, k2, k3, sent = mlp(
            me, tokens, cotangent, [flat(near[3]), flat(far[3])], (near_ks, far_ks), small,
            [a0, a1, b_0, b_1, ca0, ca1, cb0, cb1], rest_places(), 4, tile)
        got = swap(sent, *C)
        dn, far_pair, far_vec = attend_bwd(far_ks, me, n1, far[0], far[1], far[2], far[4], three(dyb), wo, far[6], hot,
                                           None, None, DP_BLOCKS)
        got = after(got, dn)
        ga0, ga1, gb0, gb1 = [kept + got[4 * i:4 * i + 4] for i, kept in enumerate((k0, k1, k2, k3))]
        xa1, yb1 = swap(ga1, *X), swap(gb1, *Y)
        xfar = swap(far_pair, *X)
        dn, near_pair, near_vec, ln = attend_bwd(
            near_ks, me, n1, near[0], near[1], near[2], near[4], three(dyb), wo, near[6], hot,
            after(dn, ga0, ga1, gb0, gb1), (x3, three(dy), small), DP_BLOCKS)
        near_vec, near_pair, xfar, xa1, yb1 = lax.optimization_barrier((near_vec, near_pair, xfar, xa1, yb1))
        vecs = assemble(me, vec, dbi, ln, [near_vec, far_vec], [near[5], far[5]])
        core = swap(near_pair[PAIR:] + xfar[PAIR:], *C)
        peak_row = lax.broadcasted_iota(jnp.int32, (32, QKV), 0) == 24
        for step in (X, C):
            got = swap(vecs, *step)
            vecs = jnp.where(peak_row, jnp.maximum(vecs, got), vecs + got)
        buf = join(near_pair[:PAIR] + xfar[:PAIR] + core, vecs.astype(bf))
        ga0, gb0 = ga0 + xa1, gb0 + yb1
        ga, gb = ga0[:2] + swap(ga0[2:], *Y), gb0[:2] + swap(gb0[2:], *X)
        ga = ga + swap(gb, *Z0)
        rest_sum = ga[0] + swap(ga[1], *Z1)
        for step in (Y, Z0, Z1):
            half = (buf.shape[0] - 64) // 2
            got = swap(buf[half:], *step)
            own = join(buf[:half], buf[2 * half:])
            peak = lax.broadcasted_iota(jnp.int32, own.shape, 0) == half + 56
            buf = jnp.where(peak, jnp.maximum(own, got), own + got)
        outw, inner, outer = unpack_rest(rest_sum)
        triple, table, clipped, peaks, dbi, *v = unpack(me, buf, triple_weight)
        return (result, flat(dn), v[0], v[1], triple, v[2], v[3], table, outw.T, v[7], v[5], v[6], inner, dbi, outer.T, v[4],
                peaks, clipped)

    rows, own = D // ndp, D // nmp
    both = ("mp", "dp")
    shape = (nmp, ndp, rows, -1)
    me = jnp.stack([0 * me_dp, 0 * me_mp, me_mp * nw, me_dp * nmp + me_mp]).astype(jnp.int32)
    everywhere = lambda a: lax.all_gather(a.astype(bf), both).reshape(shape)
    wcanon = canonical(everywhere(triple_weight.transpose(1, 0, 2).reshape(rows, 3 * own)), 3)
    warrs = [jnp.concatenate([canonical(everywhere(a), 1) for a in (output_weight.T, inner_weight, outer_weight.T)], axis=2)]
    eight = lax.all_gather(jnp.stack(smalls[:8]).astype(bf), "dp", axis=1, tiled=True).reshape(8, 8, 64).transpose(1, 0, 2)
    eight = jnp.pad(eight, ((0, 0), (0, 0), (0, QKV - 64)))
    ninth = lax.all_gather(inner_bias.astype(bf), "dp", tiled=True).reshape(8, 1, 256)
    ninth = jnp.pad(ninth, ((0, 0), (0, 7), (0, QKV - 256)))
    small_src = jnp.concatenate([eight, ninth], axis=1)
    tables = lax.all_gather(offset_table.astype(bf), "mp", tiled=True)
    tables = jnp.pad(tables, ((0, 0), (0, TLANES - TABLE))).reshape(4, 16, 640)
    bias = [bias_grid([tables[k], tables[k + 1]], hot) for k in (0, 2)]
    blocks = [0]
    wk = [wcanon[k:k + 1] for k in range(4)]
    n1, small, *near = attend_fwd(near_ks, me, x3, wk[:2], small_src, bias[0], regions, blocks)
    far = attend_fwd(far_ks, me, n1, wk[2:], small, bias[1], regions, blocks)
    result, dy, dyb, wo, vec, dbi, rg = mlp(
        me, tokens, cotangent, [flat(near[3]), flat(far[3])], (near_ks, far_ks), small, warrs,
        [(0, k, k, 0) for k in range(4)], 1, tile)
    dn, far_pair, far_vec = attend_bwd(far_ks, me, n1, far[0], far[1], far[2], far[4], three(dyb), wo, far[6], hot,
                                       None, None, blocks)
    dx, near_pair, near_vec, ln = attend_bwd(
        near_ks, me, n1, near[0], near[1], near[2], near[4], three(dyb), wo, near[6], hot, dn, (x3, three(dy), small), blocks)
    vecs = assemble(me, vec, dbi, ln, [near_vec, far_vec], [near[5], far[5]])
    pairs = jnp.concatenate([near_pair, far_pair]).reshape(4, PAIR, QKV)
    dx = flat(dx)
    reduce = lambda a, parts: lax.psum_scatter(uncanonical(a, parts, nmp, ndp), both, tiled=True)[0].astype(f32)
    triple = reduce(pairs[:, :D], 3).reshape(rows, 3, own).transpose(1, 0, 2)
    outw = reduce(rg[:, :, 0:128], 1).T
    inner = reduce(rg[:, :, 128:640], 1)
    outer = reduce(rg[:, :, 640:1152], 1).T
    here = HEADS // nmp
    table = lax.psum(pairs[:, D:D + 28].astype(f32).reshape(HEADS, 7 * QKV)[:, :TABLE], both)
    table = lax.dynamic_slice_in_dim(table, me_mp * here, here)
    peaks = lax.dynamic_slice_in_dim(lax.pmax(vecs[24, :HEADS], both), me_mp * here, here)
    sums = lax.psum(vecs[:24].reshape(12, 2 * QKV)[:, :D], both)

    def piece(vector):
        width = vector.shape[0] // (ndp * nmp)
        return lax.dynamic_slice_in_dim(vector, (me_dp * nmp + me_mp) * width, width)

    factor = clip_target / jnp.maximum(peaks, clip_target)
    clipped = triple_weight[:2] * jnp.repeat(jnp.sqrt(factor), HEAD_DIM)[None, None, :]
    v = [piece(sums[i]) for i in range(8)]
    dbi = piece(sums[8:12].reshape(FF))
    return (result, dx, v[0], v[1], triple, v[2], v[3], table, outw, v[7], v[5], v[6], inner, dbi, outer, v[4], peaks, clipped)


def solution(mesh):
    rows = P(("dp", "mp"), None)
    vector = P("dp")
    every = P(("dp", "mp"))
    three = P(None, "dp", "mp")
    down, across = P("mp", "dp"), P("dp", "mp")
    return jax.shard_map(
        shards,
        mesh=mesh,
        in_specs=(rows, P("dp", None), vector, vector, three, vector, vector, P("mp", None), down, vector, vector, vector,
                  across, vector, down, vector, rows),
        out_specs=(rows, rows, every, every, three, every, every, P("mp", None), down, every, every, every, across, every,
                   down, every, P("mp"), three),
        check_vma=False,
    )
```

```python
import functools
import math

import jax
import jax.numpy as jnp
import numpy as np
from jax import lax
from jax.experimental import pallas as pl
from jax.experimental.pallas import tpu as pltpu
from jax.sharding import PartitionSpec as P

D = 512
HEADS = 16
HEAD_DIM = 32
FF = 2048
WIN = 392
PLACES = 49
TIMES = 8
SPACE = 169
TABLE = 2535
TLANES = 2560
GROUP = 128
QKV = 384
REST = 1152
SMALL = 16
SLANES = 8 * QKV
norm_epsilon = 1e-05
masked_score = -1e9
clip_target = 10.0
log2e = math.log2(math.e)
score_scale = 1.0 / math.sqrt(HEAD_DIM)
bf = jnp.bfloat16
f32 = jnp.float32
ROWS = [(s, min(64, WIN - s)) for s in range(0, WIN, 64)]
PAIR = D + 32
density_scale = 0.3989422804014327
ERFC = [c * 0.5 / density_scale for c in (0.254829592, -0.284496736, 1.421413741, -1.453152027, 1.061405429)]
VMEM_ALL = 63 * 2**20
sds = jax.ShapeDtypeStruct


def dd(a, b, ca, cb):
    return lax.dot_general(a, b, (((ca,), (cb,)), ((), ())), preferred_element_type=f32)


def fold_max(acc, x):
    for r in range(0, x.shape[0], 8):
        acc = jnp.maximum(acc, x[r:r + 8])
    return acc


def full(shape):
    return pl.BlockSpec(shape, lambda w, me: (0,) * len(shape), pipeline_mode=pl.Buffered(1))


def win(shape):
    return pl.BlockSpec((1,) + shape, lambda w, me: (w,) + (0,) * len(shape))


HBM = pl.BlockSpec(memory_space=pl.ANY)


def small_vector(small, row):
    return jnp.concatenate([small[row:row + 1, d * QKV:d * QKV + 64] for d in range(8)], axis=1)


def group_vector(small, row, group):
    parts = []
    for half in range(2):
        at = pl.multiple_of((group * 2 + half) * QKV, 128)
        parts.append(small[row:row + 1, pl.ds(at, 128)][:, :64])
    return jnp.concatenate(parts, axis=1)


def pack_kernel(tri, outw, inner, outer, table, *refs):
    smalls, (pk, rest, tab) = refs[:9], refs[9:]
    for c in range(3):
        pk[0:64, c * 128:(c + 1) * 128] = tri[c].astype(bf)
    rows = [jnp.pad(s[...].reshape(1, -1), ((0, 0), (0, QKV - s.shape[0]))) for s in smalls]
    pk[64:80, :] = jnp.concatenate(rows + [jnp.zeros((7, QKV), f32)], axis=0).astype(bf)
    rest[:, 0:128] = outw[...].astype(bf)
    rest[:, 128:640] = inner[...].astype(bf)
    rest[:, 640:1152] = outer[...].astype(bf)
    t = jnp.pad(table[...], ((0, 0), (0, TLANES - TABLE)))
    tab[...] = jnp.concatenate([t[h:h + 1, c * 640:(c + 1) * 640] for h in range(4) for c in range(4)], axis=0).astype(bf)


def pack(*params):
    return pl.pallas_call(
        pack_kernel,
        out_shape=[sds((80, QKV), bf), sds((64, REST), bf), sds((16, 640), bf)],
        compiler_params=pltpu.CompilerParams(vmem_limit_bytes=VMEM_ALL),
    )(*params)


SLABS = (0, 768, 1408)
SLAB = 1152


def place_onehot():
    at = np.arange(PLACES)
    code = (at // 7) * 13 + at % 7
    hot = np.zeros((TLANES, 768), np.float32)
    for a in range(15):
        hot[a * SPACE + code, a * PLACES + at] = 1.0
    return np.stack([hot[r:r + SLAB, j * 256:(j + 1) * 256] for j, r in enumerate(SLABS)]).astype(bf)


def grid_kernel(t0, t1, hot_hbm, out_hbm, hot, rolled, spread, out, hsem, osem):
    hot_copy = pltpu.make_async_copy(hot_hbm, hot, hsem)
    hot_copy.start()
    for h in range(8):
        t = t0 if h < 4 else t1
        flat = jnp.concatenate([t[4 * (h % 4) + c:4 * (h % 4) + c + 1] for c in range(4)], axis=1).astype(f32)
        steps = pltpu.roll(jnp.broadcast_to(flat, (8, TLANES)), 0, 1, stride=1, stride_axis=0)
        for y in range(7):
            rolled[h * 56 + y * 7:h * 56 + y * 7 + 8, :] = pltpu.roll(steps, TLANES - (84 - 13 * y), 1)
    hot_copy.wait()
    copies = []
    for j, r in enumerate(SLABS):
        spread[:, j * 256:(j + 1) * 256] = dd(rolled[0:448, r:r + SLAB].astype(bf), hot[j], 1, 0) * log2e
    for h in range(8):
        for t in range(TIMES):
            lo = (7 - t) * PLACES
            out[h, t * PLACES:(t + 1) * PLACES, :] = spread[h * 56:h * 56 + PLACES, lo:lo + WIN]
        copies.append(pltpu.make_async_copy(out.at[h], out_hbm.at[h], osem.at[h]))
        copies[-1].start()
    for c in copies:
        c.wait()


def bias_grid(tables, hot):
    vmem = pl.BlockSpec(memory_space=pltpu.VMEM)
    return pl.pallas_call(
        grid_kernel, out_shape=sds((8, WIN, WIN), f32),
        in_specs=[vmem, vmem, HBM], out_specs=HBM,
        scratch_shapes=[pltpu.VMEM((3, SLAB, 256), bf), pltpu.VMEM((456, TLANES), f32), pltpu.VMEM((448, 768), f32),
                        pltpu.VMEM((8, WIN, WIN), f32), pltpu.SemaphoreType.DMA, pltpu.SemaphoreType.DMA((8,))],
        compiler_params=pltpu.CompilerParams(vmem_limit_bytes=VMEM_ALL),
        cost_estimate=pl.CostEstimate(flops=5 * 10**9, bytes_accessed=9 * 10**6, transcendentals=0),
    )(*tables, hot)


def fwd_kernel(first, ks, nwin, blocks, *refs):
    ng = len(ks)
    refs = list(refs)
    take = lambda n: [refs.pop(0) for _ in range(n)]
    me_ref, x_ref = take(2)
    w_hbm = take(ng)
    s_in, = take(1)
    bias_hbm, = take(1)
    reg_ref, = take(1)
    if first:
        n1_out, s_out = take(2)
    qkv_out, e_out, ot_out, o_out, linv_out, hm_out, w_out = take(7)
    bias, mask, s_scr, hm_scr, wsem, bsem = take(6)
    if first:
        s_bf, ssem = take(2)
    w = pl.program_id(0)
    rows = D // len(blocks)
    bias_copies = [pltpu.make_async_copy(bias_hbm.at[pl.ds(4 * g, 4)], bias.at[pl.ds(4 * g, 4)], bsem.at[g]) for g in range(ng)]

    @pl.when(w == 0)
    def _():
        copies = []
        if first:
            at_row = s_in.shape[1] - SMALL
            order = blocks if len(blocks) == 8 else list(range(8))
            for p, blk in enumerate(order):
                at = pl.multiple_of((me_ref[0] ^ blk) * QKV, 128)
                copies.append(pltpu.make_async_copy(
                    s_in.at[p, at_row:at_row + SMALL], s_bf.at[:, pl.ds(at, QKV)], ssem.at[p]))
        for g in range(ng):
            for p, blk in enumerate(blocks):
                at = pl.multiple_of((me_ref[0] ^ blk) * rows, rows)
                copies.append(pltpu.make_async_copy(
                    w_hbm[g].at[p, 0:rows], w_out.at[pl.ds(at, rows), g * QKV:(g + 1) * QKV], wsem.at[g * len(blocks) + p]))
        for c in copies + bias_copies:
            c.start()
        for c in copies:
            c.wait()
        if first:
            s_out[...] = s_bf[...].astype(f32)
        hm_scr[...] = jnp.full(hm_scr.shape, -jnp.inf, f32)

    small = s_out if first else s_in
    region = reg_ref[pl.ds(me_ref[2] + w, 1), :].astype(f32)
    column = jnp.broadcast_to(region, (8, WIN)).T[:, 0:1]
    mask[...] = jnp.where(column == region, 0.0, masked_score)
    if first:
        x = x_ref[0].astype(f32)
        xc = x - jnp.mean(x, axis=1, keepdims=True)
        inv = lax.rsqrt(jnp.mean(xc * xc, axis=1, keepdims=True) + norm_epsilon)
        n1 = (xc * inv * small_vector(small, 0) + small_vector(small, 1)).astype(bf)
        n1_out[0] = n1
    else:
        n1 = x_ref[0]
    pall = dd(n1, w_out[...], 1, 0)
    ones = jnp.ones((16, WIN), bf)

    kbs, qTs, vTs = [], [], []
    for g in range(ng):
        group = me_ref[1] ^ ks[g]
        p = pall[:, g * QKV:(g + 1) * QKV]
        q = (p[:, :128] + group_vector(small, 2, group)) * (score_scale * log2e)
        kb = p[:, 128:256].astype(bf)
        v = p[:, 256:] + group_vector(small, 3, group)
        qkv_out[0, :, g * QKV:g * QKV + 128] = q.astype(bf)
        qkv_out[0, :, g * QKV + 128:g * QKV + 256] = kb
        qkv_out[0, :, g * QKV + 256:g * QKV + 384] = v.astype(bf)
        kbs.append(kb)
        qTs.append(q.T.astype(bf))
        vTs.append(v.T.astype(bf))

    nh = 4 * ng
    outs, linvs = [], []

    def scores(h):
        sl = slice(h % 4 * 32, h % 4 * 32 + 32)
        return dd(kbs[h // 4][:, sl], qTs[h // 4][sl], 1, 0)

    def mix(h):
        sl = slice(h % 4 * 32, h % 4 * 32 + 32)
        ol = dd(jnp.concatenate([vTs[h // 4][sl], ones], axis=0), e_out[0, h], 1, 0)
        linv = 1.0 / ol[32:33]
        linvs.append(linv)
        outs.append(ol[:32] * linv)
        if h % 4 == 3:
            g = h // 4
            oT = jnp.concatenate(outs[-4:], axis=0)
            ot_out[0, g * 128:(g + 1) * 128] = oT.astype(bf)
            o_out[0, :, g * 128:(g + 1) * 128] = oT.T.astype(bf)

    s = scores(0)

    @pl.when(w == 0)
    def _():
        for c in bias_copies:
            c.wait()

    for h in range(nh):
        after_s = scores(h + 1) if h + 1 < nh else None
        hm = jnp.full((8, WIN), -jnp.inf, f32)
        m = jnp.full((8, WIN), -jnp.inf, f32)
        for r, n in ROWS:
            c = s[r:r + n]
            hm = fold_max(hm, c)
            c = c + bias[h, r:r + n] + mask[r:r + n]
            m = fold_max(m, c)
            s_scr[h % 2, r:r + n] = c
        hm_scr[h] = jnp.maximum(hm_scr[h], hm)
        m = jnp.max(m, axis=0, keepdims=True)
        if h > 0:
            mix(h - 1)
        for r, n in ROWS:
            e_out[0, h, r:r + n] = jnp.exp2(s_scr[h % 2, r:r + n] - m).astype(bf)
        s = after_s
    mix(nh - 1)
    if ng == 1:
        linvs.append(jnp.zeros((4, WIN), f32))
    linv_out[0] = jnp.concatenate(linvs, axis=0)

    @pl.when(w == nwin - 1)
    def _():
        tops = [jnp.broadcast_to(jnp.max(hm_scr[h], keepdims=True), (1, 128)) for h in range(4 * ng)]
        if ng == 1:
            tops.append(jnp.zeros((4, 128), f32))
        hm_out[...] = jnp.concatenate(tops, axis=0) * (1.0 / log2e)


def attend_fwd(ks, me, x, wblk, small, bias, regions, blocks):
    first = ks[0] == 0
    ng = len(ks)
    nw = x.shape[0]
    ins = [x, *wblk, small, bias, regions]
    in_specs = [win((WIN, D))] + [HBM] * ng + [HBM if first else full(small.shape), HBM, full(regions.shape)]
    outs = ([sds((nw, WIN, D), bf), sds((SMALL, SLANES), f32)] if first else []) + [
        sds((nw, WIN, ng * QKV), bf), sds((nw, ng * 4, WIN, WIN), bf), sds((nw, ng * GROUP, WIN), bf),
        sds((nw, WIN, ng * GROUP), bf), sds((nw, 8, WIN), f32), sds((8, 128), f32), sds((D, ng * QKV), bf)]
    out_specs = ([win((WIN, D)), full((SMALL, SLANES))] if first else []) + [
        win((WIN, ng * QKV)), win((ng * 4, WIN, WIN)), win((ng * GROUP, WIN)), win((WIN, ng * GROUP)), win((8, WIN)),
        full((8, 128)), full((D, ng * QKV))]
    scratch = [pltpu.VMEM((ng * 4, WIN, WIN), f32), pltpu.VMEM((WIN, WIN), f32), pltpu.VMEM((2, WIN, WIN), f32),
               pltpu.VMEM((ng * 4, 8, WIN), f32), pltpu.SemaphoreType.DMA((ng * len(blocks),)), pltpu.SemaphoreType.DMA((ng,))]
    if first:
        scratch += [pltpu.VMEM((SMALL, SLANES), bf), pltpu.SemaphoreType.DMA((8,))]
    return pl.pallas_call(
        functools.partial(fwd_kernel, first, ks, nw, blocks), out_shape=outs,
        grid_spec=pltpu.PrefetchScalarGridSpec(
            num_scalar_prefetch=1, grid=(nw,), in_specs=in_specs, out_specs=out_specs, scratch_shapes=scratch),
        compiler_params=pltpu.CompilerParams(vmem_limit_bytes=VMEM_ALL),
        cost_estimate=pl.CostEstimate(flops=ng * nw * 3 * 10**9, bytes_accessed=nw * ng * 4 * 10**6,
                                      transcendentals=ng * nw * 4 * WIN * WIN),
    )(me, *ins)


def bwd_kernel(ks, first, last, nwin, blocks, *refs):
    ng = len(ks)
    refs = list(refs)
    take = lambda n: [refs.pop(0) for _ in range(n)]
    me_ref, n1_ref, qkv_ref, e_ref, ot_ref, linv_ref, dyb_ref, wo_ref, w_ref, hot_hbm = take(10)
    prev_ref = None if first else take(1)[0]
    if last:
        x_ref, dy_ref, small_ref = take(3)
    dn_out, dw_out, vec_out = take(3)
    if last:
        ln_out, = take(1)
    dwacc, dls, p_scr, dl_scr, hot, spread, rolled, hsem = take(8)
    w = pl.program_id(0)
    hot_copy = pltpu.make_async_copy(hot_hbm, hot, hsem)

    @pl.when(w == 0)
    def _():
        hot_copy.start()
        dwacc[...] = jnp.zeros(dwacc.shape, f32)
        dls[...] = jnp.zeros(dls.shape, f32)
        vec_out[...] = jnp.zeros(vec_out.shape, f32)
        if last:
            ln_out[...] = jnp.zeros(ln_out.shape, f32)

    do_all = dd(dyb_ref[0], wo_ref[:, ks[0] * 128:(ks[0] + ng) * 128], 1, 0)
    lane = lax.broadcasted_iota(jnp.int32, (1, 128), 1) // 32
    nh = 4 * ng
    qs, vs, kTs, doTs, dos, rs = [], [], [], [], [], []
    for g in range(ng):
        qs.append(qkv_ref[0, :, g * QKV:g * QKV + 128])
        k = qkv_ref[0, :, g * QKV + 128:g * QKV + 256]
        vs.append(qkv_ref[0, :, g * QKV + 256:g * QKV + 384])
        doT = do_all[:, g * 128:(g + 1) * 128].T
        oT = ot_ref[0, g * 128:(g + 1) * 128].astype(f32)
        scaled = []
        for h in range(4):
            sl = slice(h * 32, h * 32 + 32)
            s = (doT[sl] * linv_ref[0, 4 * g + h:4 * g + h + 1]).astype(bf)
            scaled.append(s)
            rs.append(jnp.sum(s.astype(f32) * oT[sl], axis=0, keepdims=True))
        doTs.append(jnp.concatenate(scaled, axis=0))
        dos.append(doTs[g].astype(f32).T.astype(bf))
        kTs.append(k.astype(f32).T.astype(bf))
    none = jnp.zeros((), bf)
    dks = [jnp.zeros((WIN, 128), f32)] * ng
    dvs = [jnp.zeros((WIN, 128), f32)] * ng
    dqT = []

    def slopes(h):
        sl = slice(h % 4 * 32, h % 4 * 32 + 32)
        return dd(vs[h // 4][:, sl], doTs[h // 4][sl], 1, 0)

    def products(h):
        g = h // 4
        own = lane == h % 4
        dqT.append(dd(kTs[g][h % 4 * 32:h % 4 * 32 + 32], dl_scr[h % 2], 1, 0))
        yield
        dks[g] = dks[g] + dd(dl_scr[h % 2], jnp.where(own, qs[g], none), 1, 0)
        yield
        dvs[g] = dvs[g] + dd(e_ref[0, h], jnp.where(own, dos[g], none), 1, 0)
        yield

    p = slopes(0)
    for h in range(nh):
        nextp = slopes(h + 1) if h + 1 < nh else None
        heavy = products(h - 1) if h > 0 else iter(())
        for i, (r, n) in enumerate(ROWS):
            if i % 3 == 0:
                next(heavy, None)
            dl = e_ref[0, h, r:r + n].astype(f32) * (p[r:r + n] - rs[h])
            dls[h, r:r + n] += dl
            dl_scr[h % 2, r:r + n] = dl.astype(bf)
        for _ in heavy:
            pass
        p = nextp
    for _ in products(nh - 1):
        pass
    parts = []
    for g in range(ng):
        dq = jnp.concatenate(dqT[4 * g:4 * g + 4], axis=0).T * score_scale
        vec_out[2 * g:2 * g + 1] += jnp.sum(dq, axis=0, keepdims=True)
        vec_out[2 * g + 1:2 * g + 2] += jnp.sum(dvs[g], axis=0, keepdims=True)
        parts += [dq.astype(bf), (dks[g] * (1.0 / log2e)).astype(bf), dvs[g].astype(bf)]
    dqkv = jnp.concatenate(parts, axis=1)
    dwacc[...] += dd(n1_ref[0], dqkv, 0, 0)
    dn1 = dd(dqkv, w_ref[...], 1, 1)
    if not first:
        dn1 = dn1 + prev_ref[0]
    if last:
        x = x_ref[0].astype(f32)
        xc = x - jnp.mean(x, axis=1, keepdims=True)
        inv = lax.rsqrt(jnp.mean(xc * xc, axis=1, keepdims=True) + norm_epsilon)
        u = xc * inv
        ln_out[0:1] += jnp.sum(dn1 * u, axis=0, keepdims=True)
        ln_out[1:2] += jnp.sum(dn1, axis=0, keepdims=True)
        a = dn1 * small_vector(small_ref, 0)
        gr = inv * (a - jnp.mean(a, axis=1, keepdims=True) - u * jnp.mean(a * u, axis=1, keepdims=True))
        dn_out[0] = (dy_ref[0] + gr).astype(bf)
    else:
        dn_out[0] = dn1

    @pl.when(w == nwin - 1)
    def _():
        rows = D // len(blocks)
        spread[...] = jnp.zeros(spread.shape, f32)
        for h in range(4 * ng):
            for t in range(TIMES):
                lo = (7 - t) * PLACES
                spread[h * 56:h * 56 + PLACES, lo:lo + WIN] += dls[h, t * PLACES:(t + 1) * PLACES, :]
        for g in range(ng):
            for kk, blk in enumerate(blocks):
                at = pl.multiple_of((me_ref[0] ^ blk) * rows, rows)
                dw_out[g * PAIR + kk * rows:g * PAIR + (kk + 1) * rows] = dwacc[pl.ds(at, rows), g * QKV:(g + 1) * QKV].astype(bf)
        hot_copy.wait()
        slab = [dd(spread[:, j * 256:(j + 1) * 256].astype(bf), hot[j], 1, 1) for j in range(3)]
        low, high = SLABS[1], SLABS[2]
        rolled[0:224 * ng, 0:low] = slab[0][:, :low]
        rolled[0:224 * ng, low:SLAB] = slab[0][:, low:] + slab[1][:, :SLAB - low]
        rolled[0:224 * ng, SLAB:high] = slab[1][:, SLAB - low:high - low]
        rolled[0:224 * ng, high:low + SLAB] = slab[1][:, high - low:] + slab[2][:, :low + SLAB - high]
        rolled[0:224 * ng, low + SLAB:TLANES] = slab[2][:, low + SLAB - high:]
        rolled[224 * ng:224 * ng + 8] = jnp.zeros((8, TLANES), f32)
        row = lax.broadcasted_iota(jnp.int32, (8, 1), 0)
        for g in range(ng):
            lines = []
            for h in range(4 * g, 4 * g + 4):
                acc = jnp.zeros((8, TLANES), f32)
                for y in range(7):
                    part = rolled[h * 56 + y * 7:h * 56 + y * 7 + 8, :]
                    acc += pltpu.roll(jnp.where(row < 7, part, 0.0), 84 - 13 * y, 1)
                for bit in (1, 2, 4):
                    acc = jnp.where((row & bit) != 0, pltpu.roll(acc, TLANES - bit, 1), acc)
                flat = jnp.sum(acc, axis=0, keepdims=True)
                flat = jnp.concatenate([flat, jnp.zeros((1, 7 * QKV - TLANES), f32)], axis=1)
                lines += [flat[:, c * QKV:(c + 1) * QKV] for c in range(7)]
            lines.append(jnp.zeros((4, QKV), f32))
            dw_out[g * PAIR + D:(g + 1) * PAIR] = jnp.concatenate(lines, axis=0).astype(bf)


def attend_bwd(ks, me, n1, qkv, e, oT, linv, dyb, wo, w, hot, prev, last, blocks):
    ng = len(ks)
    nw = n1.shape[0]
    first = prev is None
    ins = [n1, qkv, e, oT, linv, dyb, wo, w, hot] + ([] if first else [prev]) + (list(last) if last else [])
    in_specs = ([win((WIN, D)), win((WIN, ng * QKV)), win((ng * 4, WIN, WIN)), win((ng * GROUP, WIN)), win((8, WIN)),
                 win((WIN, D)), full((D, D)), full((D, ng * QKV)), HBM] + ([] if first else [win((WIN, D))]) +
                ([win((WIN, D)), win((WIN, D)), full(last[2].shape)] if last else []))
    outs = [sds((nw, WIN, D), bf if last else f32), sds((ng * PAIR, QKV), bf), sds((8, 128), f32)]
    out_specs = [win((WIN, D)), full((ng * PAIR, QKV)), full((8, 128))]
    if last:
        outs.append(sds((8, D), f32))
        out_specs.append(full((8, D)))
    return pl.pallas_call(
        functools.partial(bwd_kernel, ks, first, bool(last), nw, blocks), out_shape=outs,
        grid_spec=pltpu.PrefetchScalarGridSpec(
            num_scalar_prefetch=1, grid=(nw,), in_specs=in_specs, out_specs=out_specs,
            scratch_shapes=[pltpu.VMEM((D, ng * QKV), f32), pltpu.VMEM((ng * 4, WIN, WIN), f32), pltpu.VMEM((8, 128), f32),
                            pltpu.VMEM((2, WIN, WIN), bf), pltpu.VMEM((3, SLAB, 256), bf), pltpu.VMEM((224 * ng, 768), f32),
                            pltpu.VMEM((224 * ng + 8, TLANES), f32), pltpu.SemaphoreType.DMA]),
        compiler_params=pltpu.CompilerParams(vmem_limit_bytes=VMEM_ALL),
        cost_estimate=pl.CostEstimate(flops=ng * nw * 4 * 10**9, bytes_accessed=ng * nw * 5 * 10**6, transcendentals=0),
    )(me, *ins)


def chunks(n, size):
    return [(r, min(size, n - r)) for r in range(0, n, size)]


def mlp_kernel(spec, *refs):
    places, brow, nkeep, narr, ntile, groups = spec
    refs = list(refs)
    take = lambda n: [refs.pop(0) for _ in range(n)]
    me_ref, x_ref, g_ref = take(3)
    o_refs = take(len(groups))
    small, = take(1)
    w_hbm = take(narr)
    res_out, dy_out, dyb_out, wo_out, vec_out, dbi_out = take(6)
    keeps = take(nkeep)
    send = take(1)[0] if narr > nkeep else None
    wscr, acc, stage, vin, bi, y_scr, u_scr, inv_scr, n2_scr, ff_scr, dn_scr, z_scr, dh_scr, hb_scr, dz_scr, wsem, osem = take(17)
    t = pl.program_id(0)
    me = me_ref[0]
    tile = x_ref.shape[0]
    bits = ((0, 128), (128, REST))

    def rows_of(blk):
        return pl.ds(pl.multiple_of((me ^ blk) * brow, brow), brow)

    def fetch(part, i):
        arr, idx, k, blk = places[i]
        lo, hi = bits[part]
        return pltpu.make_async_copy(
            w_hbm[arr].at[idx, :, lo:hi], wscr.at[k, rows_of(blk), lo:hi], wsem.at[part * len(places) + i])

    def leave(part, i):
        arr, idx, k, blk = places[i]
        lo, hi = bits[part]
        dst = keeps[arr].at[idx] if arr < nkeep else send.at[(arr - nkeep) * keeps[0].shape[0] + idx]
        return pltpu.make_async_copy(stage.at[k, rows_of(blk), lo:hi], dst.at[:, lo:hi], osem.at[part * len(places) + i])

    of = lambda k: [i for i, p in enumerate(places) if p[2] == k]

    @pl.when(t == 0)
    def _():
        for i in range(len(places)):
            fetch(0, i).start()
        for k in range(4):
            for i in of(k):
                fetch(1, i).start()
        for i in range(4):
            vin[i:i + 1] = small_vector(small, 4 + i)
        for k in range(4):
            for half in range(2):
                at = pl.multiple_of(((me_ref[1] ^ k) * 2 + half) * QKV, 128)
                bi[0:1, k * 512 + half * 256:k * 512 + half * 256 + 256] = small[8:9, pl.ds(at, 256)]
        acc[...] = jnp.zeros(acc.shape, f32)
        vec_out[...] = jnp.zeros(vec_out.shape, f32)
        dbi_out[...] = jnp.zeros(dbi_out.shape, f32)
        for i in range(len(places)):
            fetch(0, i).wait()
            fetch(1, i).wait()

    total = None
    for o_ref, ks in zip(o_refs, groups):
        part = dd(o_ref[...], jnp.concatenate([wscr[k, :, 0:128] for k in ks], axis=1), 1, 1)
        total = part if total is None else total + part
    y_scr[...] = total
    for r, n in chunks(tile, 32):
        y = x_ref[r:r + n].astype(f32) + y_scr[r:r + n] + vin[0:1]
        y_scr[r:r + n] = y
        yc = y - jnp.mean(y, axis=1, keepdims=True)
        inv = lax.rsqrt(jnp.mean(yc * yc, axis=1, keepdims=True) + norm_epsilon)
        u = yc * inv
        u_scr[r:r + n] = u
        inv_scr[r:r + n] = jnp.broadcast_to(inv, (n, 128))
        n2_scr[r:r + n] = (u * vin[1:2] + vin[2:3]).astype(bf)
    n2 = n2_scr[...]
    gb = g_ref[...]
    gT = gb.astype(f32).T.astype(bf)
    n2T = n2.astype(f32).T.astype(bf)
    def inner(k):
        z_scr[k % 2] = dd(n2, wscr[k, :, 128:640], 1, 0)
        dh_scr[k % 2] = dd(gb, wscr[k, :, 640:1152], 1, 0)

    def gelu(k):
        bias = bi[0:1, k * 512:(k + 1) * 512]
        total = jnp.zeros((8, 512), f32)
        for r, n in chunks(tile, 16):
            z = z_scr[k % 2, r:r + n] + bias
            pdf = jnp.exp2(z * z * (-0.5 * log2e) + math.log2(density_scale))
            tt = 1.0 / (1.0 + (0.3275911 * 0.7071067811865476) * jnp.abs(z))
            c1, c2, c3, c4, c5 = ERFC
            tail = tt * (c1 + tt * (c2 + tt * (c3 + tt * (c4 + tt * c5)))) * pdf
            phi = jnp.where(z >= 0, 1.0 - tail, tail)
            hb_scr[k % 2, r:r + n] = (z * phi).astype(bf)
            dz = dh_scr[k % 2, r:r + n] * (phi + z * pdf)
            for i in range(0, n, 8):
                total = total + dz[i:i + 8]
            dz_scr[k % 2, r:r + n] = dz.astype(bf)
            yield
        dbi_out[k:k + 1] += jnp.sum(total, axis=0, keepdims=True)

    def outer(k):
        hb = hb_scr[k % 2]
        dzb = dz_scr[k % 2]
        for c in range(2):
            lo, hi = c * 256, (c + 1) * 256
            part = dd(hb, wscr[k, lo:hi, 640:1152], 1, 1)
            ff_scr[:, lo:hi] = part if k == 0 else ff_scr[:, lo:hi] + part
            yield
            part = dd(dzb, wscr[k, lo:hi, 128:640], 1, 1)
            dn_scr[:, lo:hi] = part if k == 0 else dn_scr[:, lo:hi] + part
            yield
            acc[k, :, 640 + lo:640 + hi] += dd(gT, hb[:, lo:hi], 1, 0)
            yield
            acc[k, :, 128 + lo:128 + hi] += dd(n2T, dzb[:, lo:hi], 1, 0)
            yield

    inner(0)
    for _ in gelu(0):
        pass
    for k in range(4):
        if k < 3:
            inner(k + 1)
            light = gelu(k + 1)
        per = -(-len(chunks(tile, 16)) // 8)
        for _ in outer(k):
            if k < 3:
                for _ in range(per):
                    next(light, None)
        if k < 3:
            for _ in light:
                pass

    sums = [jnp.zeros((8, D), f32) for _ in range(4)]
    for r, n in chunks(tile, 32):
        res_out[r:r + n] = (y_scr[r:r + n] + ff_scr[r:r + n] + vin[3:4]).astype(bf)
        g = g_ref[r:r + n].astype(f32)
        u = u_scr[r:r + n]
        dn2 = dn_scr[r:r + n]
        a = dn2 * vin[1:2]
        dy = g + inv_scr[r:r + n, 0:1] * (
            a - jnp.mean(a, axis=1, keepdims=True) - u * jnp.mean(a * u, axis=1, keepdims=True))
        dy_out[r:r + n] = dy
        dyb_out[r:r + n] = dy.astype(bf)
        for j, term in enumerate((g, dn2 * u, dn2, dy)):
            for i in range(0, n, 8):
                sums[j] = sums[j] + term[i:i + 8]
    for j in range(4):
        vec_out[j:j + 1] += jnp.sum(sums[j], axis=0, keepdims=True)
    dyT = dyb_out[...].astype(f32).T.astype(bf)
    for o_ref, ks in zip(o_refs, groups):
        part = dd(dyT, o_ref[...], 1, 0)
        for i, k in enumerate(ks):
            acc[k, :, 0:128] += part[:, i * 128:(i + 1) * 128]

    @pl.when(t == ntile - 1)
    def _():
        for k in range(4):
            stage[k] = acc[k].astype(bf)
            for i in of(k):
                leave(0, i).start()
                leave(1, i).start()
        for k in range(4):
            wo_out[:, k * 128:(k + 1) * 128] = wscr[k, :, 0:128]
        for part in (1, 0):
            for i in range(len(places)):
                leave(part, i).wait()


def mlp(me, x, g, o_list, groups, small, warrs, places, nkeep, tile):
    T = x.shape[0]
    narr = len(warrs)
    n, brow, _ = warrs[0].shape
    row = lambda c: pl.BlockSpec((tile, c), lambda i, me: (i, 0))
    ins = [x, g] + list(o_list) + [small] + list(warrs)
    in_specs = [row(D), row(D)] + [row(o.shape[1]) for o in o_list] + [full(small.shape)] + [HBM] * narr
    outs = [sds((T, D), bf), sds((T, D), f32), sds((T, D), bf), sds((D, D), bf), sds((8, D), f32), sds((8, 512), f32)]
    out_specs = [row(D), row(D), row(D), full((D, D)), full((8, D)), full((8, 512))]
    outs += [sds((n, brow, REST), bf)] * nkeep
    out_specs += [HBM] * nkeep
    if narr > nkeep:
        outs.append(sds((n * (narr - nkeep), brow, REST), bf))
        out_specs.append(HBM)
    return pl.pallas_call(
        functools.partial(mlp_kernel, (places, brow, nkeep, narr, T // tile, groups)), out_shape=outs,
        grid_spec=pltpu.PrefetchScalarGridSpec(
            num_scalar_prefetch=1, grid=(T // tile,), in_specs=in_specs, out_specs=out_specs,
            scratch_shapes=[pltpu.VMEM((4, D, REST), bf), pltpu.VMEM((4, D, REST), f32), pltpu.VMEM((4, D, REST), bf),
                            pltpu.VMEM((8, D), f32), pltpu.VMEM((8, FF), f32), pltpu.VMEM((tile, D), f32),
                            pltpu.VMEM((tile, D), f32), pltpu.VMEM((tile, 128), f32), pltpu.VMEM((tile, D), bf),
                            pltpu.VMEM((tile, D), f32), pltpu.VMEM((tile, D), f32), pltpu.VMEM((2, tile, 512), f32),
                            pltpu.VMEM((2, tile, 512), f32), pltpu.VMEM((2, tile, 512), bf), pltpu.VMEM((2, tile, 512), bf),
                            pltpu.SemaphoreType.DMA((2 * len(places),)), pltpu.SemaphoreType.DMA((2 * len(places),))]),
        compiler_params=pltpu.CompilerParams(vmem_limit_bytes=VMEM_ALL),
        cost_estimate=pl.CostEstimate(flops=T * 19 * 10**6, bytes_accessed=30 * 10**6, transcendentals=T * FF * 2),
    )(me, *ins)


def assemble_kernel(me_ref, vec, dbi, ln, q01, q23, p01, p23, out, nat):
    out[...] = jnp.zeros(out.shape, f32)
    nat[0:2] = ln[0:2]
    nat[4:8] = vec[0:4]
    lane = lax.broadcasted_iota(jnp.int32, (1, 128), 1)
    top = jnp.full((1, 128), masked_score, f32)
    for k in range(4):
        q, p, i = (q01, p01, k) if k < 2 else (q23, p23, k - 2)
        group = me_ref[1] ^ k
        at = pl.multiple_of(group * 128, 128)
        nat[2:4, pl.ds(at, 128)] = q[2 * i:2 * i + 2]
        nat[pl.ds(8 + group, 1), :] = dbi[k:k + 1]
        for h in range(4):
            top = jnp.where(lane == group * 4 + h, p[4 * i + h:4 * i + h + 1], top)
    for i in range(12):
        out[2 * i:2 * i + 1] = nat[i:i + 1, 0:384]
        out[2 * i + 1:2 * i + 2, 0:128] = nat[i:i + 1, 384:512]
    out[24:25, 0:128] = top


def assemble(me, vec, dbi, ln, qs, ps):
    smem = pl.BlockSpec(memory_space=pltpu.SMEM)
    vmem = pl.BlockSpec(memory_space=pltpu.VMEM)
    return pl.pallas_call(
        assemble_kernel, out_shape=sds((32, QKV), f32), in_specs=[smem] + [vmem] * 7,
        scratch_shapes=[pltpu.VMEM((16, D), f32)],
        compiler_params=pltpu.CompilerParams(vmem_limit_bytes=VMEM_ALL),
    )(me, vec, dbi, ln, *qs, *ps)


def unpack_rest_kernel(rest, outw, inner, outer):
    outw[...] = rest[:, 0:128].astype(f32)
    inner[...] = rest[:, 128:640].astype(f32)
    outer[...] = rest[:, 640:1152].astype(f32)


def unpack_rest(rest):
    return pl.pallas_call(
        unpack_rest_kernel, out_shape=[sds((64, 128), f32), sds((64, 512), f32), sds((64, 512), f32)],
        compiler_params=pltpu.CompilerParams(vmem_limit_bytes=VMEM_ALL),
    )(rest)


def unpack_kernel(me_ref, buf, tri, triple, table, clipped, peaks, dbi, *vectors):
    flat = me_ref[3]
    b = buf[...].astype(f32)
    for c in range(3):
        triple[c] = b[0:64, c * 128:(c + 1) * 128]
    for h in range(4):
        for c in range(7):
            hi = min(QKV, TABLE - c * QKV)
            table[h:h + 1, c * QKV:c * QKV + hi] = b[64 + h * 7 + c:65 + h * 7 + c, 0:hi]
    rows = [jnp.concatenate([b[96 + 2 * i:97 + 2 * i], b[97 + 2 * i:98 + 2 * i, 0:128]], axis=1) for i in range(12)]
    first = jnp.concatenate(rows[0:8], axis=0)
    first = pltpu.roll(first, 512 - flat * 16, 1)
    for i in range(8):
        vectors[i][...] = first[i:i + 1, 0:16].reshape(16)
    wide = rows[8]
    for i in range(1, 4):
        wide = jnp.where(flat // 8 == i, rows[8 + i], wide)
    dbi[...] = pltpu.roll(jnp.broadcast_to(wide, (8, 512)), 512 - (flat % 8) * 64, 1)[0:1, 0:64].reshape(64)
    top = jnp.broadcast_to(b[120:121, 0:128], (8, 128))
    top = pltpu.roll(top, 128 - me_ref[1] * 4, 1)[0:1]
    peaks[...] = top[:, 0:4].reshape(4)
    root = jnp.sqrt(clip_target / jnp.maximum(top, clip_target))
    lane = lax.broadcasted_iota(jnp.int32, (1, 128), 1) // 32
    scale = jnp.zeros((1, 128), f32)
    for h in range(4):
        scale = jnp.where(lane == h, root[:, h:h + 1], scale)
    for c in range(2):
        clipped[c] = tri[c] * scale


def unpack(me, buf, triple_weight):
    smem = pl.BlockSpec(memory_space=pltpu.SMEM)
    vmem = pl.BlockSpec(memory_space=pltpu.VMEM)
    return pl.pallas_call(
        unpack_kernel,
        out_shape=[sds((3, 64, 128), f32), sds((4, TABLE), f32), sds((2, 64, 128), f32), sds((4,), f32), sds((64,), f32)] +
        [sds((16,), f32)] * 8,
        in_specs=[smem, vmem, vmem], compiler_params=pltpu.CompilerParams(vmem_limit_bytes=VMEM_ALL),
    )(me, buf, triple_weight)


def swap(x, axis, bit):
    return lax.ppermute(x, axis, [(i, i ^ bit) for i in range(lax.axis_size(axis))])


Z1, Z0, Y, X, C = ("dp", 4), ("dp", 2), ("dp", 1), ("mp", 2), ("mp", 1)
DP_BLOCKS = [(p & 1) * 4 + (p & 2) + (p >> 2) for p in range(8)]


def after(x, *deps):
    return lax.optimization_barrier((x,) + deps)[0]


def join(x, y):
    return jnp.concatenate([x, y], axis=0)


def widen(x, step):
    return join(x, swap(x, *step))


def rest_places():
    out = []
    for arr in range(8):
        c, kind = arr >> 2, arr & 3
        for i in range(4):
            z1, z0 = i & 1, kind >> 1
            x, y = (kind & 1, i >> 1) if z0 == 0 else (i >> 1, kind & 1)
            out.append((arr, i, c + 2 * x, z1 * 4 + z0 * 2 + y))
    return out


def canonical(a, parts):
    m, d, rows, width = a.shape
    own = width // parts
    a = a.reshape(4, m // 4, d, rows, parts, own).transpose(0, 2, 3, 4, 1, 5)
    return a.reshape(4, d * rows, parts * (m // 4) * own)


def uncanonical(a, parts, m, d):
    own = a.shape[2] // parts // (m // 4)
    a = a.reshape(4, d, D // d, parts, m // 4, own).transpose(0, 4, 1, 2, 3, 5)
    return a.reshape(m * d, D // d, parts * own)


def shards(tokens, regions, first_gain, first_shift, triple_weight, query_bias, value_bias, offset_table, output_weight,
           output_bias, second_gain, second_shift, inner_weight, inner_bias, outer_weight, outer_bias, cotangent):
    ndp, nmp = lax.axis_size("dp"), lax.axis_size("mp")
    me_dp, me_mp = lax.axis_index("dp"), lax.axis_index("mp")
    nw = tokens.shape[0] // WIN
    hot = jnp.asarray(place_onehot())
    smalls = [first_gain, first_shift, query_bias, value_bias, output_bias, second_gain, second_shift, outer_bias, inner_bias]
    T = tokens.shape[0]
    x3 = tokens.reshape(nw, WIN, D)
    three = lambda a: a.reshape(nw, WIN, a.shape[-1])
    flat = lambda a: a.reshape(T, a.shape[-1])
    tile = 392 if T % 392 == 0 else T
    near_ks, far_ks = (0, 1), (2, 3)
    if (ndp, nmp) == (8, 4):
        me = jnp.stack([me_dp, me_mp, me_mp * nw, me_dp * nmp + me_mp]).astype(jnp.int32)
        pk, rest, t0 = pack(triple_weight, output_weight.T, inner_weight, outer_weight.T, offset_table, *smalls)
        t1 = swap(t0, *C)
        t2 = swap(t0, *X)
        w = pk[None]
        w_z1 = swap(w, *Z1)
        t3 = swap(t2, *C)
        a = rest[None]
        a_z1 = swap(a, *Z1)
        near_bias = bias_grid([t0, t1], hot)
        w = join(w, after(w_z1, near_bias))
        a = join(a, after(a_z1, near_bias))
        w_z0 = swap(w, *Z0)
        b = swap(a, *Z0)
        w = join(w, w_z0)
        w_y = swap(w, *Y)
        far_bias = bias_grid([after(t2, w), t3], hot)
        w0 = join(w, after(w_y, far_bias, b))
        ay = swap(after(a, w0), *Y)
        w1 = swap(w0, *C)
        w2 = swap(w0, *X)
        n1, small, *near = attend_fwd(near_ks, me, after(x3, b), [w0, w1], w0, near_bias, regions, DP_BLOCKS)
        bx = swap(b, *X)
        w3 = swap(after(w2, n1), *C)
        a0, b_0 = join(a, after(ay, n1)), join(b, after(bx, n1))
        a1, b_1 = swap(a0, *X), swap(b_0, *Y)
        ca0, cb0 = swap(a0, *C), swap(b_0, *C)
        far = attend_fwd(far_ks, me, after(n1, a0, b_0), [w2, w3], small, far_bias, regions, DP_BLOCKS)
        ca1, cb1 = swap(after(a1, far[0]), *C), swap(after(b_1, far[0]), *C)
        result, dy, dyb, wo, vec, dbi, k0, k1, k2, k3, sent = mlp(
            me, tokens, cotangent, [flat(near[3]), flat(far[3])], (near_ks, far_ks), small,
            [a0, a1, b_0, b_1, ca0, ca1, cb0, cb1], rest_places(), 4, tile)
        got = swap(sent, *C)
        dn, far_pair, far_vec = attend_bwd(far_ks, me, n1, far[0], far[1], far[2], far[4], three(dyb), wo, far[6], hot,
                                           None, None, DP_BLOCKS)
        got = after(got, dn)
        ga0, ga1, gb0, gb1 = [kept + got[4 * i:4 * i + 4] for i, kept in enumerate((k0, k1, k2, k3))]
        xa1, yb1 = swap(ga1, *X), swap(gb1, *Y)
        xfar = swap(far_pair, *X)
        dn, near_pair, near_vec, ln = attend_bwd(
            near_ks, me, n1, near[0], near[1], near[2], near[4], three(dyb), wo, near[6], hot,
            after(dn, ga0, ga1, gb0, gb1), (x3, three(dy), small), DP_BLOCKS)
        near_vec, near_pair, xfar, xa1, yb1 = lax.optimization_barrier((near_vec, near_pair, xfar, xa1, yb1))
        pair = near_pair[PAIR:] + xfar[PAIR:]
        core = swap(pair, *C)
        vecs = assemble(me, vec, dbi, after(ln, pair), [near_vec, far_vec], [near[5], far[5]])
        peak_row = lax.broadcasted_iota(jnp.int32, (32, QKV), 0) == 24
        ga0, gb0 = ga0 + after(xa1, vecs), gb0 + after(yb1, vecs)
        for step in (X, C):
            got = after(swap(vecs, *step), ga0, gb0)
            vecs = jnp.where(peak_row, jnp.maximum(vecs, got), vecs + got)
        buf = join(near_pair[:PAIR] + xfar[:PAIR] + after(core, ga0, gb0), vecs.astype(bf))
        ga, gb = ga0[:2] + swap(ga0[2:], *Y), gb0[:2] + swap(gb0[2:], *X)
        ga = ga + swap(gb, *Z0)
        rest_sum = ga[0] + swap(ga[1], *Z1)
        for step in (Y, Z0, Z1):
            half = (buf.shape[0] - 64) // 2
            got = swap(buf[half:], *step)
            own = join(buf[:half], buf[2 * half:])
            peak = lax.broadcasted_iota(jnp.int32, own.shape, 0) == half + 56
            buf = jnp.where(peak, jnp.maximum(own, got), own + got)
        outw, inner, outer = unpack_rest(rest_sum)
        triple, table, clipped, peaks, dbi, *v = unpack(me, buf, triple_weight)
        return (result, flat(dn), v[0], v[1], triple, v[2], v[3], table, outw.T, v[7], v[5], v[6], inner, dbi, outer.T, v[4],
                peaks, clipped)

    rows, own = D // ndp, D // nmp
    both = ("mp", "dp")
    shape = (nmp, ndp, rows, -1)
    me = jnp.stack([0 * me_dp, 0 * me_mp, me_mp * nw, me_dp * nmp + me_mp]).astype(jnp.int32)
    everywhere = lambda a: lax.all_gather(a.astype(bf), both).reshape(shape)
    wcanon = canonical(everywhere(triple_weight.transpose(1, 0, 2).reshape(rows, 3 * own)), 3)
    warrs = [jnp.concatenate([canonical(everywhere(a), 1) for a in (output_weight.T, inner_weight, outer_weight.T)], axis=2)]
    eight = lax.all_gather(jnp.stack(smalls[:8]).astype(bf), "dp", axis=1, tiled=True).reshape(8, 8, 64).transpose(1, 0, 2)
    eight = jnp.pad(eight, ((0, 0), (0, 0), (0, QKV - 64)))
    ninth = lax.all_gather(inner_bias.astype(bf), "dp", tiled=True).reshape(8, 1, 256)
    ninth = jnp.pad(ninth, ((0, 0), (0, 7), (0, QKV - 256)))
    small_src = jnp.concatenate([eight, ninth], axis=1)
    tables = lax.all_gather(offset_table.astype(bf), "mp", tiled=True)
    tables = jnp.pad(tables, ((0, 0), (0, TLANES - TABLE))).reshape(4, 16, 640)
    bias = [bias_grid([tables[k], tables[k + 1]], hot) for k in (0, 2)]
    blocks = [0]
    wk = [wcanon[k:k + 1] for k in range(4)]
    n1, small, *near = attend_fwd(near_ks, me, x3, wk[:2], small_src, bias[0], regions, blocks)
    far = attend_fwd(far_ks, me, n1, wk[2:], small, bias[1], regions, blocks)
    result, dy, dyb, wo, vec, dbi, rg = mlp(
        me, tokens, cotangent, [flat(near[3]), flat(far[3])], (near_ks, far_ks), small, warrs,
        [(0, k, k, 0) for k in range(4)], 1, tile)
    dn, far_pair, far_vec = attend_bwd(far_ks, me, n1, far[0], far[1], far[2], far[4], three(dyb), wo, far[6], hot,
                                       None, None, blocks)
    dx, near_pair, near_vec, ln = attend_bwd(
        near_ks, me, n1, near[0], near[1], near[2], near[4], three(dyb), wo, near[6], hot, dn, (x3, three(dy), small), blocks)
    vecs = assemble(me, vec, dbi, ln, [near_vec, far_vec], [near[5], far[5]])
    pairs = jnp.concatenate([near_pair, far_pair]).reshape(4, PAIR, QKV)
    dx = flat(dx)
    reduce = lambda a, parts: lax.psum_scatter(uncanonical(a, parts, nmp, ndp), both, tiled=True)[0].astype(f32)
    triple = reduce(pairs[:, :D], 3).reshape(rows, 3, own).transpose(1, 0, 2)
    outw = reduce(rg[:, :, 0:128], 1).T
    inner = reduce(rg[:, :, 128:640], 1)
    outer = reduce(rg[:, :, 640:1152], 1).T
    here = HEADS // nmp
    table = lax.psum(pairs[:, D:D + 28].astype(f32).reshape(HEADS, 7 * QKV)[:, :TABLE], both)
    table = lax.dynamic_slice_in_dim(table, me_mp * here, here)
    peaks = lax.dynamic_slice_in_dim(lax.pmax(vecs[24, :HEADS], both), me_mp * here, here)
    sums = lax.psum(vecs[:24].reshape(12, 2 * QKV)[:, :D], both)

    def piece(vector):
        width = vector.shape[0] // (ndp * nmp)
        return lax.dynamic_slice_in_dim(vector, (me_dp * nmp + me_mp) * width, width)

    factor = clip_target / jnp.maximum(peaks, clip_target)
    clipped = triple_weight[:2] * jnp.repeat(jnp.sqrt(factor), HEAD_DIM)[None, None, :]
    v = [piece(sums[i]) for i in range(8)]
    dbi = piece(sums[8:12].reshape(FF))
    return (result, dx, v[0], v[1], triple, v[2], v[3], table, outw, v[7], v[5], v[6], inner, dbi, outer, v[4], peaks, clipped)


def solution(mesh):
    rows = P(("dp", "mp"), None)
    vector = P("dp")
    every = P(("dp", "mp"))
    three = P(None, "dp", "mp")
    down, across = P("mp", "dp"), P("dp", "mp")
    return jax.shard_map(
        shards,
        mesh=mesh,
        in_specs=(rows, P("dp", None), vector, vector, three, vector, vector, P("mp", None), down, vector, vector, vector,
                  across, vector, down, vector, rows),
        out_specs=(rows, rows, every, every, three, every, every, P("mp", None), down, every, every, every, across, every,
                   down, every, P("mp"), three),
        check_vma=False,
    )
```
